128 devices in a mesh: dp: 2 (over z_lo), ctx: 8 (over x, core), exp: 8 (over y, z_hi).
Axes of the slice: x: 4, y: 4, z: 4 (z_hi: 2, z_lo: 2; z = z_hi * 2 + z_lo), core: 2. Of those that a mesh axis runs over, the one named last changes fastest.
Arguments:
- queries: bfloat16 [6144, 8192], P(('dp', 'ctx'), 'exp'), parts along dimension 0, may hold values from -140 to 140
- keys: bfloat16 [6144, 512], P(('dp', 'ctx')), parts along dimension 0, may hold values from -4.5 to 4.5
- values: bfloat16 [6144, 512], P(('dp', 'ctx')), parts along dimension 0, may hold values from -5 to 5
- offsets: int32 [16], P('dp'), parts along dimension 0, may hold values from 0 to 2688, as said below
- out_proj: bfloat16 [8192, 4096], P('exp', 'ctx'), may hold values from -0.0625 to 0.0625
- residual: bfloat16 [6144, 4096], P(('dp', 'ctx', 'exp')), parts along dimension 0, may hold values from -12 to 12
- norm_gain: float32 [4096], replicated, may hold values from 0.1 to 1.9
- expert_ids: int32 [6144, 8], P(('dp', 'ctx', 'exp')), parts along dimension 0, may hold values from 0 to 63, all different within a row; in each aligned block of 48 rows (0 to 47, 48 to 95, ...) at most 12 rows name the same one
- gate_probs: float32 [6144, 8], P(('dp', 'ctx', 'exp')), parts along dimension 0, may hold values from 0.05 to 0.3
- w_gate: bfloat16 [64, 4096, 768], P(('ctx', 'exp')), may hold values from -0.09375 to 0.09375
- w_up: bfloat16 [64, 4096, 768], P(('ctx', 'exp')), may hold values from -0.09375 to 0.09375
- w_down: bfloat16 [64, 768, 4096], P(('ctx', 'exp')), may hold values from -0.21875 to 0.21875
Outputs:
- output: bfloat16 [6144, 4096], P(('dp', 'ctx', 'exp')), parts along dimension 0
The draws below stay inside these ranges and needn't reach their ends.
There are 2 independent parts, one for each index of `dp`. The reference program is written for one: setup_inputs(seed, part) draws one part's arguments, and reference() takes and returns one part's arrays. A program takes and returns all parts, laid end to end along the dimension named above; an argument that names none is the same for every part. Nothing has to cross between parts.
Inputs may be any that keep to these rules, and one draw needn't show every extreme that they name: A permutation of 0, 384, ..., 2688: span c holds the tokens at window positions offsets[c] to offsets[c] + 383. `expert_ids`: each row names 8 different experts; within the rows of one device (aligned blocks of 48 rows) no expert is named by more than 12 rows, a bound that some block reaches.
All inputs are finite; a program needn't handle non-finite values.
Results may differ from the reference program's by a relative error of at most 0.017.
Values may be sent and summed in bfloat16 or wider, within the bound.
A program may use at most 192 MiB of HBM per device.

```python
import math
import jax
import jax.numpy as jnp
import numpy as np
from jax import lax

D = 4096
HQ = 64
KVH = 4
HD = 128
FF = 768
TOP = 8
TOK_DEV = 48
CT = 384
S = 3072
EXPERTS = 64
CAP = 12
N_CTX = 8
N_EXP = 8


def shared_keys(key):
    base = jnp.clip(jax.random.normal(key, (S, KVH * HD), jnp.float32), -4.0, 4.0)
    marked = (jnp.arange(S) % 64 == 8)[:, None]
    blended = base
    return jnp.clip(jnp.where(marked, blended, base), -4.5, 4.5)


def draw_keys(key, part):
    result = shared_keys(key)
    return result.astype(jnp.bfloat16)


def draw_queries(key, part):
    key = jax.random.fold_in(key, 3)
    first_key = jax.random.fold_in(key, 0)
    result = 4.0 * jnp.clip(jax.random.normal(first_key, (S, HQ * HD), jnp.float32), -4.0, 4.0)
    return result.astype(jnp.bfloat16)


def draw_offsets(key, part):
    key = jax.random.fold_in(key, 5)
    order_drawn = jax.random.permutation(key, N_CTX)
    return (order_drawn * CT).astype(jnp.int32)


def draw_residual(key, part):
    key = jax.random.fold_in(key, 7)
    first_key, second_key, third_key = jax.random.split(key, 3)
    row_scale = jnp.exp(jax.random.uniform(second_key, (S, 1), jnp.float32, math.log(0.25), math.log(2.5)))
    col_scale = jnp.exp(jax.random.uniform(third_key, (1, D), jnp.float32, math.log(0.15), math.log(1.5)))
    base = jnp.clip(jax.random.normal(first_key, (S, D), jnp.float32), -3.0, 3.0)
    return (base * row_scale * col_scale).astype(jnp.bfloat16)


def block_levels(own_key, shape, cuts, smallest, top_value):
    def one(dim, parts):
        steps = jax.random.uniform(jax.random.fold_in(jax.random.fold_in(own_key, 6), dim), (parts,), jnp.float32, smallest / len(cuts), top_value / len(cuts))
        return jnp.repeat(jnp.exp(steps), shape[dim] // parts).reshape((-1,) + (1,) * (len(shape) - dim - 1))

    level = one(*cuts[0])
    for cut in cuts[1:]:
        level = level * one(*cut)
    return level


def routed_block(key, own, number, rows, number_of, top, reach, slope):
    ranking = jax.random.permutation(key, number_of)
    packed, usual = portions_of(number_of, rows * top, reach, slope, True), portions_of(number_of, rows * top, reach, slope, False)
    places = jnp.arange(number_of)

    def named(tallies, rotation):
        used = int((tallies > 0).sum())
        fixed = max(1, used // 4)
        passed = fixed + (places - fixed + rotation * (used - fixed)) % max(1, number_of - fixed)
        return jnp.zeros((number_of,), jnp.int32).at[ranking[jnp.where(places < fixed, places, passed)]].set(jnp.asarray(tallies, jnp.int32))

    tallies = jnp.where(number % 4 == 0, named(packed, number // 4), named(usual, number - number // 4 - 1))
    mixed = jax.random.permutation(jax.random.fold_in(own, 3), number_of)
    donor, sink = mixed[0:number_of // 2 * 2:2], mixed[1:number_of // 2 * 2:2]
    room = jnp.minimum(tallies[donor] - 1, reach - tallies[sink]) // 2
    room = jnp.where((donor == ranking[0]) | (sink == ranking[0]) | (tallies[sink] == 0), 0, jnp.maximum(room, 0))
    passed = jax.random.randint(jax.random.fold_in(own, 4), (number_of // 2,), 0, 1 << 20) % (room + 1)
    tallies = tallies.at[donor].add(-passed).at[sink].add(passed)
    labels = jnp.searchsorted(jnp.cumsum(tallies), jnp.arange(rows * top), side="right").astype(jnp.int32)
    table = labels.reshape(top, rows).T
    table = table[jax.random.permutation(jax.random.fold_in(own, 1), rows)]
    rotation = jax.random.randint(jax.random.fold_in(own, 2), (rows, 1), 0, top)
    return jnp.take_along_axis(table, (jnp.arange(top)[None, :] + rotation) % top, axis=1)


def portions_of(count, total, most, slope, full):
    weights = [(1 << 20) // math.isqrt(standing ** slope) + 1 for standing in range(1, count + 1)]
    largest = most if full else min(most, max(-(-total // count), total * weights[0] // sum(weights)))
    least = 1 if total - largest >= count - 1 else 0
    given, spare = [largest] + [least] * (count - 1), total - largest - least * (count - 1)
    while spare > 0:
        candidates = [i for i in range(1, count) if given[i] < largest] or [i for i in range(1, count) if given[i] < most]
        mass, budget = sum([weights[i] for i in candidates]), spare
        for i in candidates:
            addition = min(most - given[i], max(1, budget * weights[i] // mass), spare)
            given[i] = given[i] + addition
            spare = spare - addition
    return np.array(given)


def normal_values(key, dims, scale, reach, shards=(), held_as=jnp.bfloat16):
    factor_of = block_levels(key, dims, shards, -0.22, 0.18) if shards else 1.0
    values = jax.random.normal(key, dims, jnp.float32) * scale * factor_of
    return jnp.minimum(jnp.maximum(values, -reach), reach).astype(held_as)


def setup_inputs(seed: int = 0, part: int = 0) -> dict:
    seeds = jax.random.split(jax.random.key(seed), 13)
    part_keys = jax.random.split(jax.random.fold_in(seeds[12], part), 13)
    queries = draw_queries(jax.random.fold_in(jax.random.fold_in(seeds[12], part), 71), part)
    keys = draw_keys(jax.random.fold_in(jax.random.fold_in(seeds[12], part), 71), part)
    values = normal_values(part_keys[2], (S, KVH * HD), 1.0, 5.0, ((0, 8),))
    offsets = draw_offsets(jax.random.fold_in(jax.random.fold_in(seeds[12], part), 71), part)
    out_proj = normal_values(seeds[4], (HQ * HD, D), (HQ * HD) ** -0.5, 0.0625, ((0, 8), (1, 8)))
    residual = draw_residual(jax.random.fold_in(jax.random.fold_in(seeds[12], part), 71), part)
    norm_gain = jnp.clip(1.0 + 0.18 * jax.random.normal(seeds[6], (D,), jnp.float32), 0.1, 1.9)
    expert_ids_keys = jax.random.split(jax.random.fold_in(part_keys[7], 1), S // TOK_DEV)
    expert_ids_turns = jax.random.permutation(jax.random.fold_in(part_keys[7], 3), S // TOK_DEV)
    expert_ids = jax.vmap(lambda own, number: routed_block(jax.random.fold_in(part_keys[7], 2), own, number, TOK_DEV, EXPERTS, TOP, CAP, 2))(expert_ids_keys, expert_ids_turns).reshape((S, TOP))
    gate_probs = jnp.clip(0.05 + 0.25 * jax.random.uniform(part_keys[8], (S, TOP), jnp.float32) ** block_levels(part_keys[8], (S, TOP), ((0, 64),), -0.2, 0.2), 0.05, 0.3)
    w_gate = normal_values(seeds[9], (EXPERTS, D, FF), D ** -0.5, 0.09375, ((0, 64),))
    w_up = normal_values(seeds[10], (EXPERTS, D, FF), D ** -0.5, 0.09375, ((0, 64),))
    w_down = normal_values(seeds[11], (EXPERTS, FF, D), FF ** -0.5, 0.21875, ((0, 64),))
    return dict(queries=queries, keys=keys, values=values, offsets=offsets, out_proj=out_proj, residual=residual, norm_gain=norm_gain, expert_ids=expert_ids, gate_probs=gate_probs, w_gate=w_gate, w_up=w_up, w_down=w_down)


def head_output(queries, keys, values, positions, head_index):
    group_size = HQ // KVH
    query_cols = lax.dynamic_slice_in_dim(queries, head_index * HD, HD, 1)
    kv_start = head_index // group_size * HD
    key_cols = lax.dynamic_slice_in_dim(keys, kv_start, HD, 1)
    value_cols = lax.dynamic_slice_in_dim(values, kv_start, HD, 1)
    scores = jnp.dot(query_cols, key_cols.T, preferred_element_type=jnp.float32) * HD ** (-0.5)
    visible = positions[None, :] <= positions[:, None]
    scores = jnp.where(visible, scores, -1e+30)
    row_max = lax.optimization_barrier(jnp.max(scores, axis=1, keepdims=True))
    weights = jnp.where(visible, jnp.exp(scores - row_max), 0.0)
    denominator = lax.optimization_barrier(jnp.sum(weights, axis=1, keepdims=True))
    mixed_values = jnp.dot(weights.astype(jnp.bfloat16), value_cols, preferred_element_type=jnp.float32)
    return mixed_values / denominator

def expert_rows(row_block, gate_matrix, up_matrix, down_matrix):
    gate_proj = jnp.dot(row_block, gate_matrix, preferred_element_type=jnp.float32)
    up_proj = jnp.dot(row_block, up_matrix, preferred_element_type=jnp.float32)
    activated = (jax.nn.silu(gate_proj) * up_proj).astype(jnp.bfloat16)
    return jnp.dot(activated, down_matrix, preferred_element_type=jnp.float32).astype(jnp.bfloat16)

def reference(queries, keys, values, offsets, out_proj, residual, norm_gain, expert_ids, gate_probs, w_gate, w_up, w_down):
    token_index = jnp.arange(S, dtype=jnp.int32)
    positions = offsets[token_index // CT] + token_index % CT
    per_head = lax.map(lambda head_index: head_output(queries, keys, values, positions, head_index), jnp.arange(HQ, dtype=jnp.int32))
    attention = jnp.transpose(per_head, (1, 0, 2)).reshape(S, HQ * HD).astype(jnp.bfloat16)
    block_width = HQ * HD // N_EXP

    def add_partial(running, block_index):
        attn_cols = lax.dynamic_slice_in_dim(attention, block_index * block_width, block_width, 1)
        proj_rows = lax.dynamic_slice_in_dim(out_proj, block_index * block_width, block_width, 0)
        partial_sum = jnp.dot(attn_cols, proj_rows, preferred_element_type=jnp.float32)
        rounded = lax.optimization_barrier(partial_sum.astype(jnp.bfloat16)).astype(jnp.float32)
        return (running + rounded, None)
    attn_sum, unused = lax.scan(add_partial, jnp.zeros((S, D), jnp.float32), jnp.arange(N_EXP, dtype=jnp.int32))
    hidden = residual.astype(jnp.float32) + attn_sum
    inverse = lax.rsqrt(lax.optimization_barrier(jnp.mean(hidden * hidden, axis=1, keepdims=True)) + 1e-06)
    normed = (hidden * inverse * norm_gain[None, :]).astype(jnp.bfloat16)
    route_count = S * TOP
    flat_ids = expert_ids.reshape(-1)
    ordering = jnp.argsort(flat_ids, stable=True).astype(jnp.int32)
    matches = flat_ids[:, None] == jnp.arange(EXPERTS, dtype=jnp.int32)[None, :]
    counts = lax.optimization_barrier(jnp.sum(matches.astype(jnp.int32), axis=0))
    starts = (jnp.cumsum(counts) - counts).astype(jnp.int32)
    longest = EXPERTS * CAP
    padded_order = jnp.concatenate([ordering, jnp.full((longest,), route_count, jnp.int32)])

    def one_expert(routed, inputs):
        gate_matrix, up_matrix, down_matrix, first_route, route_number = inputs
        picked = lax.dynamic_slice_in_dim(padded_order, first_route, longest, 0)
        valid = jnp.arange(longest, dtype=jnp.int32) < route_number
        source_rows = jnp.where(valid, picked // TOP, 0)
        results = expert_rows(normed[source_rows], gate_matrix, up_matrix, down_matrix)
        targets = jnp.where(valid, picked, route_count)
        return (routed.at[targets].set(results, mode='drop'), None)
    routed, unused_two = lax.scan(one_expert, jnp.zeros((route_count, D), jnp.bfloat16), (w_gate, w_up, w_down, starts, counts))
    routed_rows = routed.reshape(S, TOP, D)
    mixture = jnp.zeros((S, D), jnp.float32)
    for slot_index in range(TOP):
        mixture = mixture + gate_probs[:, slot_index:slot_index + 1] * routed_rows[:, slot_index].astype(jnp.float32)
    return (hidden + mixture).astype(jnp.bfloat16)
```

```python
import jax
import jax.numpy as jnp
from jax import lax
from jax.experimental import pallas as pl
from jax.experimental.pallas import tpu as pltpu
from jax.sharding import PartitionSpec as P

HQ = 64
KVH = 4
HD = 128
D = 4096
HALF = D // 2
FF = 768
TOK = 48
CAP = 12
PEERS = 8
BLK = PEERS * CAP
SLOTS = PEERS * BLK
SPAN = PEERS * TOK

NEG_FILL = -1e30
MESH = pl.DeviceIdType.MESH
F32 = jnp.float32
BF16 = jnp.bfloat16


def span_positions(offsets, owners, within):
    slot_ids = lax.iota(jnp.int32, offsets.shape[0])
    table = jnp.where(owners[:, None] == slot_ids[None, :], offsets[None, :], 0)
    return jnp.sum(table, axis=1) + within


def fold_update(carry, key_piece, value_piece, query_block, query_pos, key_pos):
    run_max, run_sum, run_acc = carry
    visible = key_pos[None, :] <= query_pos[:, None]
    scores = jnp.einsum(
        "qhd,kd->hqk", query_block, key_piece, preferred_element_type=jnp.float32
    ) * HD ** (-0.5)
    scores = jnp.where(visible[None], scores, NEG_FILL)
    new_max = jnp.maximum(run_max, jnp.max(scores, axis=2))
    weights = jnp.where(visible[None], jnp.exp(scores - new_max[:, :, None]), 0.0)
    new_sum = jnp.sum(weights, axis=2)
    mixed = jnp.einsum(
        "hqk,kd->hqd", weights.astype(jnp.bfloat16), value_piece, preferred_element_type=jnp.float32
    )
    return (new_max, new_sum, mixed)


def route_codes(packed, experts):
    named = packed[None, :8] == experts.astype(F32)[:, None, None]
    member = jnp.any(named, axis=1)
    prob = jnp.sum(jnp.where(named, packed[None, 8:], 0.0), axis=1)
    t = lax.iota(jnp.int32, SPAN)
    earlier = (t[:, None] < t[None, :]) & (t[:, None] // TOK == t[None, :] // TOK)
    rank = jnp.dot(member.astype(BF16), earlier.astype(BF16), preferred_element_type=F32)
    code = jnp.where(member, (t // TOK * CAP)[None, :] + rank.astype(jnp.int32), -1)
    return code, prob


def moe_kernel(
    hid_ref, nrm_ref, code_a, code_b, prob_a, prob_b, perm_ref, wg_hbm, wu_hbm, wd_hbm,
    out_ref,
    gat_a, gat_b, snd_a, snd_b, arr_a, arr_b, ret_a, ret_b, fin_a, fin_b, prt_a, prt_b,
    xb, act, act_b, pm, wt, wg, wu, wd,
    w_sem, s_sem, r_sem,
):
    dp, c, e = lax.axis_index("dp"), lax.axis_index("ctx"), lax.axis_index("exp")
    v = lax.rem(dp + e, 2)

    def at_exp(other):
        return (lax.rem(v + other, 2), c, other)

    def at_ctx(other):
        return (dp, other, e)

    weights = [
        pltpu.make_async_copy(src.at[0], dst, w_sem.at[i])
        for i, (src, dst) in enumerate(((wg_hbm, wg), (wu_hbm, wu), (wd_hbm, wd)))
    ]
    for w in weights:
        w.start()

    def rows(ref, index, size):
        return ref.at[pl.ds(pl.multiple_of(index * size, 16), size)]

    def push(src, src_at, dst, mine, other, size, stage, dev):
        pltpu.make_async_remote_copy(
            src_ref=rows(src, src_at, size),
            dst_ref=rows(dst, mine, size),
            send_sem=s_sem.at[stage, other],
            recv_sem=r_sem.at[stage, mine],
            device_id=dev,
            device_id_type=MESH,
        ).start()

    def waiter(ref, index, size, stage):
        return pltpu.make_async_remote_copy(
            src_ref=rows(ref, index, size),
            dst_ref=rows(ref, index, size),
            send_sem=s_sem.at[stage, index],
            recv_sem=r_sem.at[stage, index],
            device_id=at_ctx(lax.rem(c + 1, PEERS)),
            device_id_type=MESH,
        )

    def wait_all(ref, size, stage, me):
        def body(i, _):
            waiter(ref, lax.rem(me + i, PEERS), size, stage).wait_recv()
            return 0
        lax.fori_loop(1, PEERS, body, 0)

    def sent_all(ref, size, stage, me):
        def body(i, _):
            waiter(ref, lax.rem(me + i, PEERS), size, stage).wait_send()
            return 0
        lax.fori_loop(1, PEERS, body, 0)

    barrier = pltpu.get_barrier_semaphore()

    def greet(i, _):
        pl.semaphore_signal(barrier, 1, device_id=at_exp(lax.rem(e + i, PEERS)), device_id_type=MESH)
        pl.semaphore_signal(barrier, 1, device_id=at_ctx(lax.rem(c + i, PEERS)), device_id_type=MESH)
        return 0

    lax.fori_loop(1, PEERS, greet, 0)
    rows(gat_a, e, TOK)[...] = nrm_ref[:, :HALF]
    rows(gat_b, c, TOK)[...] = nrm_ref[:, HALF:]
    pl.semaphore_wait(barrier, 2 * (PEERS - 1))

    def spread(i, _):
        oe, oc = lax.rem(e + i, PEERS), lax.rem(c + i, PEERS)
        push(gat_a, e, gat_a, e, oe, TOK, 0, at_exp(oe))
        push(gat_b, c, gat_b, c, oc, TOK, 1, at_ctx(oc))
        return 0

    lax.fori_loop(1, PEERS, spread, 0)
    perm = perm_ref[...]
    for half in range(2):
        cols = slice(half * 384, half * 384 + 384)
        at = lax.broadcasted_iota(jnp.int32, (SLOTS, 384), 1) + half * 384
        pm[:, cols] = jnp.where(perm == at, 1.0, 0.0).astype(BF16)
    wait_all(gat_a, TOK, 0, e)
    wait_all(gat_b, TOK, 1, c)

    slot_of = lax.broadcasted_iota(jnp.int32, (BLK, SPAN), 0)

    def pick(code, index):
        return jnp.where(code[pl.ds(index, 1), :] == slot_of, 1.0, 0.0).astype(BF16)

    def select(code, gat, pair):
        hot = jnp.concatenate([pick(code, 2 * pair), pick(code, 2 * pair + 1)], axis=0)
        return jnp.dot(hot, gat[...], preferred_element_type=F32).astype(BF16)

    def route(i, _):
        pc, pe = lax.rem(c // 2 + i, 4), lax.rem(e // 2 + i, 4)
        rows(snd_a, pc, 2 * BLK)[...] = select(code_a, gat_a, pc)
        for k in range(2):
            push(snd_a, 2 * pc + k, arr_a, c, 2 * pc + k, BLK, 2, at_ctx(2 * pc + k))
        rows(snd_b, pe, 2 * BLK)[...] = select(code_b, gat_b, pe)
        for k in range(2):
            push(snd_b, 2 * pe + k, arr_b, e, 2 * pe + k, BLK, 3, at_exp(2 * pe + k))
        return 0

    lax.fori_loop(1, 4, route, 0)
    pc, pe = c // 2, e // 2
    sc, se = 2 * pc + 1 - lax.rem(c, 2), 2 * pe + 1 - lax.rem(e, 2)
    rows(snd_a, pc, 2 * BLK)[...] = select(code_a, gat_a, pc)
    push(snd_a, sc, arr_a, c, sc, BLK, 2, at_ctx(sc))
    rows(snd_b, pe, 2 * BLK)[...] = select(code_b, gat_b, pe)
    push(snd_b, se, arr_b, e, se, BLK, 3, at_exp(se))
    rows(arr_a, c, BLK)[...] = rows(snd_a, c, BLK)[...]
    rows(arr_b, e, BLK)[...] = rows(snd_b, e, BLK)[...]

    for w in weights:
        w.wait()
    wait_all(arr_b, BLK, 3, e)

    def reorder(n, _):
        cols = pl.ds(pl.multiple_of(n * 512, 512), 512)
        xb[:, cols] = jnp.dot(pm[...], arr_b[:, cols], preferred_element_type=F32).astype(BF16)
        return 0

    lax.fori_loop(0, HALF // 512, reorder, 0)
    wait_all(arr_a, BLK, 2, c)

    def hidden_tile(k, _):
        n, m = k // 2, lax.rem(k, 2)
        cols = pl.ds(pl.multiple_of(n * 256, 256), 256)
        part = pl.ds(pl.multiple_of(m * 384, 128), 384)
        a, b = arr_a[part, :], xb[part, :]
        gate = jnp.dot(a, wg[:HALF, cols], preferred_element_type=F32)
        gate += jnp.dot(b, wg[HALF:, cols], preferred_element_type=F32)
        up = jnp.dot(a, wu[:HALF, cols], preferred_element_type=F32)
        up += jnp.dot(b, wu[HALF:, cols], preferred_element_type=F32)
        act[part, cols] = (gate / (1.0 + jnp.exp(-gate)) * up).astype(BF16)
        return 0

    lax.fori_loop(0, 6, hidden_tile, 0)
    act_b[...] = jnp.dot(pm[...], act[...], preferred_element_type=F32).astype(BF16)
    sent_all(snd_a, BLK, 2, c)
    sent_all(snd_b, BLK, 3, e)

    def down(src, pair, first, dst):
        part = pl.ds(pl.multiple_of(pair * 2 * BLK, 64), 2 * BLK)
        dst[part, :] = jnp.dot(
            src[part, :], wd[:, first:first + HALF], preferred_element_type=F32
        ).astype(BF16)

    def give_back(i, _):
        pc, pe = lax.rem(c // 2 + i, 4), lax.rem(e // 2 + i, 4)
        down(act, pc, 0, snd_a)
        for k in range(2):
            push(snd_a, 2 * pc + k, ret_a, c, 2 * pc + k, BLK, 4, at_ctx(2 * pc + k))
        down(act_b, pe, HALF, snd_b)
        for k in range(2):
            push(snd_b, 2 * pe + k, ret_b, e, 2 * pe + k, BLK, 5, at_exp(2 * pe + k))
        return 0

    lax.fori_loop(1, 4, give_back, 0)
    down(act, pc, 0, snd_a)
    push(snd_a, sc, ret_a, c, sc, BLK, 4, at_ctx(sc))
    down(act_b, pe, HALF, snd_b)
    push(snd_b, se, ret_b, e, se, BLK, 5, at_exp(se))
    rows(ret_a, c, BLK)[...] = rows(snd_a, c, BLK)[...]
    rows(ret_b, e, BLK)[...] = rows(snd_b, e, BLK)[...]

    def mix(code, prob, ret, prt):
        def weigh(i, _):
            at = pl.ds(pl.multiple_of(i * BLK, 16), BLK)
            wt[at, :] = jnp.where(
                code[pl.ds(i, 1), :] == slot_of, prob[pl.ds(i, 1), :], 0.0
            ).astype(BF16)
            return 0

        lax.fori_loop(0, PEERS, weigh, 0)

        def tile(n, _):
            cols = pl.ds(pl.multiple_of(n * 512, 512), 512)
            prt[:, cols] = lax.dot_general(
                wt[...], ret[:, cols], (((0,), (0,)), ((), ())), preferred_element_type=F32
            ).astype(BF16)
            return 0

        lax.fori_loop(0, HALF // 512, tile, 0)

    wait_all(ret_a, BLK, 4, c)
    mix(code_a, prob_a, ret_a, prt_a)

    def home_a(i, _):
        oe = lax.rem(e + i, PEERS)
        push(prt_a, oe, fin_a, e, oe, TOK, 6, at_exp(oe))
        return 0

    lax.fori_loop(1, PEERS, home_a, 0)
    rows(fin_a, e, TOK)[...] = rows(prt_a, e, TOK)[...]
    wait_all(ret_b, BLK, 5, e)
    mix(code_b, prob_b, ret_b, prt_b)

    def home_b(i, _):
        oc = lax.rem(c + i, PEERS)
        push(prt_b, oc, fin_b, c, oc, TOK, 7, at_ctx(oc))
        return 0

    lax.fori_loop(1, PEERS, home_b, 0)
    rows(fin_b, c, TOK)[...] = rows(prt_b, c, TOK)[...]

    wait_all(fin_a, TOK, 6, e)
    total = hid_ref[:, :HALF]
    for k in range(PEERS):
        total += fin_a[k * TOK:(k + 1) * TOK, :].astype(F32)
    out_ref[:, :HALF] = total.astype(BF16)
    wait_all(fin_b, TOK, 7, c)
    total = hid_ref[:, HALF:]
    for k in range(PEERS):
        total += fin_b[k * TOK:(k + 1) * TOK, :].astype(F32)
    out_ref[:, HALF:] = total.astype(BF16)

    sent_all(gat_a, TOK, 0, e)
    sent_all(gat_b, TOK, 1, c)
    sent_all(snd_a, BLK, 4, c)
    sent_all(snd_b, BLK, 5, e)
    sent_all(prt_a, TOK, 6, e)
    sent_all(prt_b, TOK, 7, c)


def moe(hidden, normed, code_a, code_b, prob_a, prob_b, w_gate, w_up, w_down):
    i = lax.iota(jnp.int32, SLOTS)
    perm = (i % BLK // CAP * BLK + i // BLK * CAP + i % CAP)[:, None]
    vm = pl.BlockSpec(memory_space=pltpu.VMEM)
    hbm = pl.BlockSpec(memory_space=pl.ANY)
    return pl.pallas_call(
        moe_kernel,
        out_shape=jax.ShapeDtypeStruct((TOK, D), BF16),
        in_specs=[vm] * 7 + [hbm] * 3,
        out_specs=vm,
        scratch_shapes=[
            pltpu.VMEM((SPAN, HALF), BF16),
            pltpu.VMEM((SPAN, HALF), BF16),
            pltpu.VMEM((SLOTS, HALF), BF16),
            pltpu.VMEM((SLOTS, HALF), BF16),
            pltpu.VMEM((SLOTS, HALF), BF16),
            pltpu.VMEM((SLOTS, HALF), BF16),
            pltpu.VMEM((SLOTS, HALF), BF16),
            pltpu.VMEM((SLOTS, HALF), BF16),
            pltpu.VMEM((SPAN, HALF), BF16),
            pltpu.VMEM((SPAN, HALF), BF16),
            pltpu.VMEM((SPAN, HALF), BF16),
            pltpu.VMEM((SPAN, HALF), BF16),
            pltpu.VMEM((SLOTS, HALF), BF16),
            pltpu.VMEM((SLOTS, FF), BF16),
            pltpu.VMEM((SLOTS, FF), BF16),
            pltpu.VMEM((SLOTS, SLOTS), BF16),
            pltpu.VMEM((SLOTS, SPAN), BF16),
            pltpu.VMEM((D, FF), BF16),
            pltpu.VMEM((D, FF), BF16),
            pltpu.VMEM((FF, D), BF16),
            pltpu.SemaphoreType.DMA((3,)),
            pltpu.SemaphoreType.DMA((8, PEERS)),
            pltpu.SemaphoreType.DMA((8, PEERS)),
        ],
        compiler_params=pltpu.CompilerParams(
            collective_id=1, has_side_effects=True, vmem_limit_bytes=62 * 1024 * 1024
        ),
        cost_estimate=pl.CostEstimate(flops=18_000_000_000, bytes_accessed=20_000_000, transcendentals=600_000),
        name="moe",
    )(hidden, normed, code_a, code_b, prob_a, prob_b, perm, w_gate, w_up, w_down)


def shards(
    queries, keys, values, offsets, out_proj, residual, norm_gain, expert_ids, gate_probs, w_gate, w_up, w_down,
):
    span = queries.shape[0]
    heads_here = queries.shape[1] // HD
    group_size = HQ // KVH
    dp_place = lax.axis_index("dp")
    ctx_place = lax.axis_index("ctx")
    exp_place = lax.axis_index("exp")

    packed = jnp.concatenate([expert_ids.T.astype(F32), gate_probs.T], axis=0)
    near = lax.all_gather(packed, ("dp", "exp"), axis=0, tiled=False).reshape(2, PEERS, 16, TOK)
    which = (dp_place + exp_place + lax.iota(jnp.int32, PEERS)) % 2
    packed_a = jnp.where(which[:, None, None] == 0, near[0], near[1])
    packed_b = lax.all_gather(packed, "ctx", axis=0, tiled=False)
    packed_a = jnp.transpose(packed_a, (1, 0, 2)).reshape(16, SPAN)
    packed_b = jnp.transpose(packed_b, (1, 0, 2)).reshape(16, SPAN)
    steps = lax.iota(jnp.int32, PEERS)
    code_a, prob_a = route_codes(packed_a, steps * PEERS + exp_place)
    code_b, prob_b = route_codes(packed_b, ctx_place * PEERS + steps)

    kv_head = exp_place * heads_here // group_size
    key_head = lax.dynamic_slice_in_dim(keys, kv_head * HD, HD, 1)
    value_head = lax.dynamic_slice_in_dim(values, kv_head * HD, HD, 1)
    own_index = lax.iota(jnp.int32, span)
    query_pos = span_positions(offsets, jnp.zeros((span,), jnp.int32) + ctx_place, own_index)
    query_block = queries.reshape(span, heads_here, HD)
    start_state = (
        jnp.full((heads_here, span), NEG_FILL, jnp.float32),
        jnp.zeros((heads_here, span), jnp.float32),
        jnp.zeros((heads_here, span, HD), jnp.float32),
    )
    key_piece = lax.all_gather(key_head, "ctx", axis=0, tiled=True)
    value_piece = lax.all_gather(value_head, "ctx", axis=0, tiled=True)
    count = key_piece.shape[0]
    key_index = lax.iota(jnp.int32, count)
    key_pos = span_positions(offsets, key_index // span, key_index % span)
    final_max, final_sum, final_acc = fold_update(
        start_state, key_piece, value_piece, query_block, query_pos, key_pos
    )
    attention = (
        jnp.transpose(final_acc / final_sum[:, :, None], (1, 0, 2))
        .reshape(span, heads_here * HD)
        .astype(jnp.bfloat16)
    )
    partial_sum = jnp.dot(
        attention,
        lax.all_gather(out_proj, "ctx", axis=1, tiled=True),
        preferred_element_type=jnp.float32,
    )
    rounded = lax.optimization_barrier(partial_sum.astype(jnp.bfloat16)).astype(jnp.float32)
    attn_sum = lax.psum_scatter(
        rounded.astype(jnp.bfloat16), "exp", scatter_dimension=0, tiled=True
    ).astype(jnp.float32)
    hidden = residual.astype(jnp.float32) + attn_sum
    inverse = lax.rsqrt(jnp.mean(hidden * hidden, axis=1, keepdims=True) + 1e-06)
    normed = (hidden * inverse * norm_gain[None, :]).astype(jnp.bfloat16)
    return moe(hidden, normed, code_a, code_b, prob_a, prob_b, w_gate, w_up, w_down)


def solution(mesh):
    return jax.shard_map(
        shards,
        mesh=mesh,
        in_specs=(
            P(("dp", "ctx"), "exp"),
            P(("dp", "ctx"), None),
            P(("dp", "ctx"), None),
            P("dp"),
            P("exp", "ctx"),
            P(("dp", "ctx", "exp"), None),
            P(),
            P(("dp", "ctx", "exp"), None),
            P(("dp", "ctx", "exp"), None),
            P(("ctx", "exp"), None, None),
            P(("ctx", "exp"), None, None),
            P(("ctx", "exp"), None, None),
        ),
        out_specs=P(("dp", "ctx", "exp"), None),
        check_vma=False,
    )
```

```python
import math

import jax
import jax.numpy as jnp
from jax import lax
from jax.experimental import pallas as pl
from jax.experimental.pallas import tpu as pltpu
from jax.sharding import PartitionSpec as P

KVH = 4
HD = 128
D = 4096
HALF = D // 2
FF = 768
TOK = 48
CAP = 12
PEERS = 8
BLK = PEERS * CAP
SLOTS = PEERS * BLK
SPAN = PEERS * TOK
HEADS = 8 * HD

NEG_FILL = -1e30
MESH = pl.DeviceIdType.MESH
F32 = jnp.float32
BF16 = jnp.bfloat16


def route_table(packed, expert_of, code, prob, member):
    ids, probs = packed[:8], packed[8:]
    for j in range(PEERS):
        named = ids == expert_of(j).astype(F32)
        member[j:j + 1, :] = jnp.sum(jnp.where(named, 1.0, 0.0), axis=0, keepdims=True)
        prob[j:j + 1, :] = jnp.sum(jnp.where(named, probs, 0.0), axis=0, keepdims=True)

    def block_of(dim):
        t = lax.broadcasted_iota(jnp.int32, (SPAN, SPAN), dim)
        return t, ((t.astype(F32) + 0.5) * (1.0 / TOK)).astype(jnp.int32)

    before, before_block = block_of(0)
    t, block = block_of(1)
    earlier = jnp.where((before < t) & (before_block == block), 1.0, 0.0).astype(BF16)
    inside = member[...]
    rank = jnp.dot(inside.astype(BF16), earlier, preferred_element_type=F32)
    code[...] = jnp.where(inside > 0.5, block[:8] * CAP + rank.astype(jnp.int32), -1)


def moe_kernel(
    hid_ref, nrm_ref, own_a, own_b, perm_ref, wg_hbm, wu_hbm, wd_hbm,
    out_ref,
    gat_a, gat_b, snd_a, snd_b, arr_a, arr_b, ret_a, ret_b, fin_a, fin_b, prt_a, prt_b,
    xb, act, act_b, pm, wt, wg, wu, wd,
    rts_a, rts_b, code_a, code_b, prob_a, prob_b, member,
    w_sem, s_sem, r_sem,
):
    dp, c, e = lax.axis_index("dp"), lax.axis_index("ctx"), lax.axis_index("exp")
    v = lax.rem(dp + e, 2)

    def at_exp(other):
        return (lax.rem(v + other, 2), c, other)

    def at_ctx(other):
        return (dp, other, e)

    weights = [
        pltpu.make_async_copy(src.at[0], dst, w_sem.at[i])
        for i, (src, dst) in enumerate(((wg_hbm, wg), (wu_hbm, wu), (wd_hbm, wd)))
    ]
    for w in weights:
        w.start()

    def rows(ref, index, size):
        return ref.at[pl.ds(pl.multiple_of(index * size, 16), size)]

    def push(src, src_at, dst, mine, other, size, stage, dev):
        pltpu.make_async_remote_copy(
            src_ref=rows(src, src_at, size),
            dst_ref=rows(dst, mine, size),
            send_sem=s_sem.at[stage, other],
            recv_sem=r_sem.at[stage, mine],
            device_id=dev,
            device_id_type=MESH,
        ).start()

    def waiter(ref, index, size, stage):
        return pltpu.make_async_remote_copy(
            src_ref=rows(ref, index, size),
            dst_ref=rows(ref, index, size),
            send_sem=s_sem.at[stage, index],
            recv_sem=r_sem.at[stage, index],
            device_id=at_ctx(lax.rem(c + 1, PEERS)),
            device_id_type=MESH,
        )

    def wait_all(ref, size, stage, me):
        def body(i, _):
            waiter(ref, lax.rem(me + i, PEERS), size, stage).wait_recv()
            return 0
        lax.fori_loop(1, PEERS, body, 0)

    def sent_all(ref, size, stage, me):
        def body(i, _):
            waiter(ref, lax.rem(me + i, PEERS), size, stage).wait_send()
            return 0
        lax.fori_loop(1, PEERS, body, 0)

    barrier = pltpu.get_barrier_semaphore()

    def greet(i, _):
        pl.semaphore_signal(barrier, 1, device_id=at_exp(lax.rem(e + i, PEERS)), device_id_type=MESH)
        pl.semaphore_signal(barrier, 1, device_id=at_ctx(lax.rem(c + i, PEERS)), device_id_type=MESH)
        return 0

    lax.fori_loop(1, PEERS, greet, 0)
    rows(gat_a, e, TOK)[...] = nrm_ref[:, :HALF]
    rows(gat_b, c, TOK)[...] = nrm_ref[:, HALF:]
    rows(rts_a, e, 16)[...] = own_a[...]
    rows(rts_b, c, 16)[...] = own_b[...]
    pl.semaphore_wait(barrier, 2 * (PEERS - 1))

    def spread(i, _):
        oe, oc = lax.rem(e + i, PEERS), lax.rem(c + i, PEERS)
        push(rts_a, e, rts_a, e, oe, 16, 8, at_exp(oe))
        push(rts_b, c, rts_b, c, oc, 16, 9, at_ctx(oc))
        push(gat_a, e, gat_a, e, oe, TOK, 0, at_exp(oe))
        push(gat_b, c, gat_b, c, oc, TOK, 1, at_ctx(oc))
        return 0

    lax.fori_loop(1, PEERS, spread, 0)
    perm = perm_ref[...]
    for half in range(2):
        cols = slice(half * 384, half * 384 + 384)
        at = lax.broadcasted_iota(jnp.int32, (SLOTS, 384), 1) + half * 384
        pm[:, cols] = jnp.where(perm == at, 1.0, 0.0).astype(BF16)
    wait_all(rts_a, 16, 8, e)
    wait_all(rts_b, 16, 9, c)
    packed_a, packed_b = rts_a[:16, :], rts_b[:16, :]
    for k in range(1, PEERS):
        packed_a += rts_a[k * 16:k * 16 + 16, :]
        packed_b += rts_b[k * 16:k * 16 + 16, :]
    route_table(packed_a, lambda j: j * PEERS + e, code_a, prob_a, member)
    route_table(packed_b, lambda j: c * PEERS + j, code_b, prob_b, member)
    wait_all(gat_a, TOK, 0, e)
    wait_all(gat_b, TOK, 1, c)

    slot_of = lax.broadcasted_iota(jnp.int32, (BLK, SPAN), 0)

    def pick(code, index):
        return jnp.where(code[pl.ds(index, 1), :] == slot_of, 1.0, 0.0).astype(BF16)

    def select(code, gat, pair):
        hot = jnp.concatenate([pick(code, 2 * pair), pick(code, 2 * pair + 1)], axis=0)
        return jnp.dot(hot, gat[...], preferred_element_type=F32).astype(BF16)

    def route(i, _):
        pc, pe = lax.rem(c // 2 + i, 4), lax.rem(e // 2 + i, 4)
        rows(snd_a, pc, 2 * BLK)[...] = select(code_a, gat_a, pc)
        for k in range(2):
            push(snd_a, 2 * pc + k, arr_a, c, 2 * pc + k, BLK, 2, at_ctx(2 * pc + k))
        rows(snd_b, pe, 2 * BLK)[...] = select(code_b, gat_b, pe)
        for k in range(2):
            push(snd_b, 2 * pe + k, arr_b, e, 2 * pe + k, BLK, 3, at_exp(2 * pe + k))
        return 0

    lax.fori_loop(1, 4, route, 0)
    pc, pe = c // 2, e // 2
    sc, se = 2 * pc + 1 - lax.rem(c, 2), 2 * pe + 1 - lax.rem(e, 2)
    rows(snd_a, pc, 2 * BLK)[...] = select(code_a, gat_a, pc)
    push(snd_a, sc, arr_a, c, sc, BLK, 2, at_ctx(sc))
    rows(snd_b, pe, 2 * BLK)[...] = select(code_b, gat_b, pe)
    push(snd_b, se, arr_b, e, se, BLK, 3, at_exp(se))
    rows(arr_a, c, BLK)[...] = rows(snd_a, c, BLK)[...]
    rows(arr_b, e, BLK)[...] = rows(snd_b, e, BLK)[...]

    for w in weights:
        w.wait()
    wait_all(arr_b, BLK, 3, e)

    def reorder(n, _):
        cols = pl.ds(pl.multiple_of(n * 512, 512), 512)
        xb[:, cols] = jnp.dot(pm[...], arr_b[:, cols], preferred_element_type=F32).astype(BF16)
        return 0

    lax.fori_loop(0, HALF // 512, reorder, 0)
    wait_all(arr_a, BLK, 2, c)

    def hidden_tile(k, _):
        n, m = k // 2, lax.rem(k, 2)
        cols = pl.ds(pl.multiple_of(n * 256, 256), 256)
        part = pl.ds(pl.multiple_of(m * 384, 128), 384)
        a, b = arr_a[part, :], xb[part, :]
        gate = jnp.dot(a, wg[:HALF, cols], preferred_element_type=F32)
        gate += jnp.dot(b, wg[HALF:, cols], preferred_element_type=F32)
        up = jnp.dot(a, wu[:HALF, cols], preferred_element_type=F32)
        up += jnp.dot(b, wu[HALF:, cols], preferred_element_type=F32)
        act[part, cols] = (gate / (1.0 + jnp.exp(-gate)) * up).astype(BF16)
        return 0

    lax.fori_loop(0, 6, hidden_tile, 0)
    act_b[...] = jnp.dot(pm[...], act[...], preferred_element_type=F32).astype(BF16)
    sent_all(snd_a, BLK, 2, c)
    sent_all(snd_b, BLK, 3, e)

    def down(src, pair, first, dst):
        part = pl.ds(pl.multiple_of(pair * 2 * BLK, 64), 2 * BLK)
        dst[part, :] = jnp.dot(
            src[part, :], wd[:, first:first + HALF], preferred_element_type=F32
        ).astype(BF16)

    def give_back(i, _):
        pc, pe = lax.rem(c // 2 + i, 4), lax.rem(e // 2 + i, 4)
        down(act, pc, 0, snd_a)
        for k in range(2):
            push(snd_a, 2 * pc + k, ret_a, c, 2 * pc + k, BLK, 4, at_ctx(2 * pc + k))
        down(act_b, pe, HALF, snd_b)
        for k in range(2):
            push(snd_b, 2 * pe + k, ret_b, e, 2 * pe + k, BLK, 5, at_exp(2 * pe + k))
        return 0

    lax.fori_loop(1, 4, give_back, 0)
    down(act, pc, 0, snd_a)
    push(snd_a, sc, ret_a, c, sc, BLK, 4, at_ctx(sc))
    down(act_b, pe, HALF, snd_b)
    push(snd_b, se, ret_b, e, se, BLK, 5, at_exp(se))
    rows(ret_a, c, BLK)[...] = rows(snd_a, c, BLK)[...]
    rows(ret_b, e, BLK)[...] = rows(snd_b, e, BLK)[...]

    def mix(code, prob, ret, prt):
        def weigh(i, _):
            at = pl.ds(pl.multiple_of(i * BLK, 16), BLK)
            wt[at, :] = jnp.where(
                code[pl.ds(i, 1), :] == slot_of, prob[pl.ds(i, 1), :], 0.0
            ).astype(BF16)
            return 0

        lax.fori_loop(0, PEERS, weigh, 0)

        def tile(n, _):
            cols = pl.ds(pl.multiple_of(n * 512, 512), 512)
            prt[:, cols] = lax.dot_general(
                wt[...], ret[:, cols], (((0,), (0,)), ((), ())), preferred_element_type=F32
            ).astype(BF16)
            return 0

        lax.fori_loop(0, HALF // 512, tile, 0)

    wait_all(ret_a, BLK, 4, c)
    mix(code_a, prob_a, ret_a, prt_a)

    def home_a(i, _):
        oe = lax.rem(e + i, PEERS)
        push(prt_a, oe, fin_a, e, oe, TOK, 6, at_exp(oe))
        return 0

    lax.fori_loop(1, PEERS, home_a, 0)
    rows(fin_a, e, TOK)[...] = rows(prt_a, e, TOK)[...]
    wait_all(ret_b, BLK, 5, e)
    mix(code_b, prob_b, ret_b, prt_b)

    def home_b(i, _):
        oc = lax.rem(c + i, PEERS)
        push(prt_b, oc, fin_b, c, oc, TOK, 7, at_ctx(oc))
        return 0

    lax.fori_loop(1, PEERS, home_b, 0)
    rows(fin_b, c, TOK)[...] = rows(prt_b, c, TOK)[...]

    wait_all(fin_a, TOK, 6, e)
    total = hid_ref[:, :HALF]
    for k in range(PEERS):
        total += fin_a[k * TOK:(k + 1) * TOK, :].astype(F32)
    out_ref[:, :HALF] = total.astype(BF16)
    wait_all(fin_b, TOK, 7, c)
    total = hid_ref[:, HALF:]
    for k in range(PEERS):
        total += fin_b[k * TOK:(k + 1) * TOK, :].astype(F32)
    out_ref[:, HALF:] = total.astype(BF16)

    sent_all(gat_a, TOK, 0, e)
    sent_all(gat_b, TOK, 1, c)
    sent_all(snd_a, BLK, 4, c)
    sent_all(snd_b, BLK, 5, e)
    sent_all(prt_a, TOK, 6, e)
    sent_all(prt_b, TOK, 7, c)
    sent_all(rts_a, 16, 8, e)
    sent_all(rts_b, 16, 9, c)


def moe(hidden, normed, own_a, own_b, w_gate, w_up, w_down):
    i = lax.iota(jnp.int32, SLOTS)
    perm = (i % BLK // CAP * BLK + i // BLK * CAP + i % CAP)[:, None]
    vm = pl.BlockSpec(memory_space=pltpu.VMEM)
    hbm = pl.BlockSpec(memory_space=pl.ANY)
    return pl.pallas_call(
        moe_kernel,
        out_shape=jax.ShapeDtypeStruct((TOK, D), BF16),
        in_specs=[vm] * 5 + [hbm] * 3,
        out_specs=vm,
        scratch_shapes=[
            pltpu.VMEM((SPAN, HALF), BF16),
            pltpu.VMEM((SPAN, HALF), BF16),
            pltpu.VMEM((SLOTS, HALF), BF16),
            pltpu.VMEM((SLOTS, HALF), BF16),
            pltpu.VMEM((SLOTS, HALF), BF16),
            pltpu.VMEM((SLOTS, HALF), BF16),
            pltpu.VMEM((SLOTS, HALF), BF16),
            pltpu.VMEM((SLOTS, HALF), BF16),
            pltpu.VMEM((SPAN, HALF), BF16),
            pltpu.VMEM((SPAN, HALF), BF16),
            pltpu.VMEM((SPAN, HALF), BF16),
            pltpu.VMEM((SPAN, HALF), BF16),
            pltpu.VMEM((SLOTS, HALF), BF16),
            pltpu.VMEM((SLOTS, FF), BF16),
            pltpu.VMEM((SLOTS, FF), BF16),
            pltpu.VMEM((SLOTS, SLOTS), BF16),
            pltpu.VMEM((SLOTS, SPAN), BF16),
            pltpu.VMEM((D, FF), BF16),
            pltpu.VMEM((D, FF), BF16),
            pltpu.VMEM((FF, D), BF16),
            pltpu.VMEM((PEERS * 16, SPAN), F32),
            pltpu.VMEM((PEERS * 16, SPAN), F32),
            pltpu.VMEM((PEERS, SPAN), jnp.int32),
            pltpu.VMEM((PEERS, SPAN), jnp.int32),
            pltpu.VMEM((PEERS, SPAN), F32),
            pltpu.VMEM((PEERS, SPAN), F32),
            pltpu.VMEM((PEERS, SPAN), F32),
            pltpu.SemaphoreType.DMA((3,)),
            pltpu.SemaphoreType.DMA((10, PEERS)),
            pltpu.SemaphoreType.DMA((10, PEERS)),
        ],
        compiler_params=pltpu.CompilerParams(
            collective_id=1, has_side_effects=True, vmem_limit_bytes=62 * 1024 * 1024
        ),
        cost_estimate=pl.CostEstimate(flops=18_000_000_000, bytes_accessed=20_000_000, transcendentals=600_000),
        name="moe",
    )(hidden, normed, own_a, own_b, perm, w_gate, w_up, w_down)


def attn_kernel(
    off_ref, q_ref, k_hbm, v_hbm, w_hbm, res_ref, gain_ref,
    hid_ref, nrm_ref,
    kv, wbuf, mx, acc, att, pbuf, rbuf, tot, zsnd, zbuf,
    l_sem, kv_s, kv_r, w_s, w_r, y_s, y_r, z_s, z_r,
):
    dp, c, e = lax.axis_index("dp"), lax.axis_index("ctx"), lax.axis_index("exp")
    x, core, y, zh = c // 2, lax.rem(c, 2), e // 2, lax.rem(e, 2)
    sib = 2 * x + 1 - core

    def at_x(i):
        return (dp, 2 * lax.rem(x + i, 4) + core, e)

    def at_y(i):
        return (dp, c, 2 * lax.rem(y + i, 4) + zh)

    at_sib = (dp, sib, e)
    at_z = (dp, c, 2 * y + 1 - zh)

    def rows(ref, index, size):
        return ref.at[pl.ds(pl.multiple_of(index * size, 16), size)]

    def remote(src, dst, s, r, dev):
        return pltpu.make_async_remote_copy(
            src_ref=src, dst_ref=dst, send_sem=s, recv_sem=r, device_id=dev, device_id_type=MESH
        )

    kv_head = lax.rem(y, KVH)
    cols = pl.ds(pl.multiple_of(kv_head * HD, HD), HD)
    own = rows(kv, c, SPAN)
    loads = [
        pltpu.make_async_copy(k_hbm.at[:, cols], own.at[:, :HD], l_sem.at[0]),
        pltpu.make_async_copy(v_hbm.at[:, cols], own.at[:, HD:], l_sem.at[1]),
        pltpu.make_async_copy(w_hbm, rows(wbuf, c, HEADS), l_sem.at[2]),
    ]
    for load in loads:
        load.start()
    barrier = pltpu.get_barrier_semaphore()
    peers = [at_x(i) for i in (1, 2, 3)] + [at_y(i) for i in (1, 2, 3)] + [at_sib, at_z]
    for dev in peers:
        pl.semaphore_signal(barrier, 1, device_id=dev, device_id_type=MESH)
    loads[0].wait()
    loads[1].wait()
    pl.semaphore_wait(barrier, len(peers))

    def copies(buf, size, s, r):
        def direct(i):
            return remote(rows(buf, c, size), rows(buf, c, size), s.at[i], r.at[i], at_x(i))

        def arrival(i):
            block = rows(buf, 2 * lax.rem(x + 4 - i, 4) + core, size)
            return remote(block, block, s.at[3 + i], r.at[i], at_sib)

        def handed(i):
            block = rows(buf, 2 * lax.rem(x + 4 - i, 4) + core, size)
            return remote(block, block, s.at[3 + i], r.at[3 + i], at_sib)

        def handed_arrival(i):
            block = rows(buf, 2 * lax.rem(x + 4 - i, 4) + 1 - core, size)
            return remote(block, block, s.at[3 + i], r.at[3 + i], at_sib)

        to_sib = remote(rows(buf, c, size), rows(buf, c, size), s.at[0], r.at[0], at_sib)
        from_sib = remote(rows(buf, sib, size), rows(buf, sib, size), s.at[0], r.at[0], at_sib)
        return direct, arrival, handed, handed_arrival, to_sib, from_sib

    k_direct, k_arrival, k_handed, k_handed_arrival, k_to_sib, k_from_sib = copies(kv, SPAN, kv_s, kv_r)
    w_direct, w_arrival, w_handed, w_handed_arrival, w_to_sib, w_from_sib = copies(wbuf, HEADS, w_s, w_r)
    k_to_sib.start()
    for i in (1, 3, 2):
        k_direct(i).start()

    scale = HD ** (-0.5) * math.log2(math.e)
    lane = lax.broadcasted_iota(jnp.int32, (1, 2 * SPAN), 1)
    ones = jnp.ones((2 * SPAN, HD), BF16)

    def group(i):
        chip = lax.rem(x + 4 - i, 4)
        at = pl.ds(pl.multiple_of(chip * 2 * SPAN, 2 * SPAN), 2 * SPAN)
        first, second = off_ref[2 * chip], off_ref[2 * chip + 1]
        key_pos = jnp.where(lane < SPAN, first + lane, second + lane - SPAN)
        if i:
            bias = jnp.where(key_pos <= off_ref[c] + SPAN - 1, 0.0, NEG_FILL)

        def head(h, _):
            hcols = pl.ds(pl.multiple_of(h * HD, HD), HD)
            mine = pl.ds(pl.multiple_of(h * SPAN, SPAN), SPAN)
            s = lax.dot_general(
                q_ref[:, hcols], kv[at, :HD], (((1,), (1,)), ((), ())), preferred_element_type=F32
            ) * scale
            if i:
                s = s + bias
            else:
                query_pos = off_ref[c] + lax.broadcasted_iota(jnp.int32, (SPAN, 1), 0)
                s = jnp.where(key_pos <= query_pos, s, NEG_FILL)
            top = jnp.max(s, axis=1, keepdims=True)
            if i:
                old = mx[mine, :]
                new = jnp.maximum(old, top)
                p = jnp.exp2(s - jnp.concatenate([new] * 6, axis=1)).astype(BF16)
            else:
                new = jnp.broadcast_to(top, (SPAN, HD))
                p = jnp.exp2(s - top).astype(BF16)
            mixed = jnp.dot(
                p, jnp.concatenate([kv[at, HD:], ones], axis=1), preferred_element_type=F32
            )
            if i:
                keep = jnp.exp2(old - new)
                mixed = acc[mine, :] * jnp.concatenate([keep, keep], axis=1) + mixed
            mx[mine, :] = new
            acc[mine, :] = mixed
            return 0

        lax.fori_loop(0, 8, head, 0)

    k_from_sib.wait_recv()
    group(0)
    loads[2].wait()
    w_to_sib.start()
    for i in (1, 3, 2):
        w_direct(i).start()
    for i in (1, 3):
        k_arrival(i).wait_recv()
        k_handed(i).start()
    k_handed_arrival(1).wait_recv()
    group(1)
    k_arrival(2).wait_recv()
    k_handed(2).start()
    k_handed_arrival(3).wait_recv()
    group(3)
    k_handed_arrival(2).wait_recv()
    group(2)

    def divide(h, _):
        hcols = pl.ds(pl.multiple_of(h * HD, HD), HD)
        mine = pl.ds(pl.multiple_of(h * SPAN, SPAN), SPAN)
        att[:, hcols] = (acc[mine, :HD] / acc[mine, HD:]).astype(BF16)
        return 0

    lax.fori_loop(0, 8, divide, 0)

    def piece(k):
        k2 = k // 2
        chip = lax.rem(x + 4 - lax.rem(k2 * (k2 + 1) // 2, 4), 4)
        return 2 * chip + lax.rem(core + k, 2)

    def to_y(w, i):
        return remote(
            rows(pbuf, w * 4 + lax.rem(y + i, 4), 2 * TOK), rows(rbuf, w * 3 + i - 1, 2 * TOK),
            y_s.at[w, i - 1], y_r.at[w, i - 1], at_y(i),
        )

    def to_z(w):
        return remote(rows(zsnd, w, TOK), rows(zbuf, w, TOK), z_s.at[w], z_r.at[w], at_z)

    def project(k, _):
        w = piece(k)
        rows(pbuf, w, SPAN)[...] = jnp.dot(
            att[...], rows(wbuf, w, HEADS)[...], preferred_element_type=F32
        ).astype(BF16)
        for i in (1, 3, 2):
            to_y(w, i).start()
        return 0

    def reduce(k, _):
        w = piece(k)
        total = rows(pbuf, w * 4 + y, 2 * TOK)[...].astype(F32)
        for i in (1, 3, 2):
            to_y(w, i).wait_recv()
            total += rows(rbuf, w * 3 + i - 1, 2 * TOK)[...].astype(F32)
        tot[...] = total
        rows(zsnd, w, TOK)[...] = rows(tot, 1 - zh, TOK)[...].astype(BF16)
        to_z(w).start()
        wcols = pl.ds(pl.multiple_of(w * 512, 512), 512)
        hid_ref[:, wcols] = rows(tot, zh, TOK)[...] + res_ref[:, wcols].astype(F32)
        return 0

    w_from_sib.wait_recv()
    lax.fori_loop(0, 2, project, 0)
    for i in (1, 3):
        w_arrival(i).wait_recv()
        w_handed(i).start()
    for i in (1, 3):
        w_handed_arrival(i).wait_recv()
    lax.fori_loop(2, 6, project, 0)
    w_arrival(2).wait_recv()
    w_handed(2).start()
    lax.fori_loop(0, 2, reduce, 0)
    w_handed_arrival(2).wait_recv()
    lax.fori_loop(6, 8, project, 0)
    lax.fori_loop(2, 8, reduce, 0)

    square = jnp.zeros((TOK, 1), F32)

    def finish(k, square):
        w = piece(k)
        to_z(w).wait_recv()
        wcols = pl.ds(pl.multiple_of(w * 512, 512), 512)
        h = hid_ref[:, wcols] + rows(zbuf, w, TOK)[...].astype(F32)
        hid_ref[:, wcols] = h
        return square + jnp.sum(h * h, axis=1, keepdims=True)

    square = lax.fori_loop(0, 8, finish, square)
    inverse = lax.rsqrt(square * (1.0 / D) + 1e-06)
    nrm_ref[...] = (hid_ref[...] * inverse * gain_ref[...]).astype(BF16)

    k_to_sib.wait_send()
    w_to_sib.wait_send()
    for i in (1, 2, 3):
        k_direct(i).wait_send()
        k_handed(i).wait_send()
        w_direct(i).wait_send()
        w_handed(i).wait_send()

    def sent(k, _):
        w = piece(k)
        for i in (1, 2, 3):
            to_y(w, i).wait_send()
        to_z(w).wait_send()
        return 0

    lax.fori_loop(0, 8, sent, 0)


def attend(offsets, queries, keys, values, out_proj, residual, gain):
    vm = pl.BlockSpec(memory_space=pltpu.VMEM)
    hbm = pl.BlockSpec(memory_space=pl.ANY)
    dma = pltpu.SemaphoreType.DMA
    return pl.pallas_call(
        attn_kernel,
        out_shape=(jax.ShapeDtypeStruct((TOK, D), F32), jax.ShapeDtypeStruct((TOK, D), BF16)),
        in_specs=[pl.BlockSpec(memory_space=pltpu.SMEM), vm, hbm, hbm, hbm, vm, vm],
        out_specs=(vm, vm),
        scratch_shapes=[
            pltpu.VMEM((PEERS * SPAN, 2 * HD), BF16),
            pltpu.VMEM((PEERS * HEADS, 512), BF16),
            pltpu.VMEM((8 * SPAN, HD), F32),
            pltpu.VMEM((8 * SPAN, 2 * HD), F32),
            pltpu.VMEM((SPAN, HEADS), BF16),
            pltpu.VMEM((PEERS * SPAN, 512), BF16),
            pltpu.VMEM((PEERS * 3 * 2 * TOK, 512), BF16),
            pltpu.VMEM((2 * TOK, 512), F32),
            pltpu.VMEM((PEERS * TOK, 512), BF16),
            pltpu.VMEM((PEERS * TOK, 512), BF16),
            dma((3,)), dma((7,)), dma((7,)), dma((7,)), dma((7,)),
            dma((PEERS, 3)), dma((PEERS, 3)), dma((PEERS,)), dma((PEERS,)),
        ],
        compiler_params=pltpu.CompilerParams(
            collective_id=2, has_side_effects=True, vmem_limit_bytes=48 * 1024 * 1024
        ),
        cost_estimate=pl.CostEstimate(flops=9_000_000_000, bytes_accessed=4_000_000, transcendentals=10_000_000),
        name="attend",
    )(offsets, queries, keys, values, out_proj, residual, gain)


def shards(
    queries, keys, values, offsets, out_proj, residual, norm_gain, expert_ids, gate_probs, w_gate, w_up, w_down,
):
    packed = jnp.concatenate([expert_ids.T.astype(F32), gate_probs.T], axis=0)
    tiled = jnp.tile(packed, (1, PEERS))
    block = lax.iota(jnp.int32, SPAN) // TOK
    own_a = jnp.where(block == lax.axis_index("exp"), tiled, 0.0)
    own_b = jnp.where(block == lax.axis_index("ctx"), tiled, 0.0)
    hidden, normed = attend(offsets, queries, keys, values, out_proj, residual, norm_gain[None, :])
    return moe(hidden, normed, own_a, own_b, w_gate, w_up, w_down)


def solution(mesh):
    return jax.shard_map(
        shards,
        mesh=mesh,
        in_specs=(
            P(("dp", "ctx"), "exp"),
            P(("dp", "ctx"), None),
            P(("dp", "ctx"), None),
            P("dp"),
            P("exp", "ctx"),
            P(("dp", "ctx", "exp"), None),
            P(),
            P(("dp", "ctx", "exp"), None),
            P(("dp", "ctx", "exp"), None),
            P(("ctx", "exp"), None, None),
            P(("ctx", "exp"), None, None),
            P(("ctx", "exp"), None, None),
        ),
        out_specs=P(("dp", "ctx", "exp"), None),
        check_vma=False,
    )
```

```python
import math

import jax
import jax.numpy as jnp
from jax import lax
from jax.experimental import pallas as pl
from jax.experimental.pallas import tpu as pltpu
from jax.sharding import PartitionSpec as P

KVH = 4
HD = 128
D = 4096
HALF = D // 2
FF = 768
TOK = 48
CAP = 12
PEERS = 8
BLK = PEERS * CAP
SLOTS = PEERS * BLK
SPAN = PEERS * TOK
HEADS = 8 * HD

NEG_FILL = -1e30
MESH = pl.DeviceIdType.MESH
F32 = jnp.float32
BF16 = jnp.bfloat16


def route_table(packed, expert_of, first, count, code, prob, member):
    ids, probs = packed[:8], packed[8:]
    for j in range(count):
        named = ids == expert_of(j).astype(F32)
        at = slice(first + j, first + j + 1)
        member[at, :] = jnp.sum(jnp.where(named, 1.0, 0.0), axis=0, keepdims=True)
        prob[at, :] = jnp.sum(jnp.where(named, probs, 0.0), axis=0, keepdims=True)


def rank_table(code, member):
    def block_of(dim):
        t = lax.broadcasted_iota(jnp.int32, (SPAN, SPAN), dim)
        return t, over(t, TOK)

    before, before_block = block_of(0)
    t, block = block_of(1)
    earlier = jnp.where((before < t) & (before_block == block), 1.0, 0.0).astype(BF16)
    inside = member[...]
    rank = jnp.dot(inside.astype(BF16), earlier, preferred_element_type=F32)
    code[...] = jnp.where(inside > 0.5, block[:8] * CAP + rank.astype(jnp.int32), -1)


def over(a, n):
    return ((a.astype(F32) + 0.5) * (1.0 / n)).astype(jnp.int32)


def moe_kernel(
    hid_ref, nrm_ref, ids_ref, probs_ref, wg_hbm, wu_hbm, wd_hbm,
    out_ref,
    gat_a, gat_b, snd_a, snd_b, arr_a, arr_b, ret_a, ret_b, fin_a, fin_b, sib_b, zed, zin, tot, keep,
    xb, act, act_b, pm, wt, wg, wu, wd,
    rts_a, rts_b, code_a, code_b, prob_a, prob_b, member,
    w_sem, s_sem, r_sem,
):
    dp, c, e = lax.axis_index("dp"), lax.axis_index("ctx"), lax.axis_index("exp")
    x, core, y, zh = c // 2, lax.rem(c, 2), e // 2, lax.rem(e, 2)
    v = lax.rem(dp + e, 2)
    sib = 2 * x + 1 - core

    def at_exp(other):
        return (lax.rem(v + other, 2), c, other)

    def at_ctx(other):
        return (dp, other, e)

    def at_far(other):
        return (1 - dp, other, 2 * y + 1 - zh)

    def chip_x(i):
        return lax.rem(x + i, 4)

    def at_x(i):
        return (dp, 2 * chip_x(i) + core, e)

    def row_y(i):
        return lax.rem(y + i, 4)

    def at_y(i):
        return (dp, c, 2 * row_y(i) + zh)

    at_sib = (dp, sib, e)
    at_z = at_far(c)

    weights = [
        pltpu.make_async_copy(src.at[0], dst, w_sem.at[i])
        for i, (src, dst) in enumerate(((wg_hbm, wg), (wu_hbm, wu), (wd_hbm, wd)))
    ]
    for w in weights:
        w.start()

    def rows(ref, index, size):
        return ref.at[pl.ds(pl.multiple_of(index * size, 16), size)]

    def copy(src, dst, stage, sent, got, dev):
        return pltpu.make_async_remote_copy(
            src_ref=src, dst_ref=dst, send_sem=s_sem.at[stage, sent], recv_sem=r_sem.at[stage, got],
            device_id=dev, device_id_type=MESH,
        )

    def same(ref, stage, index):
        return copy(ref, ref, stage, index, index, at_sib)

    barrier = pltpu.get_barrier_semaphore()

    def greet(i, _):
        oe, oc = lax.rem(e + i, PEERS), lax.rem(c + i, PEERS)
        for dev in (at_exp(oe), at_ctx(oc), at_far(oc)):
            pl.semaphore_signal(barrier, 1, device_id=dev, device_id_type=MESH)
        return 0

    lax.fori_loop(1, PEERS, greet, 0)
    b_own = core * 8 + x * 2 + zh
    b_far = core * 8 + x * 2 + 1 - zh
    e_far = 2 * y + 1 - zh
    rows(gat_a, e, TOK)[...] = nrm_ref[:, :HALF]
    rows(gat_b, b_own, TOK)[...] = nrm_ref[:, HALF:]
    token = lax.broadcasted_iota(jnp.int32, (TOK, SPAN), 0)
    lane = lax.broadcasted_iota(jnp.int32, (TOK, SPAN), 1)
    for rts, index, place in ((rts_a, e, e), (rts_b, b_own, 2 * x + zh)):
        put = jnp.where(lane == token + place * TOK, 1.0, 0.0)
        spread = [
            jnp.dot(a, put, preferred_element_type=F32, precision=lax.Precision.HIGHEST)
            for a in (ids_ref[...].astype(F32), probs_ref[...])
        ]
        rows(rts, index, 16)[...] = jnp.concatenate(spread, axis=0)
    pl.semaphore_wait(barrier, 3 * (PEERS - 1))

    own_a, own_b = rows(gat_a, e, TOK), rows(gat_b, b_own, TOK)
    far_a, far_b = rows(gat_a, e_far, TOK), rows(gat_b, b_far, TOK)
    copy(own_a, own_a, 0, 0, 0, at_z).start()
    copy(own_b, own_b, 2, 0, 0, at_z).start()

    def routes(i, _):
        oe, oc = lax.rem(e + i, PEERS), lax.rem(c + i, PEERS)
        mine_a, mine_b = rows(rts_a, e, 16), rows(rts_b, b_own, 16)
        copy(mine_a, mine_a, 11, oe, e, at_exp(oe)).start()
        copy(mine_b, mine_b, 12, oc, c, at_ctx(oc)).start()
        copy(mine_b, mine_b, 13, oc, c, at_far(oc)).start()
        return 0

    def along(stage, a, b):
        for i in (1, 3, 2):
            copy(a, a, stage, i, i, at_y(i)).start()
            copy(b, b, stage + 2, i, i, at_x(i)).start()
        copy(b, b, stage + 2, 4, 4, at_sib).start()

    along(0, own_a, own_b)
    lax.fori_loop(1, PEERS, routes, 0)
    copy(rows(rts_b, b_own, 16), rows(rts_b, b_own, 16), 13, c, c, at_z).start()
    same(far_a, 0, 0).wait_recv()
    same(far_b, 2, 0).wait_recv()
    along(1, far_a, far_b)

    def order(k, _):
        part = pl.ds(pl.multiple_of(k * 128, 128), 128)
        i = lax.broadcasted_iota(jnp.int32, (128, SLOTS), 0) + k * 128
        at = lax.broadcasted_iota(jnp.int32, (128, SLOTS), 1)
        ctx = over(i, BLK)
        rest = i - ctx * BLK
        oe = over(rest, CAP)
        oy, ox = over(oe, 2), over(ctx, 2)
        want = oy * 192 + (ctx - 2 * ox) * BLK + (ox * 2 + oe - 2 * oy) * CAP + rest - oe * CAP
        pm[part, :] = jnp.where(at == want, 1.0, 0.0).astype(BF16)
        return 0

    lax.fori_loop(0, SLOTS // 128, order, 0)

    def chip_block(who, i):
        return rows(gat_b, who * 4 + chip_x(4 - i), 2 * TOK)

    def hand_on(i):
        for z in range(2):
            block = rows(gat_b, core * 8 + chip_x(4 - i) * 2 + lax.rem(zh + z, 2), TOK)
            same(block, 2 + z, i).wait_recv()
        both = chip_block(core, i)
        copy(both, both, 4, i, i, at_sib).start()

    hand_on(1)
    hand_on(3)

    def routes_in(i, _):
        oe, oc = lax.rem(e + i, PEERS), lax.rem(c + i, PEERS)
        slot = lax.rem(oc, 2) * 8 + oc // 2 * 2
        same(rows(rts_a, oe, 16), 11, oe).wait_recv()
        same(rows(rts_b, slot + zh, 16), 12, oc).wait_recv()
        same(rows(rts_b, slot + 1 - zh, 16), 13, oc).wait_recv()
        return 0

    lax.fori_loop(1, PEERS, routes_in, 0)
    same(rows(rts_b, b_far, 16), 13, c).wait_recv()

    def gathered(rts, first):
        packed = rts[first * 16:first * 16 + 16, :]
        for k in range(first + 1, first + PEERS):
            packed += rts[k * 16:k * 16 + 16, :]
        return packed

    route_table(gathered(rts_a, 0), lambda j: j * PEERS + e, 0, PEERS, code_a, prob_a, member)
    rank_table(code_a, member)
    for k in range(2):
        route_table(
            gathered(rts_b, 8 * k), lambda j: c * PEERS + 2 * j + zh, 4 * k, 4, code_b, prob_b, member
        )
    rank_table(code_b, member)
    hand_on(2)

    slot_of = lax.broadcasted_iota(jnp.int32, (BLK, SPAN), 0)

    def pick(code, index):
        return jnp.where(code[pl.ds(index, 1), :] == slot_of, 1.0, 0.0).astype(BF16)

    def select_a(pair):
        hot = jnp.concatenate([pick(code_a, 2 * pair), pick(code_a, 2 * pair + 1)], axis=0)
        rows(snd_a, pair, 2 * BLK)[...] = jnp.dot(
            hot, gat_a[...], preferred_element_type=F32
        ).astype(BF16)

    def select_b(oy):
        for k in range(2):
            rows(snd_b, 2 * oy + k, BLK)[...] = jnp.dot(
                pick(code_b, 4 * k + oy), gat_b[k * SPAN:(k + 1) * SPAN, :], preferred_element_type=F32
            ).astype(BF16)

    for i in (1, 3, 2):
        for z in range(2):
            same(rows(gat_a, 2 * row_y(4 - i) + lax.rem(zh + z, 2), TOK), z, i).wait_recv()
    first = True
    for i in (1, 3, 2):
        oc = chip_x(i)
        select_a(oc)
        for k in range(2):
            copy(rows(snd_a, 2 * oc + k, BLK), rows(arr_a, c, BLK), 5, 2 * oc + k, c, at_ctx(2 * oc + k)).start()
        if first:
            first = False
            for z, far in enumerate((zh, 1 - zh)):
                same(rows(gat_b, (1 - core) * 8 + x * 2 + far, TOK), 2 + z, 4).wait_recv()
            for k in (1, 3, 2):
                same(chip_block(1 - core, k), 4, k).wait_recv()
        oy = row_y(i)
        select_b(oy)
        copy(rows(snd_b, oy, 2 * BLK), rows(arr_b, y, 2 * BLK), 6, i, i, at_y(i)).start()
    select_a(x)
    copy(rows(snd_a, sib, BLK), rows(arr_a, c, BLK), 5, sib, c, at_sib).start()
    select_b(y)
    rows(arr_a, c, BLK)[...] = rows(snd_a, c, BLK)[...]
    rows(arr_b, y, 2 * BLK)[...] = rows(snd_b, y, 2 * BLK)[...]

    for w in weights:
        w.wait()
    for i in (1, 3, 2):
        same(rows(arr_b, row_y(4 - i), 2 * BLK), 6, i).wait_recv()

    def reorder(n, _):
        cols = pl.ds(pl.multiple_of(n * 512, 512), 512)
        xb[:, cols] = jnp.dot(pm[...], arr_b[:, cols], preferred_element_type=F32).astype(BF16)
        return 0

    lax.fori_loop(0, HALF // 512, reorder, 0)

    def each(ref, size, stage, me, got):
        def body(i, _):
            index = lax.rem(me + i, PEERS)
            w = same(rows(ref, index, size), stage, index)
            if got:
                w.wait_recv()
            else:
                w.wait_send()
            return 0

        lax.fori_loop(1, PEERS, body, 0)

    each(arr_a, BLK, 5, c, True)

    def hidden_tile(k, _):
        n, m = k // 2, lax.rem(k, 2)
        cols = pl.ds(pl.multiple_of(n * 256, 256), 256)
        part = pl.ds(pl.multiple_of(m * 384, 128), 384)
        a, b = arr_a[part, :], xb[part, :]
        gate = jnp.dot(a, wg[:HALF, cols], preferred_element_type=F32)
        gate += jnp.dot(b, wg[HALF:, cols], preferred_element_type=F32)
        up = jnp.dot(a, wu[:HALF, cols], preferred_element_type=F32)
        up += jnp.dot(b, wu[HALF:, cols], preferred_element_type=F32)
        act[part, cols] = (gate / (1.0 + jnp.exp(-gate)) * up).astype(BF16)
        return 0

    lax.fori_loop(0, 6, hidden_tile, 0)
    act_b[...] = lax.dot_general(
        pm[...], act[...], (((0,), (0,)), ((), ())), preferred_element_type=F32
    ).astype(BF16)
    each(snd_a, BLK, 5, c, False)
    for i in (1, 2, 3):
        same(rows(snd_b, row_y(i), 2 * BLK), 6, i).wait_send()

    def down(src, pair, first, dst):
        part = pl.ds(pl.multiple_of(pair * 2 * BLK, 64), 2 * BLK)
        dst[part, :] = jnp.dot(
            src[part, :], wd[:, first:first + HALF], preferred_element_type=F32
        ).astype(BF16)

    for i in (1, 3, 2):
        oc, oy = chip_x(i), row_y(i)
        down(act, oc, 0, snd_a)
        for k in range(2):
            copy(rows(snd_a, 2 * oc + k, BLK), rows(ret_a, c, BLK), 7, 2 * oc + k, c, at_ctx(2 * oc + k)).start()
        down(act_b, oy, HALF, snd_b)
        for k in range(2):
            copy(
                rows(snd_b, 2 * oy + k, BLK), rows(ret_b, 4 * k + y, BLK), 8, 4 * k + i, 4 * k + i, at_y(i)
            ).start()
    down(act, x, 0, snd_a)
    copy(rows(snd_a, sib, BLK), rows(ret_a, c, BLK), 7, sib, c, at_sib).start()
    down(act_b, y, HALF, snd_b)
    rows(ret_a, c, BLK)[...] = rows(snd_a, c, BLK)[...]
    for k in range(2):
        rows(ret_b, 4 * k + y, BLK)[...] = rows(snd_b, 2 * y + k, BLK)[...]

    for stage, a, b in ((0, own_a, own_b), (1, far_a, far_b)):
        for i in (1, 2, 3):
            same(a, stage, i).wait_send()
            same(b, stage + 2, i).wait_send()
        same(b, stage + 2, 4).wait_send()
    same(own_a, 0, 0).wait_send()
    same(own_b, 2, 0).wait_send()
    for i in (1, 2, 3):
        same(chip_block(core, i), 4, i).wait_send()

    def mix(code, prob, first, count, ret, prt):
        size = count * BLK
        base = first * BLK

        def weigh(i, _):
            at = pl.ds(pl.multiple_of(i * BLK, 16), BLK)
            wt[at, :] = jnp.where(
                code[pl.ds(first + i, 1), :] == slot_of, prob[pl.ds(first + i, 1), :], 0.0
            ).astype(BF16)
            return 0

        lax.fori_loop(0, count, weigh, 0)

        def tile(n, _):
            cols = pl.ds(pl.multiple_of(n * 512, 512), 512)
            prt[:, cols] = lax.dot_general(
                wt[:size, :], ret[pl.ds(pl.multiple_of(base, 128), size), cols],
                (((0,), (0,)), ((), ())), preferred_element_type=F32,
            ).astype(BF16)
            return 0

        lax.fori_loop(0, HALF // 512, tile, 0)

    for i in (1, 3, 2):
        for k in range(2):
            same(rows(ret_b, 4 * k + row_y(4 - i), BLK), 8, 4 * k + i).wait_recv()
    sib_half, own_half = rows(gat_b, 1 - core, SPAN), rows(gat_b, core, SPAN)
    mix(code_b, prob_b, 4 * (1 - core), 4, ret_b, sib_half)
    copy(sib_half, sib_b, 10, 0, 0, at_sib).start()
    mix(code_b, prob_b, 4 * core, 4, ret_b, own_half)
    same(sib_b, 10, 0).wait_recv()

    def add_sib(k, _):
        at = pl.ds(pl.multiple_of(k * 2 * TOK, 32), 2 * TOK)
        own_half[at, :] = (own_half[at, :].astype(F32) + sib_b[at, :].astype(F32)).astype(BF16)
        return 0

    lax.fori_loop(0, 4, add_sib, 0)
    for i in (1, 3, 2):
        copy(rows(own_half, chip_x(i), 2 * TOK), rows(fin_b, i - 1, 2 * TOK), 10, i, i, at_x(i)).start()
    each(ret_a, BLK, 7, c, True)
    mix(code_a, prob_a, 0, PEERS, ret_a, gat_a)
    for i in (1, 3, 2):
        copy(rows(gat_a, row_y(i), 2 * TOK), rows(fin_a, i - 1, 2 * TOK), 9, i, i, at_y(i)).start()

    def home(k, part, fin, stage, zsem):
        for i in (1, 3, 2):
            same(rows(fin, i - 1, 2 * TOK), stage, i).wait_recv()
        tot[...] = part[...].astype(F32)
        for i in range(3):
            tot[...] += rows(fin, i, 2 * TOK)[...].astype(F32)
        rows(zed, k, TOK)[...] = rows(tot, 1 - zh, TOK)[...].astype(BF16)
        copy(rows(zed, k, TOK), rows(zin, k, TOK), stage, zsem, zsem, at_z).start()
        rows(keep, k, TOK)[...] = hid_ref[:, k * HALF:(k + 1) * HALF] + rows(tot, zh, TOK)[...]

    home(1, rows(own_half, x, 2 * TOK), fin_b, 10, 4)
    home(0, rows(gat_a, y, 2 * TOK), fin_a, 9, 0)
    same(rows(zin, 1, TOK), 10, 4).wait_recv()
    out_ref[:, HALF:] = (keep[TOK:, :] + zin[TOK:, :].astype(F32)).astype(BF16)
    same(rows(zin, 0, TOK), 9, 0).wait_recv()
    out_ref[:, :HALF] = (keep[:TOK, :] + zin[:TOK, :].astype(F32)).astype(BF16)

    each(snd_a, BLK, 7, c, False)
    for i in (1, 2, 3):
        for k in range(2):
            same(rows(snd_b, 2 * row_y(i) + k, BLK), 8, 4 * k + i).wait_send()
        same(rows(own_half, chip_x(i), 2 * TOK), 10, i).wait_send()
        same(rows(gat_a, row_y(i), 2 * TOK), 9, i).wait_send()
    same(sib_half, 10, 0).wait_send()
    same(rows(zed, 1, TOK), 10, 4).wait_send()
    same(rows(zed, 0, TOK), 9, 0).wait_send()

    def routes_out(i, _):
        oe, oc = lax.rem(e + i, PEERS), lax.rem(c + i, PEERS)
        same(rows(rts_a, e, 16), 11, oe).wait_send()
        same(rows(rts_b, b_own, 16), 12, oc).wait_send()
        same(rows(rts_b, b_own, 16), 13, oc).wait_send()
        return 0

    lax.fori_loop(1, PEERS, routes_out, 0)
    same(rows(rts_b, b_own, 16), 13, c).wait_send()


def moe(hidden, normed, ids, probs, w_gate, w_up, w_down):
    vm = pl.BlockSpec(memory_space=pltpu.VMEM)
    hbm = pl.BlockSpec(memory_space=pl.ANY)
    half = [(SPAN, HALF), (2 * SPAN, HALF)] + [(SLOTS, HALF)] * 6 + [(6 * TOK, HALF)] * 2
    half += [(SPAN, HALF), (2 * TOK, HALF), (2 * TOK, HALF)]
    return pl.pallas_call(
        moe_kernel,
        out_shape=jax.ShapeDtypeStruct((TOK, D), BF16),
        in_specs=[vm] * 4 + [hbm] * 3,
        out_specs=vm,
        scratch_shapes=[pltpu.VMEM(shape, BF16) for shape in half] + [
            pltpu.VMEM((2 * TOK, HALF), F32),
            pltpu.VMEM((2 * TOK, HALF), F32),
            pltpu.VMEM((SLOTS, HALF), BF16),
            pltpu.VMEM((SLOTS, FF), BF16),
            pltpu.VMEM((SLOTS, FF), BF16),
            pltpu.VMEM((SLOTS, SLOTS), BF16),
            pltpu.VMEM((SLOTS, SPAN), BF16),
            pltpu.VMEM((D, FF), BF16),
            pltpu.VMEM((D, FF), BF16),
            pltpu.VMEM((FF, D), BF16),
            pltpu.VMEM((PEERS * 16, SPAN), F32),
            pltpu.VMEM((2 * PEERS * 16, SPAN), F32),
            pltpu.VMEM((PEERS, SPAN), jnp.int32),
            pltpu.VMEM((PEERS, SPAN), jnp.int32),
            pltpu.VMEM((PEERS, SPAN), F32),
            pltpu.VMEM((PEERS, SPAN), F32),
            pltpu.VMEM((PEERS, SPAN), F32),
            pltpu.SemaphoreType.DMA((3,)),
            pltpu.SemaphoreType.DMA((14, PEERS)),
            pltpu.SemaphoreType.DMA((14, PEERS)),
        ],
        compiler_params=pltpu.CompilerParams(
            collective_id=1, has_side_effects=True, vmem_limit_bytes=62 * 1024 * 1024
        ),
        cost_estimate=pl.CostEstimate(flops=20_000_000_000, bytes_accessed=20_000_000, transcendentals=600_000),
        name="moe",
    )(hidden, normed, ids, probs, w_gate, w_up, w_down)


def attn_kernel(
    off_ref, q_hbm, k_hbm, v_hbm, w_hbm, res_hbm, gain_hbm,
    hid_ref, nrm_ref,
    q_ref, res_ref, gain_ref, kv, wbuf, mx, acc, att, pbuf, rbuf, tot, zsnd, zbuf,
    l_sem, kv_s, kv_r, w_s, w_r, y_s, y_r, z_s, z_r,
):
    dp, c, e = lax.axis_index("dp"), lax.axis_index("ctx"), lax.axis_index("exp")
    x, core, y, zh = c // 2, lax.rem(c, 2), e // 2, lax.rem(e, 2)
    sib = 2 * x + 1 - core

    def at_x(i):
        return (dp, 2 * lax.rem(x + i, 4) + core, e)

    def at_y(i):
        return (dp, c, 2 * lax.rem(y + i, 4) + zh)

    at_sib = (dp, sib, e)
    at_z = (dp, c, 2 * y + 1 - zh)

    def rows(ref, index, size):
        return ref.at[pl.ds(pl.multiple_of(index * size, 16), size)]

    def remote(src, dst, s, r, dev):
        return pltpu.make_async_remote_copy(
            src_ref=src, dst_ref=dst, send_sem=s, recv_sem=r, device_id=dev, device_id_type=MESH
        )

    kv_head = lax.rem(y, KVH)
    cols = pl.ds(pl.multiple_of(kv_head * HD, HD), HD)
    own = rows(kv, c, SPAN)
    loads = [
        pltpu.make_async_copy(k_hbm.at[:, cols], own.at[:, :HD], l_sem.at[0]),
        pltpu.make_async_copy(v_hbm.at[:, cols], own.at[:, HD:], l_sem.at[1]),
        pltpu.make_async_copy(w_hbm, rows(wbuf, c, HEADS), l_sem.at[2]),
        pltpu.make_async_copy(q_hbm, q_ref, l_sem.at[3]),
        pltpu.make_async_copy(res_hbm, res_ref, l_sem.at[4]),
        pltpu.make_async_copy(gain_hbm, gain_ref, l_sem.at[5]),
    ]
    for load in loads:
        load.start()
    barrier = pltpu.get_barrier_semaphore()
    peers = [at_x(i) for i in (1, 2, 3)] + [at_y(i) for i in (1, 2, 3)] + [at_sib, at_z]
    for dev in peers:
        pl.semaphore_signal(barrier, 1, device_id=dev, device_id_type=MESH)
    loads[0].wait()
    loads[1].wait()
    pl.semaphore_wait(barrier, len(peers))

    def copies(buf, size, s, r):
        def direct(i):
            return remote(rows(buf, c, size), rows(buf, c, size), s.at[i], r.at[i], at_x(i))

        def arrival(i):
            block = rows(buf, 2 * lax.rem(x + 4 - i, 4) + core, size)
            return remote(block, block, s.at[3 + i], r.at[i], at_sib)

        def handed(i):
            block = rows(buf, 2 * lax.rem(x + 4 - i, 4) + core, size)
            return remote(block, block, s.at[3 + i], r.at[3 + i], at_sib)

        def handed_arrival(i):
            block = rows(buf, 2 * lax.rem(x + 4 - i, 4) + 1 - core, size)
            return remote(block, block, s.at[3 + i], r.at[3 + i], at_sib)

        to_sib = remote(rows(buf, c, size), rows(buf, c, size), s.at[0], r.at[0], at_sib)
        from_sib = remote(rows(buf, sib, size), rows(buf, sib, size), s.at[0], r.at[0], at_sib)
        return direct, arrival, handed, handed_arrival, to_sib, from_sib

    k_direct, k_arrival, k_handed, k_handed_arrival, k_to_sib, k_from_sib = copies(kv, SPAN, kv_s, kv_r)
    w_direct, w_arrival, w_handed, w_handed_arrival, w_to_sib, w_from_sib = copies(wbuf, HEADS, w_s, w_r)
    k_to_sib.start()
    for i in (1, 3, 2):
        k_direct(i).start()

    scale = HD ** (-0.5) * math.log2(math.e)
    lane = lax.broadcasted_iota(jnp.int32, (1, 2 * SPAN), 1)
    ones = jnp.ones((2 * SPAN, HD), BF16)

    def group(i):
        chip = lax.rem(x + 4 - i, 4)
        at = pl.ds(pl.multiple_of(chip * 2 * SPAN, 2 * SPAN), 2 * SPAN)
        first, second = off_ref[2 * chip], off_ref[2 * chip + 1]
        key_pos = jnp.where(lane < SPAN, first + lane, second + lane - SPAN)
        if i:
            bias = jnp.where(key_pos <= off_ref[c] + SPAN - 1, 0.0, NEG_FILL)

        def head(h, _):
            hcols = pl.ds(pl.multiple_of(h * HD, HD), HD)
            mine = pl.ds(pl.multiple_of(h * SPAN, SPAN), SPAN)
            s = lax.dot_general(
                q_ref[:, hcols], kv[at, :HD], (((1,), (1,)), ((), ())), preferred_element_type=F32
            ) * scale
            if i:
                s = s + bias
            else:
                query_pos = off_ref[c] + lax.broadcasted_iota(jnp.int32, (SPAN, 1), 0)
                s = jnp.where(key_pos <= query_pos, s, NEG_FILL)
            top = jnp.max(s, axis=1, keepdims=True)
            if i:
                old = mx[mine, :]
                new = jnp.maximum(old, top)
                p = jnp.exp2(s - jnp.concatenate([new] * 6, axis=1)).astype(BF16)
            else:
                new = jnp.broadcast_to(top, (SPAN, HD))
                p = jnp.exp2(s - top).astype(BF16)
            mixed = jnp.dot(
                p, jnp.concatenate([kv[at, HD:], ones], axis=1), preferred_element_type=F32
            )
            if i:
                keep = jnp.exp2(old - new)
                mixed = acc[mine, :] * jnp.concatenate([keep, keep], axis=1) + mixed
            mx[mine, :] = new
            acc[mine, :] = mixed
            return 0

        lax.fori_loop(0, 8, head, 0)

    loads[2].wait()
    w_to_sib.start()
    for i in (1, 3, 2):
        w_direct(i).start()
    for load in loads[3:]:
        load.wait()
    k_from_sib.wait_recv()
    group(0)
    for i in (1, 3):
        k_arrival(i).wait_recv()
        k_handed(i).start()
    k_handed_arrival(1).wait_recv()
    group(1)
    k_arrival(2).wait_recv()
    k_handed(2).start()
    k_handed_arrival(3).wait_recv()
    group(3)
    k_handed_arrival(2).wait_recv()
    group(2)

    def divide(h, _):
        hcols = pl.ds(pl.multiple_of(h * HD, HD), HD)
        mine = pl.ds(pl.multiple_of(h * SPAN, SPAN), SPAN)
        att[:, hcols] = (acc[mine, :HD] / acc[mine, HD:]).astype(BF16)
        return 0

    lax.fori_loop(0, 8, divide, 0)

    def piece(k):
        k2 = k // 2
        chip = lax.rem(x + 4 - lax.rem(k2 * (k2 + 1) // 2, 4), 4)
        return 2 * chip + lax.rem(core + k, 2)

    def to_y(w, i):
        return remote(
            rows(pbuf, w * 4 + lax.rem(y + i, 4), 2 * TOK), rows(rbuf, w * 3 + i - 1, 2 * TOK),
            y_s.at[w, i - 1], y_r.at[w, i - 1], at_y(i),
        )

    def to_z(w):
        return remote(rows(zsnd, w, TOK), rows(zbuf, w, TOK), z_s.at[w], z_r.at[w], at_z)

    def project(k, _):
        w = piece(k)
        rows(pbuf, w, SPAN)[...] = jnp.dot(
            att[...], rows(wbuf, w, HEADS)[...], preferred_element_type=F32
        ).astype(BF16)
        for i in (1, 3, 2):
            to_y(w, i).start()
        return 0

    def reduce(k, _):
        w = piece(k)
        total = rows(pbuf, w * 4 + y, 2 * TOK)[...].astype(F32)
        for i in (1, 3, 2):
            to_y(w, i).wait_recv()
            total += rows(rbuf, w * 3 + i - 1, 2 * TOK)[...].astype(F32)
        tot[...] = total
        rows(zsnd, w, TOK)[...] = rows(tot, 1 - zh, TOK)[...].astype(BF16)
        to_z(w).start()
        wcols = pl.ds(pl.multiple_of(w * 512, 512), 512)
        hid_ref[:, wcols] = rows(tot, zh, TOK)[...] + res_ref[:, wcols].astype(F32)
        return 0

    w_from_sib.wait_recv()
    lax.fori_loop(0, 2, project, 0)
    for i in (1, 3):
        w_arrival(i).wait_recv()
        w_handed(i).start()
    for i in (1, 3):
        w_handed_arrival(i).wait_recv()
    lax.fori_loop(2, 6, project, 0)
    w_arrival(2).wait_recv()
    w_handed(2).start()
    lax.fori_loop(0, 2, reduce, 0)
    w_handed_arrival(2).wait_recv()
    lax.fori_loop(6, 8, project, 0)
    lax.fori_loop(2, 8, reduce, 0)

    square = jnp.zeros((TOK, 1), F32)

    def finish(k, square):
        w = piece(k)
        to_z(w).wait_recv()
        wcols = pl.ds(pl.multiple_of(w * 512, 512), 512)
        h = hid_ref[:, wcols] + rows(zbuf, w, TOK)[...].astype(F32)
        hid_ref[:, wcols] = h
        return square + jnp.sum(h * h, axis=1, keepdims=True)

    square = lax.fori_loop(0, 8, finish, square)
    inverse = lax.rsqrt(square * (1.0 / D) + 1e-06)
    nrm_ref[...] = (hid_ref[...] * inverse * gain_ref[...]).astype(BF16)

    k_to_sib.wait_send()
    w_to_sib.wait_send()
    for i in (1, 2, 3):
        k_direct(i).wait_send()
        k_handed(i).wait_send()
        w_direct(i).wait_send()
        w_handed(i).wait_send()

    def sent(k, _):
        w = piece(k)
        for i in (1, 2, 3):
            to_y(w, i).wait_send()
        to_z(w).wait_send()
        return 0

    lax.fori_loop(0, 8, sent, 0)


def attend(offsets, queries, keys, values, out_proj, residual, gain):
    vm = pl.BlockSpec(memory_space=pltpu.VMEM)
    hbm = pl.BlockSpec(memory_space=pl.ANY)
    dma = pltpu.SemaphoreType.DMA
    return pl.pallas_call(
        attn_kernel,
        out_shape=(jax.ShapeDtypeStruct((TOK, D), F32), jax.ShapeDtypeStruct((TOK, D), BF16)),
        in_specs=[pl.BlockSpec(memory_space=pltpu.SMEM)] + [hbm] * 6,
        out_specs=(vm, vm),
        scratch_shapes=[
            pltpu.VMEM((SPAN, HEADS), BF16),
            pltpu.VMEM((TOK, D), BF16),
            pltpu.VMEM((1, D), F32),
            pltpu.VMEM((PEERS * SPAN, 2 * HD), BF16),
            pltpu.VMEM((PEERS * HEADS, 512), BF16),
            pltpu.VMEM((8 * SPAN, HD), F32),
            pltpu.VMEM((8 * SPAN, 2 * HD), F32),
            pltpu.VMEM((SPAN, HEADS), BF16),
            pltpu.VMEM((PEERS * SPAN, 512), BF16),
            pltpu.VMEM((PEERS * 3 * 2 * TOK, 512), BF16),
            pltpu.VMEM((2 * TOK, 512), F32),
            pltpu.VMEM((PEERS * TOK, 512), BF16),
            pltpu.VMEM((PEERS * TOK, 512), BF16),
            dma((6,)), dma((7,)), dma((7,)), dma((7,)), dma((7,)),
            dma((PEERS, 3)), dma((PEERS, 3)), dma((PEERS,)), dma((PEERS,)),
        ],
        compiler_params=pltpu.CompilerParams(
            collective_id=2, has_side_effects=True, vmem_limit_bytes=62 * 1024 * 1024
        ),
        cost_estimate=pl.CostEstimate(flops=9_000_000_000, bytes_accessed=4_000_000, transcendentals=10_000_000),
        name="attend",
    )(offsets, queries, keys, values, out_proj, residual, gain)


def shards(
    queries, keys, values, offsets, out_proj, residual, norm_gain, expert_ids, gate_probs, w_gate, w_up, w_down,
):
    hidden, normed = attend(offsets, queries, keys, values, out_proj, residual, norm_gain[None, :])
    return moe(hidden, normed, expert_ids.T, gate_probs.T, w_gate, w_up, w_down)


def solution(mesh):
    return jax.shard_map(
        shards,
        mesh=mesh,
        in_specs=(
            P(("dp", "ctx"), "exp"),
            P(("dp", "ctx"), None),
            P(("dp", "ctx"), None),
            P("dp"),
            P("exp", "ctx"),
            P(("dp", "ctx", "exp"), None),
            P(),
            P(("dp", "ctx", "exp"), None),
            P(("dp", "ctx", "exp"), None),
            P(("ctx", "exp"), None, None),
            P(("ctx", "exp"), None, None),
            P(("ctx", "exp"), None, None),
        ),
        out_specs=P(("dp", "ctx", "exp"), None),
        check_vma=False,
    )
```

```python
import math

import jax
import jax.numpy as jnp
from jax import lax
from jax.experimental import pallas as pl
from jax.experimental.pallas import tpu as pltpu
from jax.sharding import PartitionSpec as P

KVH = 4
HD = 128
D = 4096
HALF = D // 2
FF = 768
TOK = 48
CAP = 12
PEERS = 8
BLK = PEERS * CAP
SLOTS = PEERS * BLK
SPAN = PEERS * TOK
HEADS = 8 * HD

NEG_FILL = -1e30
MESH = pl.DeviceIdType.MESH
F32 = jnp.float32
BF16 = jnp.bfloat16


def over(a, n):
    return ((a.astype(F32) + 0.5) * (1.0 / n)).astype(jnp.int32)


def route_table(packed, expert_of, count, code, prob, member):
    ids, probs = packed[:8], packed[8:]
    width = packed.shape[1]
    for j in range(count):
        named = ids == expert_of(j).astype(F32)
        member[j:j + 1, :] = jnp.sum(jnp.where(named, 1.0, 0.0), axis=0, keepdims=True)
        prob[j:j + 1, :] = jnp.sum(jnp.where(named, probs, 0.0), axis=0, keepdims=True)
    before = lax.broadcasted_iota(jnp.int32, (width, width), 0)
    t = lax.broadcasted_iota(jnp.int32, (width, width), 1)
    block = over(t, TOK)
    earlier = jnp.where((before < t) & (before >= block * TOK), 1.0, 0.0).astype(BF16)
    inside = member[...]
    rank = jnp.dot(inside.astype(BF16), earlier, preferred_element_type=F32)
    code[...] = jnp.where(inside > 0.5, block[:8] * CAP + rank.astype(jnp.int32), -1)


def moe_kernel(
    hid_ref, nrm_ref, ids_ref, probs_ref, wg_hbm, wu_hbm, wd_hbm,
    out_ref,
    gat_a, gat_b, snd_a, snd_b, arr_a, arr_b, ret_a, ret_b, fin_a, fin_b, sib_b, zed, zin,
    xb, act, act_b, pm, wt_a, wt_b, wg, wu, wd,
    rts_a, rts_b, code_a, code_b, prob_a, prob_b, member_a, member_b, keep,
    w_sem, s_sem, r_sem,
):
    dp, c, e = lax.axis_index("dp"), lax.axis_index("ctx"), lax.axis_index("exp")
    x, core, y, zh = c // 2, lax.rem(c, 2), e // 2, lax.rem(e, 2)
    v = lax.rem(dp + e, 2)
    sib = 2 * x + 1 - core
    place_b = core * 4 + x

    def at_exp(other):
        return (lax.rem(v + other, 2), c, other)

    def at_ctx(other):
        return (dp, other, e)

    def at_far(other):
        return (1 - dp, other, 2 * y + 1 - zh)

    def chip_x(i):
        return lax.rem(x + i, 4)

    def at_x(i):
        return (dp, 2 * chip_x(i) + core, e)

    def row_y(i):
        return lax.rem(y + i, 4)

    def at_y(i):
        return (dp, c, 2 * row_y(i) + zh)

    at_sib = (dp, sib, e)
    at_z = at_far(c)

    weights = [
        pltpu.make_async_copy(src.at[0], dst, w_sem.at[i])
        for i, (src, dst) in enumerate(((wg_hbm, wg), (wu_hbm, wu), (wd_hbm, wd)))
    ]
    for w in weights:
        w.start()

    def rows(ref, index, size):
        return ref.at[pl.ds(pl.multiple_of(index * size, 16), size)]

    def copy(src, dst, stage, sent, got, dev):
        return pltpu.make_async_remote_copy(
            src_ref=src, dst_ref=dst, send_sem=s_sem.at[stage, sent], recv_sem=r_sem.at[stage, got],
            device_id=dev, device_id_type=MESH,
        )

    def same(ref, stage, index):
        return copy(ref, ref, stage, index, index, at_sib)

    def block_a(q, oy):
        return rows(gat_a, 4 * q + oy, TOK)

    def block_b(q, who, ox):
        return rows(gat_b, 8 * q + 4 * who + ox, TOK)

    barrier = pltpu.get_barrier_semaphore()

    def greet(i, _):
        oe, oc = lax.rem(e + i, PEERS), lax.rem(c + i, PEERS)
        for dev in (at_exp(oe), at_ctx(oc), at_far(oc)):
            pl.semaphore_signal(barrier, 1, device_id=dev, device_id_type=MESH)
        return 0

    lax.fori_loop(1, PEERS, greet, 0)
    block_a(0, y)[...] = nrm_ref[:, :HALF]
    block_b(0, core, x)[...] = nrm_ref[:, HALF:]
    pl.semaphore_wait(barrier, 3 * (PEERS - 1))

    def along(q):
        a, b = block_a(q, y), block_b(q, core, x)
        for i in (1, 3, 2):
            copy(a, a, q, i, i, at_y(i)).start()
            copy(b, b, 2 + q, i, i, at_x(i)).start()
        copy(b, b, 2 + q, 4, 4, at_sib).start()

    copy(block_a(0, y), block_a(1, y), 18, 0, 0, at_z).start()
    copy(block_b(0, core, x), block_b(1, core, x), 18, 1, 1, at_z).start()
    along(0)
    for rts, index, place, width in ((rts_a, y, y, 4 * TOK), (rts_b, place_b, place_b, SPAN)):
        token = lax.broadcasted_iota(jnp.int32, (TOK, width), 0)
        lane = lax.broadcasted_iota(jnp.int32, (TOK, width), 1)
        put = jnp.where(lane == token + place * TOK, 1.0, 0.0)
        spread = [
            jnp.dot(a, put, preferred_element_type=F32, precision=lax.Precision.HIGHEST)
            for a in (ids_ref[...].astype(F32), probs_ref[...])
        ]
        rows(rts, index, 16)[...] = jnp.concatenate(spread, axis=0)

    def slot_e(oe):
        far = lax.rem(oe + e, 2)
        return 4 * far + oe // 2, 4 * far + y

    def routes(i, _):
        oe, oc = lax.rem(e + i, PEERS), lax.rem(c + i, PEERS)
        _, mine = slot_e(oe)
        copy(rows(rts_a, y, 16), rows(rts_a, mine, 16), 19, i, mine, at_exp(oe)).start()
        own = rows(rts_b, place_b, 16)
        copy(own, own, 20, i, place_b, at_ctx(oc)).start()
        copy(own, rows(rts_b, 8 + place_b, 16), 21, i, place_b, at_far(oc)).start()
        return 0

    lax.fori_loop(1, PEERS, routes, 0)
    copy(rows(rts_b, place_b, 16), rows(rts_b, 8 + place_b, 16), 21, 0, place_b, at_z).start()
    same(block_a(1, y), 18, 0).wait_recv()
    same(block_b(1, core, x), 18, 1).wait_recv()
    along(1)

    i = lax.broadcasted_iota(jnp.int32, (4 * BLK, 4 * BLK), 0)
    at = lax.broadcasted_iota(jnp.int32, (4 * BLK, 4 * BLK), 1)
    from_c = over(i, TOK)
    rest = i - from_c * TOK
    from_y = over(rest, CAP)
    from_x = over(from_c, 2)
    want = from_y * BLK + ((from_c - 2 * from_x) * 4 + from_x) * CAP + rest - from_y * CAP
    pm[...] = jnp.where(at == want, 1.0, 0.0).astype(BF16)

    def hand_on(q, i):
        block = block_b(q, core, chip_x(4 - i))
        same(block, 2 + q, i).wait_recv()
        copy(block, block, 4 + q, i, i, at_sib).start()

    hand_on(0, 1)
    hand_on(0, 3)

    def routes_in(i, _):
        oe, oc = lax.rem(e + i, PEERS), lax.rem(c + i, PEERS)
        theirs, _ = slot_e(oe)
        same(rows(rts_a, theirs, 16), 19, theirs).wait_recv()
        other = lax.rem(oc, 2) * 4 + oc // 2
        same(rows(rts_b, other, 16), 20, other).wait_recv()
        same(rows(rts_b, 8 + other, 16), 21, other).wait_recv()
        return 0

    lax.fori_loop(1, PEERS, routes_in, 0)
    same(rows(rts_b, 8 + place_b, 16), 21, place_b).wait_recv()
    hand_on(0, 2)

    def gathered(rts, first, count):
        packed = rts[first * 16:first * 16 + 16, :]
        for k in range(first + 1, first + count):
            packed += rts[k * 16:k * 16 + 16, :]
        return packed

    member_b[...] = jnp.zeros_like(member_b)
    for q in range(2):
        route_table(
            gathered(rts_a, 4 * q, 4), lambda j: j * PEERS + e, PEERS, code_a.at[q], prob_a.at[q], member_a
        )
        route_table(
            gathered(rts_b, 8 * q, 8), lambda j: c * PEERS + 2 * j + zh, 4, code_b.at[q], prob_b.at[q], member_b
        )
    for i in (1, 3, 2):
        hand_on(1, i)

    slot_a = lax.broadcasted_iota(jnp.int32, (TOK, 4 * TOK), 0)
    slot_b = lax.broadcasted_iota(jnp.int32, (BLK, SPAN), 0)

    def select(q):
        for k in range(PEERS):
            wt_a[k * TOK:(k + 1) * TOK, :] = jnp.where(
                code_a[q, k:k + 1, :] == slot_a, 1.0, 0.0
            ).astype(BF16)
        for k in range(4):
            wt_b[k * BLK:(k + 1) * BLK, :] = jnp.where(
                code_b[q, k:k + 1, :] == slot_b, 1.0, 0.0
            ).astype(BF16)
        part = slice(q * SPAN, q * SPAN + SPAN)

        def tile(n, _):
            cols = pl.ds(pl.multiple_of(n * 512, 512), 512)
            snd_a[part, cols] = jnp.dot(
                wt_a[...], gat_a[q * 4 * TOK:(q + 1) * 4 * TOK, cols], preferred_element_type=F32
            ).astype(BF16)
            snd_b[part, cols] = jnp.dot(
                wt_b[...], gat_b[part, cols], preferred_element_type=F32
            ).astype(BF16)
            return 0

        lax.fori_loop(0, HALF // 512, tile, 0)

    def exchange(q, dst_a, dst_b, stage):
        for i in (1, 3, 2):
            for k in range(2):
                oc = 2 * chip_x(i) + k
                copy(
                    rows(snd_a, 8 * q + oc, TOK), rows(dst_a, 8 * q + c, TOK), stage + q, oc, c, at_ctx(oc)
                ).start()
            copy(
                rows(snd_b, 4 * q + row_y(i), BLK), rows(dst_b, 4 * q + y, BLK), stage + 2 + q, i, i, at_y(i)
            ).start()
        copy(rows(snd_a, 8 * q + sib, TOK), rows(dst_a, 8 * q + c, TOK), stage + q, sib, c, at_sib).start()
        rows(dst_a, 8 * q + c, TOK)[...] = rows(snd_a, 8 * q + c, TOK)[...]
        rows(dst_b, 4 * q + y, BLK)[...] = rows(snd_b, 4 * q + y, BLK)[...]

    def exchange_in(q, dst_a, dst_b, stage):
        for i in (1, 3, 2):
            same(rows(dst_b, 4 * q + row_y(4 - i), BLK), stage + 2 + q, i).wait_recv()

        def body(i, _):
            oc = lax.rem(c + i, PEERS)
            same(rows(dst_a, 8 * q + oc, TOK), stage + q, oc).wait_recv()
            return 0

        lax.fori_loop(1, PEERS, body, 0)

    def exchange_out(q, stage):
        for i in (1, 3, 2):
            same(rows(snd_b, 4 * q + row_y(i), BLK), stage + 2 + q, i).wait_send()

        def body(i, _):
            oc = lax.rem(c + i, PEERS)
            same(rows(snd_a, 8 * q + oc, TOK), stage + q, oc).wait_send()
            return 0

        lax.fori_loop(1, PEERS, body, 0)

    for q in (1, 0):
        for i in (1, 3, 2):
            same(block_a(q, row_y(4 - i)), q, i).wait_recv()
            same(block_b(q, 1 - core, chip_x(4 - i)), 4 + q, i).wait_recv()
        same(block_b(q, 1 - core, x), 2 + q, 4).wait_recv()
        select(q)
        if q == 0:
            exchange_out(1, 6)
        exchange(q, arr_a, arr_b, 6)

    for w in weights:
        w.wait()

    def experts(q):
        part = slice(q * SPAN, q * SPAN + SPAN)

        def reorder(n, _):
            cols = pl.ds(pl.multiple_of(n * 512, 512), 512)
            xb[:, cols] = jnp.dot(pm[...], arr_b[part, cols], preferred_element_type=F32).astype(BF16)
            return 0

        lax.fori_loop(0, HALF // 512, reorder, 0)

        def hidden_tile(n, _):
            cols = pl.ds(pl.multiple_of(n * 256, 256), 256)
            a, b = arr_a[part, :], xb[...]
            gate = jnp.dot(a, wg[:HALF, cols], preferred_element_type=F32)
            gate += jnp.dot(b, wg[HALF:, cols], preferred_element_type=F32)
            up = jnp.dot(a, wu[:HALF, cols], preferred_element_type=F32)
            up += jnp.dot(b, wu[HALF:, cols], preferred_element_type=F32)
            act[:, cols] = (gate / (1.0 + jnp.exp(-gate)) * up).astype(BF16)
            return 0

        lax.fori_loop(0, FF // 256, hidden_tile, 0)
        act_b[...] = lax.dot_general(
            pm[...], act[...], (((0,), (0,)), ((), ())), preferred_element_type=F32
        ).astype(BF16)

        def down(n, _):
            cols = pl.ds(pl.multiple_of(n * 512, 512), 512)
            late = pl.ds(pl.multiple_of(n * 512 + HALF, 512), 512)
            snd_a[part, cols] = jnp.dot(act[...], wd[:, cols], preferred_element_type=F32).astype(BF16)
            snd_b[part, cols] = jnp.dot(act_b[...], wd[:, late], preferred_element_type=F32).astype(BF16)
            return 0

        lax.fori_loop(0, HALF // 512, down, 0)

    for q in (1, 0):
        exchange_in(q, arr_a, arr_b, 6)
        if q == 0:
            exchange_out(0, 6)
        experts(q)
        exchange(q, ret_a, ret_b, 10)

    for q in range(2):
        for i in (1, 2, 3):
            same(block_a(q, y), q, i).wait_send()
            same(block_b(q, core, x), 2 + q, i).wait_send()
            same(block_b(q, core, x), 4 + q, i).wait_send()
        same(block_b(q, core, x), 2 + q, 4).wait_send()
    same(block_a(0, y), 18, 0).wait_send()
    same(block_b(0, core, x), 18, 1).wait_send()

    def half_b(q, who):
        return rows(gat_b, 2 * q + who, 4 * TOK)

    def mix(q):
        for k in range(PEERS):
            wt_a[k * TOK:(k + 1) * TOK, :] = jnp.where(
                code_a[q, k:k + 1, :] == slot_a, prob_a[q, k:k + 1, :], 0.0
            ).astype(BF16)
        for k in range(4):
            wt_b[k * BLK:(k + 1) * BLK, :] = jnp.where(
                code_b[q, k:k + 1, :] == slot_b, prob_b[q, k:k + 1, :], 0.0
            ).astype(BF16)
        part = slice(q * SPAN, q * SPAN + SPAN)

        def tile_b(n, _):
            cols = pl.ds(pl.multiple_of(n * 512, 512), 512)
            gat_b[part, cols] = lax.dot_general(
                wt_b[...], ret_b[part, cols], (((0,), (0,)), ((), ())), preferred_element_type=F32
            ).astype(BF16)
            return 0

        def tile_a(n, _):
            cols = pl.ds(pl.multiple_of(n * 512, 512), 512)
            gat_a[q * 4 * TOK:(q + 1) * 4 * TOK, cols] = lax.dot_general(
                wt_a[...], ret_a[part, cols], (((0,), (0,)), ((), ())), preferred_element_type=F32
            ).astype(BF16)
            return 0

        lax.fori_loop(0, HALF // 512, tile_b, 0)
        copy(half_b(q, 1 - core), rows(sib_b, q, 4 * TOK), 16 + q, 0, 0, at_sib).start()
        lax.fori_loop(0, HALF // 512, tile_a, 0)
        for i in (1, 3, 2):
            copy(block_a(q, row_y(i)), rows(fin_a, 3 * q + i - 1, TOK), 14 + q, i, i, at_y(i)).start()
        same(rows(sib_b, q, 4 * TOK), 16 + q, 0).wait_recv()
        for i in (1, 3, 2, 0):
            own = block_b(q, core, chip_x(i))
            own[...] = (
                own[...].astype(F32) + rows(sib_b, 4 * q + chip_x(i), TOK)[...].astype(F32)
            ).astype(BF16)
            if i:
                copy(own, rows(fin_b, 3 * q + i - 1, TOK), 16 + q, i, i, at_x(i)).start()

    for q in (1, 0):
        exchange_in(q, ret_a, ret_b, 10)
        mix(q)

    def home(q, own, fin, stage):
        total = own[...].astype(F32)
        for i in (1, 3, 2):
            same(rows(fin, 3 * q + i - 1, TOK), stage + q, i).wait_recv()
        for i in range(3):
            total += rows(fin, 3 * q + i, TOK)[...].astype(F32)
        return total

    zed[:TOK, :] = home(1, block_a(1, y), fin_a, 14).astype(BF16)
    copy(zed.at[:TOK], zin.at[:TOK], 18, 2, 2, at_z).start()
    zed[TOK:, :] = home(1, block_b(1, core, x), fin_b, 16).astype(BF16)
    copy(zed.at[TOK:], zin.at[TOK:], 18, 3, 3, at_z).start()
    keep[:TOK, :] = hid_ref[:, :HALF] + home(0, block_a(0, y), fin_a, 14)
    keep[TOK:, :] = hid_ref[:, HALF:] + home(0, block_b(0, core, x), fin_b, 16)
    same(zin.at[:TOK], 18, 2).wait_recv()
    out_ref[:, :HALF] = (keep[:TOK, :] + zin[:TOK, :].astype(F32)).astype(BF16)
    same(zin.at[TOK:], 18, 3).wait_recv()
    out_ref[:, HALF:] = (keep[TOK:, :] + zin[TOK:, :].astype(F32)).astype(BF16)

    same(zed.at[:TOK], 18, 2).wait_send()
    same(zed.at[TOK:], 18, 3).wait_send()
    for q in range(2):
        exchange_out(q, 10)
        for i in (1, 2, 3):
            same(block_a(q, row_y(i)), 14 + q, i).wait_send()
            same(block_b(q, core, chip_x(i)), 16 + q, i).wait_send()
        same(half_b(q, 1 - core), 16 + q, 0).wait_send()

    def routes_out(i, _):
        same(rows(rts_a, y, 16), 19, i).wait_send()
        same(rows(rts_b, place_b, 16), 20, i).wait_send()
        same(rows(rts_b, place_b, 16), 21, i).wait_send()
        return 0

    lax.fori_loop(1, PEERS, routes_out, 0)
    same(rows(rts_b, place_b, 16), 21, 0).wait_send()


def moe(hidden, normed, ids, probs, w_gate, w_up, w_down):
    vm = pl.BlockSpec(memory_space=pltpu.VMEM)
    hbm = pl.BlockSpec(memory_space=pl.ANY)
    half = [8 * TOK, 16 * TOK] + [SLOTS] * 6 + [6 * TOK, 6 * TOK, 8 * TOK, 2 * TOK, 2 * TOK, SPAN]
    return pl.pallas_call(
        moe_kernel,
        out_shape=jax.ShapeDtypeStruct((TOK, D), BF16),
        in_specs=[vm] * 4 + [hbm] * 3,
        out_specs=vm,
        scratch_shapes=[pltpu.VMEM((n, HALF), BF16) for n in half] + [
            pltpu.VMEM((SPAN, FF), BF16),
            pltpu.VMEM((SPAN, FF), BF16),
            pltpu.VMEM((4 * BLK, 4 * BLK), BF16),
            pltpu.VMEM((PEERS * TOK, 4 * TOK), BF16),
            pltpu.VMEM((4 * BLK, SPAN), BF16),
            pltpu.VMEM((D, FF), BF16),
            pltpu.VMEM((D, FF), BF16),
            pltpu.VMEM((FF, D), BF16),
            pltpu.VMEM((PEERS * 16, 4 * TOK), F32),
            pltpu.VMEM((2 * PEERS * 16, SPAN), F32),
            pltpu.VMEM((2, PEERS, 4 * TOK), jnp.int32),
            pltpu.VMEM((2, PEERS, SPAN), jnp.int32),
            pltpu.VMEM((2, PEERS, 4 * TOK), F32),
            pltpu.VMEM((2, PEERS, SPAN), F32),
            pltpu.VMEM((PEERS, 4 * TOK), F32),
            pltpu.VMEM((PEERS, SPAN), F32),
            pltpu.VMEM((2 * TOK, HALF), F32),
            pltpu.SemaphoreType.DMA((3,)),
            pltpu.SemaphoreType.DMA((22, PEERS)),
            pltpu.SemaphoreType.DMA((22, PEERS)),
        ],
        compiler_params=pltpu.CompilerParams(
            collective_id=1, has_side_effects=True, vmem_limit_bytes=62 * 1024 * 1024
        ),
        cost_estimate=pl.CostEstimate(flops=18_000_000_000, bytes_accessed=20_000_000, transcendentals=600_000),
        name="moe",
    )(hidden, normed, ids, probs, w_gate, w_up, w_down)


def attn_kernel(
    off_ref, q_hbm, k_hbm, v_hbm, w_hbm, res_hbm, gain_hbm,
    hid_ref, nrm_ref,
    q_ref, res_ref, gain_ref, kv, wbuf, mx, acc, att, pbuf, rbuf, tot, zsnd, zbuf,
    l_sem, kv_s, kv_r, w_s, w_r, y_s, y_r, z_s, z_r,
):
    dp, c, e = lax.axis_index("dp"), lax.axis_index("ctx"), lax.axis_index("exp")
    x, core, y, zh = c // 2, lax.rem(c, 2), e // 2, lax.rem(e, 2)
    sib = 2 * x + 1 - core

    def at_x(i):
        return (dp, 2 * lax.rem(x + i, 4) + core, e)

    def at_y(i):
        return (dp, c, 2 * lax.rem(y + i, 4) + zh)

    at_sib = (dp, sib, e)
    at_z = (dp, c, 2 * y + 1 - zh)

    def rows(ref, index, size):
        return ref.at[pl.ds(pl.multiple_of(index * size, 16), size)]

    def remote(src, dst, s, r, dev):
        return pltpu.make_async_remote_copy(
            src_ref=src, dst_ref=dst, send_sem=s, recv_sem=r, device_id=dev, device_id_type=MESH
        )

    kv_head = lax.rem(y, KVH)
    cols = pl.ds(pl.multiple_of(kv_head * HD, HD), HD)
    own = rows(kv, c, SPAN)
    loads = [
        pltpu.make_async_copy(k_hbm.at[:, cols], own.at[:, :HD], l_sem.at[0]),
        pltpu.make_async_copy(v_hbm.at[:, cols], own.at[:, HD:], l_sem.at[1]),
        pltpu.make_async_copy(w_hbm, rows(wbuf, c, HEADS), l_sem.at[2]),
        pltpu.make_async_copy(q_hbm, q_ref, l_sem.at[3]),
        pltpu.make_async_copy(res_hbm, res_ref, l_sem.at[4]),
        pltpu.make_async_copy(gain_hbm, gain_ref, l_sem.at[5]),
    ]
    for load in loads:
        load.start()
    barrier = pltpu.get_barrier_semaphore()
    peers = [at_x(i) for i in (1, 2, 3)] + [at_y(i) for i in (1, 2, 3)] + [at_sib, at_z]
    for dev in peers:
        pl.semaphore_signal(barrier, 1, device_id=dev, device_id_type=MESH)
    loads[0].wait()
    loads[1].wait()
    pl.semaphore_wait(barrier, len(peers))

    def copies(buf, size, s, r):
        def direct(i):
            return remote(rows(buf, c, size), rows(buf, c, size), s.at[i], r.at[i], at_x(i))

        def arrival(i):
            block = rows(buf, 2 * lax.rem(x + 4 - i, 4) + core, size)
            return remote(block, block, s.at[3 + i], r.at[i], at_sib)

        def handed(i):
            block = rows(buf, 2 * lax.rem(x + 4 - i, 4) + core, size)
            return remote(block, block, s.at[3 + i], r.at[3 + i], at_sib)

        def handed_arrival(i):
            block = rows(buf, 2 * lax.rem(x + 4 - i, 4) + 1 - core, size)
            return remote(block, block, s.at[3 + i], r.at[3 + i], at_sib)

        to_sib = remote(rows(buf, c, size), rows(buf, c, size), s.at[0], r.at[0], at_sib)
        from_sib = remote(rows(buf, sib, size), rows(buf, sib, size), s.at[0], r.at[0], at_sib)
        return direct, arrival, handed, handed_arrival, to_sib, from_sib

    k_direct, k_arrival, k_handed, k_handed_arrival, k_to_sib, k_from_sib = copies(kv, SPAN, kv_s, kv_r)
    w_direct, w_arrival, w_handed, w_handed_arrival, w_to_sib, w_from_sib = copies(wbuf, HEADS, w_s, w_r)
    k_to_sib.start()
    for i in (1, 3, 2):
        k_direct(i).start()

    scale = HD ** (-0.5) * math.log2(math.e)
    lane = lax.broadcasted_iota(jnp.int32, (1, 2 * SPAN), 1)
    ones = jnp.ones((2 * SPAN, HD), BF16)

    def group(i):
        chip = lax.rem(x + 4 - i, 4)
        at = pl.ds(pl.multiple_of(chip * 2 * SPAN, 2 * SPAN), 2 * SPAN)
        first, second = off_ref[2 * chip], off_ref[2 * chip + 1]
        key_pos = jnp.where(lane < SPAN, first + lane, second + lane - SPAN)
        if i:
            bias = jnp.where(key_pos <= off_ref[c] + SPAN - 1, 0.0, NEG_FILL)

        def head(h, _):
            hcols = pl.ds(pl.multiple_of(h * HD, HD), HD)
            mine = pl.ds(pl.multiple_of(h * SPAN, SPAN), SPAN)
            s = lax.dot_general(
                q_ref[:, hcols], kv[at, :HD], (((1,), (1,)), ((), ())), preferred_element_type=F32
            ) * scale
            if i:
                s = s + bias
            else:
                query_pos = off_ref[c] + lax.broadcasted_iota(jnp.int32, (SPAN, 1), 0)
                s = jnp.where(key_pos <= query_pos, s, NEG_FILL)
            top = jnp.max(s, axis=1, keepdims=True)
            if i:
                old = mx[mine, :]
                new = jnp.maximum(old, top)
                p = jnp.exp2(s - jnp.concatenate([new] * 6, axis=1)).astype(BF16)
            else:
                new = jnp.broadcast_to(top, (SPAN, HD))
                p = jnp.exp2(s - top).astype(BF16)
            mixed = jnp.dot(
                p, jnp.concatenate([kv[at, HD:], ones], axis=1), preferred_element_type=F32
            )
            if i:
                keep = jnp.exp2(old - new)
                mixed = acc[mine, :] * jnp.concatenate([keep, keep], axis=1) + mixed
            mx[mine, :] = new
            acc[mine, :] = mixed
            return 0

        lax.fori_loop(0, 8, head, 0)

    loads[2].wait()
    w_to_sib.start()
    for i in (1, 3, 2):
        w_direct(i).start()
    for load in loads[3:]:
        load.wait()
    k_from_sib.wait_recv()
    group(0)
    for i in (1, 3):
        k_arrival(i).wait_recv()
        k_handed(i).start()
    k_handed_arrival(1).wait_recv()
    group(1)
    k_arrival(2).wait_recv()
    k_handed(2).start()
    k_handed_arrival(3).wait_recv()
    group(3)
    k_handed_arrival(2).wait_recv()
    group(2)

    def divide(h, _):
        hcols = pl.ds(pl.multiple_of(h * HD, HD), HD)
        mine = pl.ds(pl.multiple_of(h * SPAN, SPAN), SPAN)
        att[:, hcols] = (acc[mine, :HD] / acc[mine, HD:]).astype(BF16)
        return 0

    lax.fori_loop(0, 8, divide, 0)

    def piece(k):
        k2 = k // 2
        chip = lax.rem(x + 4 - lax.rem(k2 * (k2 + 1) // 2, 4), 4)
        return 2 * chip + lax.rem(core + k, 2)

    def to_y(w, i):
        return remote(
            rows(pbuf, w * 4 + lax.rem(y + i, 4), 2 * TOK), rows(rbuf, w * 3 + i - 1, 2 * TOK),
            y_s.at[w, i - 1], y_r.at[w, i - 1], at_y(i),
        )

    def to_z(w):
        return remote(rows(zsnd, w, TOK), rows(zbuf, w, TOK), z_s.at[w], z_r.at[w], at_z)

    def project(k, _):
        w = piece(k)
        rows(pbuf, w, SPAN)[...] = jnp.dot(
            att[...], rows(wbuf, w, HEADS)[...], preferred_element_type=F32
        ).astype(BF16)
        for i in (1, 3, 2):
            to_y(w, i).start()
        return 0

    def reduce(k, _):
        w = piece(k)
        total = rows(pbuf, w * 4 + y, 2 * TOK)[...].astype(F32)
        for i in (1, 3, 2):
            to_y(w, i).wait_recv()
            total += rows(rbuf, w * 3 + i - 1, 2 * TOK)[...].astype(F32)
        tot[...] = total
        rows(zsnd, w, TOK)[...] = rows(tot, 1 - zh, TOK)[...].astype(BF16)
        to_z(w).start()
        wcols = pl.ds(pl.multiple_of(w * 512, 512), 512)
        hid_ref[:, wcols] = rows(tot, zh, TOK)[...] + res_ref[:, wcols].astype(F32)
        return 0

    w_from_sib.wait_recv()
    lax.fori_loop(0, 2, project, 0)
    for i in (1, 3):
        w_arrival(i).wait_recv()
        w_handed(i).start()
    for i in (1, 3):
        w_handed_arrival(i).wait_recv()
    lax.fori_loop(2, 6, project, 0)
    w_arrival(2).wait_recv()
    w_handed(2).start()
    lax.fori_loop(0, 2, reduce, 0)
    w_handed_arrival(2).wait_recv()
    lax.fori_loop(6, 8, project, 0)
    lax.fori_loop(2, 8, reduce, 0)

    square = jnp.zeros((TOK, 1), F32)

    def finish(k, square):
        w = piece(k)
        to_z(w).wait_recv()
        wcols = pl.ds(pl.multiple_of(w * 512, 512), 512)
        h = hid_ref[:, wcols] + rows(zbuf, w, TOK)[...].astype(F32)
        hid_ref[:, wcols] = h
        return square + jnp.sum(h * h, axis=1, keepdims=True)

    square = lax.fori_loop(0, 8, finish, square)
    inverse = lax.rsqrt(square * (1.0 / D) + 1e-06)
    nrm_ref[...] = (hid_ref[...] * inverse * gain_ref[...]).astype(BF16)

    k_to_sib.wait_send()
    w_to_sib.wait_send()
    for i in (1, 2, 3):
        k_direct(i).wait_send()
        k_handed(i).wait_send()
        w_direct(i).wait_send()
        w_handed(i).wait_send()

    def sent(k, _):
        w = piece(k)
        for i in (1, 2, 3):
            to_y(w, i).wait_send()
        to_z(w).wait_send()
        return 0

    lax.fori_loop(0, 8, sent, 0)


def attend(offsets, queries, keys, values, out_proj, residual, gain):
    vm = pl.BlockSpec(memory_space=pltpu.VMEM)
    hbm = pl.BlockSpec(memory_space=pl.ANY)
    dma = pltpu.SemaphoreType.DMA
    return pl.pallas_call(
        attn_kernel,
        out_shape=(jax.ShapeDtypeStruct((TOK, D), F32), jax.ShapeDtypeStruct((TOK, D), BF16)),
        in_specs=[pl.BlockSpec(memory_space=pltpu.SMEM)] + [hbm] * 6,
        out_specs=(vm, vm),
        scratch_shapes=[
            pltpu.VMEM((SPAN, HEADS), BF16),
            pltpu.VMEM((TOK, D), BF16),
            pltpu.VMEM((1, D), F32),
            pltpu.VMEM((PEERS * SPAN, 2 * HD), BF16),
            pltpu.VMEM((PEERS * HEADS, 512), BF16),
            pltpu.VMEM((8 * SPAN, HD), F32),
            pltpu.VMEM((8 * SPAN, 2 * HD), F32),
            pltpu.VMEM((SPAN, HEADS), BF16),
            pltpu.VMEM((PEERS * SPAN, 512), BF16),
            pltpu.VMEM((PEERS * 3 * 2 * TOK, 512), BF16),
            pltpu.VMEM((2 * TOK, 512), F32),
            pltpu.VMEM((PEERS * TOK, 512), BF16),
            pltpu.VMEM((PEERS * TOK, 512), BF16),
            dma((6,)), dma((7,)), dma((7,)), dma((7,)), dma((7,)),
            dma((PEERS, 3)), dma((PEERS, 3)), dma((PEERS,)), dma((PEERS,)),
        ],
        compiler_params=pltpu.CompilerParams(
            collective_id=2, has_side_effects=True, vmem_limit_bytes=62 * 1024 * 1024
        ),
        cost_estimate=pl.CostEstimate(flops=9_000_000_000, bytes_accessed=4_000_000, transcendentals=10_000_000),
        name="attend",
    )(offsets, queries, keys, values, out_proj, residual, gain)


def shards(
    queries, keys, values, offsets, out_proj, residual, norm_gain, expert_ids, gate_probs, w_gate, w_up, w_down,
):
    hidden, normed = attend(offsets, queries, keys, values, out_proj, residual, norm_gain[None, :])
    return moe(hidden, normed, expert_ids.T, gate_probs.T, w_gate, w_up, w_down)


def solution(mesh):
    return jax.shard_map(
        shards,
        mesh=mesh,
        in_specs=(
            P(("dp", "ctx"), "exp"),
            P(("dp", "ctx"), None),
            P(("dp", "ctx"), None),
            P("dp"),
            P("exp", "ctx"),
            P(("dp", "ctx", "exp"), None),
            P(),
            P(("dp", "ctx", "exp"), None),
            P(("dp", "ctx", "exp"), None),
            P(("ctx", "exp"), None, None),
            P(("ctx", "exp"), None, None),
            P(("ctx", "exp"), None, None),
        ),
        out_specs=P(("dp", "ctx", "exp"), None),
        check_vma=False,
    )
```

```python
import math

import jax
import jax.numpy as jnp
from jax import lax
from jax.experimental import pallas as pl
from jax.experimental.pallas import tpu as pltpu
from jax.sharding import PartitionSpec as P

KVH = 4
HD = 128
D = 4096
HALF = D // 2
FF = 768
TOK = 48
CAP = 12
PEERS = 8
BLK = PEERS * CAP
SLOTS = PEERS * BLK
SPAN = PEERS * TOK
HEADS = 8 * HD

NEG_FILL = -1e30
MESH = pl.DeviceIdType.MESH
F32 = jnp.float32
BF16 = jnp.bfloat16


def over(a, n):
    return ((a.astype(F32) + 0.5) * (1.0 / n)).astype(jnp.int32)


def route_table(packed, expert_of, count, code, prob, member):
    ids, probs = packed[:8], packed[8:]
    width = packed.shape[1]
    for j in range(count):
        named = ids == expert_of(j).astype(F32)
        member[j:j + 1, :] = jnp.sum(jnp.where(named, 1.0, 0.0), axis=0, keepdims=True)
        prob[j:j + 1, :] = jnp.sum(jnp.where(named, probs, 0.0), axis=0, keepdims=True)
    before = lax.broadcasted_iota(jnp.int32, (width, width), 0)
    t = lax.broadcasted_iota(jnp.int32, (width, width), 1)
    block = over(t, TOK)
    earlier = jnp.where((before < t) & (before >= block * TOK), 1.0, 0.0).astype(BF16)
    inside = member[...]
    rank = jnp.dot(inside.astype(BF16), earlier, preferred_element_type=F32)
    code[...] = jnp.where(inside > 0.5, block[:8] * CAP + rank.astype(jnp.int32), -1)


def moe_kernel(
    hid_ref, nrm_ref, ids_ref, probs_ref, wg_hbm, wu_hbm, wd_hbm,
    out_ref,
    gat_a, gat_b, snd_a, snd_b, arr_a, arr_b, ret_a, ret_b, fin_a, fin_b, sib_b, zed, zin,
    xb, act, act_b, pm, wt_a, wt_b, wg, wu, wd,
    rts_a, rts_b, code_a, code_b, prob_a, prob_b, member_a, member_b, keep,
    w_sem, s_sem, r_sem,
):
    dp, c, e = lax.axis_index("dp"), lax.axis_index("ctx"), lax.axis_index("exp")
    x, core, y, zh = c // 2, lax.rem(c, 2), e // 2, lax.rem(e, 2)
    v = lax.rem(dp + e, 2)
    sib = 2 * x + 1 - core
    place_b = core * 4 + x

    def at_exp(other):
        return (lax.rem(v + other, 2), c, other)

    def at_ctx(other):
        return (dp, other, e)

    def at_far(other):
        return (1 - dp, other, 2 * y + 1 - zh)

    def chip_x(i):
        return lax.rem(x + i, 4)

    def at_x(i):
        return (dp, 2 * chip_x(i) + core, e)

    def row_y(i):
        return lax.rem(y + i, 4)

    def at_y(i):
        return (dp, c, 2 * row_y(i) + zh)

    at_sib = (dp, sib, e)
    at_z = at_far(c)

    weights = [
        pltpu.make_async_copy(src.at[0], dst, w_sem.at[i])
        for i, (src, dst) in enumerate(((wg_hbm, wg), (wu_hbm, wu), (wd_hbm, wd)))
    ]
    for w in weights:
        w.start()

    def rows(ref, index, size):
        return ref.at[pl.ds(pl.multiple_of(index * size, 16), size)]

    def copy(src, dst, stage, sent, got, dev):
        return pltpu.make_async_remote_copy(
            src_ref=src, dst_ref=dst, send_sem=s_sem.at[stage, sent], recv_sem=r_sem.at[stage, got],
            device_id=dev, device_id_type=MESH,
        )

    def same(ref, stage, index):
        return copy(ref, ref, stage, index, index, at_sib)

    def block_a(q, oy):
        return rows(gat_a, 4 * q + oy, TOK)

    def block_b(q, who, ox):
        return rows(gat_b, 8 * q + 4 * who + ox, TOK)

    barrier = pltpu.get_barrier_semaphore()

    def greet(i, _):
        oe, oc = lax.rem(e + i, PEERS), lax.rem(c + i, PEERS)
        for dev in (at_exp(oe), at_ctx(oc), at_far(oc)):
            pl.semaphore_signal(barrier, 1, device_id=dev, device_id_type=MESH)
        return 0

    lax.fori_loop(1, PEERS, greet, 0)
    block_a(0, y)[...] = nrm_ref[:, :HALF]
    block_b(0, core, x)[...] = nrm_ref[:, HALF:]
    pl.semaphore_wait(barrier, 3 * (PEERS - 1))

    def along(q):
        a, b = block_a(q, y), block_b(q, core, x)
        for i in (1, 3, 2):
            copy(a, a, q, i, i, at_y(i)).start()
            copy(b, b, 2 + q, i, i, at_x(i)).start()
        copy(b, b, 2 + q, 4, 4, at_sib).start()

    copy(block_a(0, y), block_a(1, y), 18, 0, 0, at_z).start()
    copy(block_b(0, core, x), block_b(1, core, x), 18, 1, 1, at_z).start()
    along(0)
    for rts, index, place, width in ((rts_a, y, y, 4 * TOK), (rts_b, place_b, place_b, SPAN)):
        token = lax.broadcasted_iota(jnp.int32, (TOK, width), 0)
        lane = lax.broadcasted_iota(jnp.int32, (TOK, width), 1)
        put = jnp.where(lane == token + place * TOK, 1.0, 0.0)
        spread = [
            jnp.dot(a, put, preferred_element_type=F32, precision=lax.Precision.HIGHEST)
            for a in (ids_ref[...].astype(F32), probs_ref[...])
        ]
        rows(rts, index, 16)[...] = jnp.concatenate(spread, axis=0)

    def slot_e(oe):
        far = lax.rem(oe + e, 2)
        return 4 * far + oe // 2, 4 * far + y

    def routes(i, _):
        oe, oc = lax.rem(e + i, PEERS), lax.rem(c + i, PEERS)
        _, mine = slot_e(oe)
        copy(rows(rts_a, y, 16), rows(rts_a, mine, 16), 19, i, mine, at_exp(oe)).start()
        own = rows(rts_b, place_b, 16)
        copy(own, own, 20, i, place_b, at_ctx(oc)).start()
        copy(own, rows(rts_b, 8 + place_b, 16), 21, i, place_b, at_far(oc)).start()
        return 0

    lax.fori_loop(1, PEERS, routes, 0)
    copy(rows(rts_b, place_b, 16), rows(rts_b, 8 + place_b, 16), 21, 0, place_b, at_z).start()
    same(block_a(1, y), 18, 0).wait_recv()
    same(block_b(1, core, x), 18, 1).wait_recv()
    along(1)

    i = lax.broadcasted_iota(jnp.int32, (4 * BLK, 4 * BLK), 0)
    at = lax.broadcasted_iota(jnp.int32, (4 * BLK, 4 * BLK), 1)
    from_c = over(i, TOK)
    rest = i - from_c * TOK
    from_y = over(rest, CAP)
    from_x = over(from_c, 2)
    want = from_y * BLK + ((from_c - 2 * from_x) * 4 + from_x) * CAP + rest - from_y * CAP
    pm[...] = jnp.where(at == want, 1.0, 0.0).astype(BF16)

    def hand_on(q, i):
        block = block_b(q, core, chip_x(4 - i))
        same(block, 2 + q, i).wait_recv()
        copy(block, block, 4 + q, i, i, at_sib).start()

    hand_on(0, 1)
    hand_on(0, 3)

    def routes_in(i, _):
        oe, oc = lax.rem(e + i, PEERS), lax.rem(c + i, PEERS)
        theirs, _ = slot_e(oe)
        same(rows(rts_a, theirs, 16), 19, theirs).wait_recv()
        other = lax.rem(oc, 2) * 4 + oc // 2
        same(rows(rts_b, other, 16), 20, other).wait_recv()
        same(rows(rts_b, 8 + other, 16), 21, other).wait_recv()
        return 0

    lax.fori_loop(1, PEERS, routes_in, 0)
    same(rows(rts_b, 8 + place_b, 16), 21, place_b).wait_recv()
    hand_on(0, 2)

    def gathered(rts, first, count):
        packed = rts[first * 16:first * 16 + 16, :]
        for k in range(first + 1, first + count):
            packed += rts[k * 16:k * 16 + 16, :]
        return packed

    member_b[...] = jnp.zeros_like(member_b)
    for q in range(2):
        route_table(
            gathered(rts_a, 4 * q, 4), lambda j: j * PEERS + e, PEERS, code_a.at[q], prob_a.at[q], member_a
        )
        route_table(
            gathered(rts_b, 8 * q, 8), lambda j: c * PEERS + 2 * j + zh, 4, code_b.at[q], prob_b.at[q], member_b
        )
    for i in (1, 3, 2):
        hand_on(1, i)

    slot_a = lax.broadcasted_iota(jnp.int32, (TOK, 4 * TOK), 0)
    slot_b = lax.broadcasted_iota(jnp.int32, (BLK, SPAN), 0)

    def select(q):
        for k in range(PEERS):
            wt_a[k * TOK:(k + 1) * TOK, :] = jnp.where(
                code_a[q, k:k + 1, :] == slot_a, 1.0, 0.0
            ).astype(BF16)
        for k in range(4):
            wt_b[k * BLK:(k + 1) * BLK, :] = jnp.where(
                code_b[q, k:k + 1, :] == slot_b, 1.0, 0.0
            ).astype(BF16)
        part = slice(q * SPAN, q * SPAN + SPAN)

        def tile(n, _):
            cols = pl.ds(pl.multiple_of(n * 512, 512), 512)
            snd_a[part, cols] = jnp.dot(
                wt_a[...], gat_a[q * 4 * TOK:(q + 1) * 4 * TOK, cols], preferred_element_type=F32
            ).astype(BF16)
            snd_b[part, cols] = jnp.dot(
                wt_b[...], gat_b[part, cols], preferred_element_type=F32
            ).astype(BF16)
            return 0

        lax.fori_loop(0, HALF // 512, tile, 0)

    def exchange(q, dst_a, dst_b, stage):
        for i in (1, 3, 2):
            for k in range(2):
                oc = 2 * chip_x(i) + k
                copy(
                    rows(snd_a, 8 * q + oc, TOK), rows(dst_a, 8 * q + c, TOK), stage + q, oc, c, at_ctx(oc)
                ).start()
            copy(
                rows(snd_b, 4 * q + row_y(i), BLK), rows(dst_b, 4 * q + y, BLK), stage + 2 + q, i, i, at_y(i)
            ).start()
        copy(rows(snd_a, 8 * q + sib, TOK), rows(dst_a, 8 * q + c, TOK), stage + q, sib, c, at_sib).start()
        rows(dst_a, 8 * q + c, TOK)[...] = rows(snd_a, 8 * q + c, TOK)[...]
        rows(dst_b, 4 * q + y, BLK)[...] = rows(snd_b, 4 * q + y, BLK)[...]

    def exchange_in(q, dst_a, dst_b, stage):
        for i in (1, 3, 2):
            same(rows(dst_b, 4 * q + row_y(4 - i), BLK), stage + 2 + q, i).wait_recv()

        def body(i, _):
            oc = lax.rem(c + i, PEERS)
            same(rows(dst_a, 8 * q + oc, TOK), stage + q, oc).wait_recv()
            return 0

        lax.fori_loop(1, PEERS, body, 0)

    def exchange_out(q, stage):
        for i in (1, 3, 2):
            same(rows(snd_b, 4 * q + row_y(i), BLK), stage + 2 + q, i).wait_send()

        def body(i, _):
            oc = lax.rem(c + i, PEERS)
            same(rows(snd_a, 8 * q + oc, TOK), stage + q, oc).wait_send()
            return 0

        lax.fori_loop(1, PEERS, body, 0)

    for q in (1, 0):
        for i in (1, 3, 2):
            same(block_a(q, row_y(4 - i)), q, i).wait_recv()
            same(block_b(q, 1 - core, chip_x(4 - i)), 4 + q, i).wait_recv()
        same(block_b(q, 1 - core, x), 2 + q, 4).wait_recv()
        select(q)
        if q == 0:
            exchange_out(1, 6)
        exchange(q, arr_a, arr_b, 6)

    for w in weights:
        w.wait()

    def experts(q):
        part = slice(q * SPAN, q * SPAN + SPAN)

        def reorder(n, _):
            cols = pl.ds(pl.multiple_of(n * 512, 512), 512)
            xb[:, cols] = jnp.dot(pm[...], arr_b[part, cols], preferred_element_type=F32).astype(BF16)
            return 0

        lax.fori_loop(0, HALF // 512, reorder, 0)

        def hidden_tile(n, _):
            cols = pl.ds(pl.multiple_of(n * 256, 256), 256)
            a, b = arr_a[part, :], xb[...]
            gate = jnp.dot(a, wg[:HALF, cols], preferred_element_type=F32)
            gate += jnp.dot(b, wg[HALF:, cols], preferred_element_type=F32)
            up = jnp.dot(a, wu[:HALF, cols], preferred_element_type=F32)
            up += jnp.dot(b, wu[HALF:, cols], preferred_element_type=F32)
            act[:, cols] = (gate / (1.0 + jnp.exp(-gate)) * up).astype(BF16)
            return 0

        lax.fori_loop(0, FF // 256, hidden_tile, 0)
        act_b[...] = lax.dot_general(
            pm[...], act[...], (((0,), (0,)), ((), ())), preferred_element_type=F32
        ).astype(BF16)

        def down(n, _):
            cols = pl.ds(pl.multiple_of(n * 512, 512), 512)
            late = pl.ds(pl.multiple_of(n * 512 + HALF, 512), 512)
            snd_a[part, cols] = jnp.dot(act[...], wd[:, cols], preferred_element_type=F32).astype(BF16)
            snd_b[part, cols] = jnp.dot(act_b[...], wd[:, late], preferred_element_type=F32).astype(BF16)
            return 0

        lax.fori_loop(0, HALF // 512, down, 0)

    for q in (1, 0):
        exchange_in(q, arr_a, arr_b, 6)
        if q == 0:
            exchange_out(0, 6)
        experts(q)
        exchange(q, ret_a, ret_b, 10)

    for q in range(2):
        for i in (1, 2, 3):
            same(block_a(q, y), q, i).wait_send()
            same(block_b(q, core, x), 2 + q, i).wait_send()
            same(block_b(q, core, x), 4 + q, i).wait_send()
        same(block_b(q, core, x), 2 + q, 4).wait_send()
    same(block_a(0, y), 18, 0).wait_send()
    same(block_b(0, core, x), 18, 1).wait_send()

    def half_b(q, who):
        return rows(gat_b, 2 * q + who, 4 * TOK)

    def mix(q):
        for k in range(PEERS):
            wt_a[k * TOK:(k + 1) * TOK, :] = jnp.where(
                code_a[q, k:k + 1, :] == slot_a, prob_a[q, k:k + 1, :], 0.0
            ).astype(BF16)
        for k in range(4):
            wt_b[k * BLK:(k + 1) * BLK, :] = jnp.where(
                code_b[q, k:k + 1, :] == slot_b, prob_b[q, k:k + 1, :], 0.0
            ).astype(BF16)
        part = slice(q * SPAN, q * SPAN + SPAN)

        def tile_b(n, _):
            cols = pl.ds(pl.multiple_of(n * 512, 512), 512)
            gat_b[part, cols] = lax.dot_general(
                wt_b[...], ret_b[part, cols], (((0,), (0,)), ((), ())), preferred_element_type=F32
            ).astype(BF16)
            return 0

        def tile_a(n, _):
            cols = pl.ds(pl.multiple_of(n * 512, 512), 512)
            gat_a[q * 4 * TOK:(q + 1) * 4 * TOK, cols] = lax.dot_general(
                wt_a[...], ret_a[part, cols], (((0,), (0,)), ((), ())), preferred_element_type=F32
            ).astype(BF16)
            return 0

        lax.fori_loop(0, HALF // 512, tile_b, 0)
        copy(half_b(q, 1 - core), rows(sib_b, q, 4 * TOK), 16 + q, 0, 0, at_sib).start()
        lax.fori_loop(0, HALF // 512, tile_a, 0)
        for i in (1, 3, 2):
            copy(block_a(q, row_y(i)), rows(fin_a, 3 * q + i - 1, TOK), 14 + q, i, i, at_y(i)).start()
        same(rows(sib_b, q, 4 * TOK), 16 + q, 0).wait_recv()
        for i in (1, 3, 2, 0):
            own = block_b(q, core, chip_x(i))
            own[...] = (
                own[...].astype(F32) + rows(sib_b, 4 * q + chip_x(i), TOK)[...].astype(F32)
            ).astype(BF16)
            if i:
                copy(own, rows(fin_b, 3 * q + i - 1, TOK), 16 + q, i, i, at_x(i)).start()

    for q in (1, 0):
        exchange_in(q, ret_a, ret_b, 10)
        mix(q)

    def home(q, own, fin, stage):
        total = own[...].astype(F32)
        for i in (1, 3, 2):
            same(rows(fin, 3 * q + i - 1, TOK), stage + q, i).wait_recv()
        for i in range(3):
            total += rows(fin, 3 * q + i, TOK)[...].astype(F32)
        return total

    zed[:TOK, :] = home(1, block_a(1, y), fin_a, 14).astype(BF16)
    copy(zed.at[:TOK], zin.at[:TOK], 18, 2, 2, at_z).start()
    zed[TOK:, :] = home(1, block_b(1, core, x), fin_b, 16).astype(BF16)
    copy(zed.at[TOK:], zin.at[TOK:], 18, 3, 3, at_z).start()
    keep[:TOK, :] = hid_ref[:, :HALF] + home(0, block_a(0, y), fin_a, 14)
    keep[TOK:, :] = hid_ref[:, HALF:] + home(0, block_b(0, core, x), fin_b, 16)
    same(zin.at[:TOK], 18, 2).wait_recv()
    out_ref[:, :HALF] = (keep[:TOK, :] + zin[:TOK, :].astype(F32)).astype(BF16)
    same(zin.at[TOK:], 18, 3).wait_recv()
    out_ref[:, HALF:] = (keep[TOK:, :] + zin[TOK:, :].astype(F32)).astype(BF16)

    same(zed.at[:TOK], 18, 2).wait_send()
    same(zed.at[TOK:], 18, 3).wait_send()
    for q in range(2):
        exchange_out(q, 10)
        for i in (1, 2, 3):
            same(block_a(q, row_y(i)), 14 + q, i).wait_send()
            same(block_b(q, core, chip_x(i)), 16 + q, i).wait_send()
        same(half_b(q, 1 - core), 16 + q, 0).wait_send()

    def routes_out(i, _):
        same(rows(rts_a, y, 16), 19, i).wait_send()
        same(rows(rts_b, place_b, 16), 20, i).wait_send()
        same(rows(rts_b, place_b, 16), 21, i).wait_send()
        return 0

    lax.fori_loop(1, PEERS, routes_out, 0)
    same(rows(rts_b, place_b, 16), 21, 0).wait_send()


def moe(hidden, normed, ids, probs, w_gate, w_up, w_down):
    vm = pl.BlockSpec(memory_space=pltpu.VMEM)
    hbm = pl.BlockSpec(memory_space=pl.ANY)
    half = [8 * TOK, 16 * TOK] + [SLOTS] * 6 + [6 * TOK, 6 * TOK, 8 * TOK, 2 * TOK, 2 * TOK, SPAN]
    return pl.pallas_call(
        moe_kernel,
        out_shape=jax.ShapeDtypeStruct((TOK, D), BF16),
        in_specs=[vm] * 4 + [hbm] * 3,
        out_specs=vm,
        scratch_shapes=[pltpu.VMEM((n, HALF), BF16) for n in half] + [
            pltpu.VMEM((SPAN, FF), BF16),
            pltpu.VMEM((SPAN, FF), BF16),
            pltpu.VMEM((4 * BLK, 4 * BLK), BF16),
            pltpu.VMEM((PEERS * TOK, 4 * TOK), BF16),
            pltpu.VMEM((4 * BLK, SPAN), BF16),
            pltpu.VMEM((D, FF), BF16),
            pltpu.VMEM((D, FF), BF16),
            pltpu.VMEM((FF, D), BF16),
            pltpu.VMEM((PEERS * 16, 4 * TOK), F32),
            pltpu.VMEM((2 * PEERS * 16, SPAN), F32),
            pltpu.VMEM((2, PEERS, 4 * TOK), jnp.int32),
            pltpu.VMEM((2, PEERS, SPAN), jnp.int32),
            pltpu.VMEM((2, PEERS, 4 * TOK), F32),
            pltpu.VMEM((2, PEERS, SPAN), F32),
            pltpu.VMEM((PEERS, 4 * TOK), F32),
            pltpu.VMEM((PEERS, SPAN), F32),
            pltpu.VMEM((2 * TOK, HALF), F32),
            pltpu.SemaphoreType.DMA((3,)),
            pltpu.SemaphoreType.DMA((22, PEERS)),
            pltpu.SemaphoreType.DMA((22, PEERS)),
        ],
        compiler_params=pltpu.CompilerParams(
            collective_id=1, has_side_effects=True, vmem_limit_bytes=62 * 1024 * 1024
        ),
        cost_estimate=pl.CostEstimate(flops=18_000_000_000, bytes_accessed=20_000_000, transcendentals=600_000),
        name="moe",
    )(hidden, normed, ids, probs, w_gate, w_up, w_down)


def attn_kernel(
    off_ref, q_hbm, k_hbm, v_hbm, w_hbm, res_hbm, gain_hbm,
    hid_ref, nrm_ref,
    q_ref, res_ref, gain_ref, kv, wbuf, mx, acc, att, pbuf, rbuf, tot, zsnd, zbuf,
    l_sem, kv_s, kv_r, w_s, w_r, y_s, y_r, z_s, z_r,
):
    dp, c, e = lax.axis_index("dp"), lax.axis_index("ctx"), lax.axis_index("exp")
    x, core, y, zh = c // 2, lax.rem(c, 2), e // 2, lax.rem(e, 2)
    sib = 2 * x + 1 - core

    def at_x(i):
        return (dp, 2 * lax.rem(x + i, 4) + core, e)

    def at_y(i):
        return (dp, c, 2 * lax.rem(y + i, 4) + zh)

    at_sib = (dp, sib, e)
    at_z = (dp, c, 2 * y + 1 - zh)
    at_twin = (1 - dp, c, e)

    def rows(ref, index, size):
        return ref.at[pl.ds(pl.multiple_of(index * size, 16), size)]

    def remote(src, dst, s, r, dev):
        return pltpu.make_async_remote_copy(
            src_ref=src, dst_ref=dst, send_sem=s, recv_sem=r, device_id=dev, device_id_type=MESH
        )

    kv_head = lax.rem(y, KVH)
    cols = pl.ds(pl.multiple_of(kv_head * HD, HD), HD)
    own = rows(kv, c, SPAN)
    loads = [
        pltpu.make_async_copy(k_hbm.at[:, cols], own.at[:, :HD], l_sem.at[0]),
        pltpu.make_async_copy(v_hbm.at[:, cols], own.at[:, HD:], l_sem.at[1]),
        pltpu.make_async_copy(w_hbm, rows(wbuf, c, HEADS), l_sem.at[2]),
        pltpu.make_async_copy(q_hbm, q_ref, l_sem.at[3]),
        pltpu.make_async_copy(res_hbm, res_ref, l_sem.at[4]),
        pltpu.make_async_copy(gain_hbm, gain_ref, l_sem.at[5]),
    ]
    for load in loads:
        load.start()
    barrier = pltpu.get_barrier_semaphore()
    peers = [at_x(i) for i in (1, 2, 3)] + [at_y(i) for i in (1, 2, 3)] + [at_sib, at_z, at_twin]
    for dev in peers:
        pl.semaphore_signal(barrier, 1, device_id=dev, device_id_type=MESH)
    loads[0].wait()
    loads[1].wait()
    pl.semaphore_wait(barrier, len(peers))

    def from_chip(buf, size, i, who):
        return rows(buf, 2 * lax.rem(x + 4 - i, 4) + who, size)

    def exchange(buf, size, s, r):
        def handed(i, who):
            block = from_chip(buf, size, i, who)
            return remote(block, block, s.at[3 + i], r.at[3 + i], at_sib)

        mine, theirs = rows(buf, c, size), rows(buf, sib, size)
        to_sib = remote(mine, mine, s.at[0], r.at[0], at_sib)
        from_sib = remote(theirs, theirs, s.at[0], r.at[0], at_sib)
        return handed, to_sib, from_sib

    k_handed, k_to_sib, k_from_sib = exchange(kv, SPAN, kv_s, kv_r)
    w_handed, w_to_sib, w_from_sib = exchange(wbuf, HEADS, w_s, w_r)

    def k_direct(i):
        return remote(own, own, kv_s.at[i], kv_r.at[i], at_x(i))

    def k_arrival(i):
        block = from_chip(kv, SPAN, i, core)
        return remote(block, block, kv_s.at[i], kv_r.at[i], at_sib)

    def w_direct(i, coming):
        block = from_chip(wbuf, HEADS, i, core) if coming else rows(wbuf, c, HEADS)
        part = rows(block, dp, 512) if i == 2 else block
        return remote(part, part, w_s.at[i], w_r.at[i], at_x(i))

    def w_twin(coming):
        part = rows(from_chip(wbuf, HEADS, 2, core), 1 - dp if coming else dp, 512)
        return remote(part, part, w_s.at[7], w_r.at[7], at_twin)

    k_to_sib.start()
    for i in (1, 3, 2):
        k_direct(i).start()

    scale = HD ** (-0.5) * math.log2(math.e)
    lane = lax.broadcasted_iota(jnp.int32, (1, 2 * SPAN), 1)
    ones = jnp.ones((2 * SPAN, HD), BF16)

    def group(i):
        chip = lax.rem(x + 4 - i, 4)
        at = pl.ds(pl.multiple_of(chip * 2 * SPAN, 2 * SPAN), 2 * SPAN)
        first, second = off_ref[2 * chip], off_ref[2 * chip + 1]
        key_pos = jnp.where(lane < SPAN, first + lane, second + lane - SPAN)
        if i:
            bias = jnp.where(key_pos <= off_ref[c] + SPAN - 1, 0.0, NEG_FILL)

        def head(h, _):
            hcols = pl.ds(pl.multiple_of(h * HD, HD), HD)
            mine = pl.ds(pl.multiple_of(h * SPAN, SPAN), SPAN)
            s = lax.dot_general(
                q_ref[:, hcols], kv[at, :HD], (((1,), (1,)), ((), ())), preferred_element_type=F32
            ) * scale
            if i:
                s = s + bias
            else:
                query_pos = off_ref[c] + lax.broadcasted_iota(jnp.int32, (SPAN, 1), 0)
                s = jnp.where(key_pos <= query_pos, s, NEG_FILL)
            top = jnp.max(s, axis=1, keepdims=True)
            if i:
                old = mx[mine, :]
                new = jnp.maximum(old, top)
                p = jnp.exp2(s - jnp.concatenate([new] * 6, axis=1)).astype(BF16)
            else:
                new = jnp.broadcast_to(top, (SPAN, HD))
                p = jnp.exp2(s - top).astype(BF16)
            mixed = jnp.dot(
                p, jnp.concatenate([kv[at, HD:], ones], axis=1), preferred_element_type=F32
            )
            if i:
                keep = jnp.exp2(old - new)
                mixed = acc[mine, :] * jnp.concatenate([keep, keep], axis=1) + mixed
            mx[mine, :] = new
            acc[mine, :] = mixed
            return 0

        lax.fori_loop(0, 8, head, 0, unroll=8)

    loads[2].wait()
    w_to_sib.start()
    w_direct(2, False).start()
    for load in loads[3:]:
        load.wait()
    k_from_sib.wait_recv()
    group(0)
    w_direct(1, False).start()
    w_direct(3, False).start()
    for i in (1, 3):
        k_arrival(i).wait_recv()
        k_handed(i, core).start()
    k_handed(1, 1 - core).wait_recv()
    group(1)
    k_arrival(2).wait_recv()
    k_handed(2, core).start()
    k_handed(3, 1 - core).wait_recv()
    group(3)
    k_handed(2, 1 - core).wait_recv()
    w_direct(2, True).wait_recv()
    w_twin(False).start()
    group(2)

    def divide(h, _):
        hcols = pl.ds(pl.multiple_of(h * HD, HD), HD)
        mine = pl.ds(pl.multiple_of(h * SPAN, SPAN), SPAN)
        att[:, hcols] = (acc[mine, :HD] / acc[mine, HD:]).astype(BF16)
        return 0

    lax.fori_loop(0, 8, divide, 0)

    def piece(k):
        k2 = k // 2
        chip = lax.rem(x + 4 - lax.rem(2 * k2, 4) - k2 // 2, 4)
        return 2 * chip + lax.rem(core + k, 2)

    def to_y(w, i):
        return remote(
            rows(pbuf, w * 4 + lax.rem(y + i, 4), 2 * TOK), rows(rbuf, w * 3 + i - 1, 2 * TOK),
            y_s.at[w, i - 1], y_r.at[w, i - 1], at_y(i),
        )

    def to_z(w):
        return remote(rows(zsnd, w, TOK), rows(zbuf, w, TOK), z_s.at[w], z_r.at[w], at_z)

    def project(k, _):
        w = piece(k)
        rows(pbuf, w, SPAN)[...] = jnp.dot(
            att[...], rows(wbuf, w, HEADS)[...], preferred_element_type=F32
        ).astype(BF16)
        for i in (1, 3, 2):
            to_y(w, i).start()
        return 0

    def reduce(k, _):
        w = piece(k)
        total = rows(pbuf, w * 4 + y, 2 * TOK)[...].astype(F32)
        for i in (1, 3, 2):
            to_y(w, i).wait_recv()
            total += rows(rbuf, w * 3 + i - 1, 2 * TOK)[...].astype(F32)
        tot[...] = total
        rows(zsnd, w, TOK)[...] = rows(tot, 1 - zh, TOK)[...].astype(BF16)
        to_z(w).start()
        wcols = pl.ds(pl.multiple_of(w * 512, 512), 512)
        hid_ref[:, wcols] = rows(tot, zh, TOK)[...] + res_ref[:, wcols].astype(F32)
        return 0

    w_from_sib.wait_recv()
    lax.fori_loop(0, 2, project, 0)
    w_twin(True).wait_recv()
    w_handed(2, core).start()
    project(2, 0)
    lax.fori_loop(0, 2, reduce, 0)
    w_handed(2, 1 - core).wait_recv()
    project(3, 0)
    for i in (1, 3):
        w_direct(i, True).wait_recv()
        w_handed(i, core).start()
    lax.fori_loop(0, 2, lambda j, _: project(4 + 2 * j, 0), 0)
    for i in (1, 3):
        w_handed(i, 1 - core).wait_recv()
    lax.fori_loop(0, 2, lambda j, _: project(5 + 2 * j, 0), 0)
    lax.fori_loop(2, 5, reduce, 0)
    reduce(6, 0)
    reduce(5, 0)
    reduce(7, 0)

    square = jnp.zeros((TOK, 1), F32)

    def finish(k, square):
        w = piece(k)
        to_z(w).wait_recv()
        wcols = pl.ds(pl.multiple_of(w * 512, 512), 512)
        h = hid_ref[:, wcols] + rows(zbuf, w, TOK)[...].astype(F32)
        hid_ref[:, wcols] = h
        return square + jnp.sum(h * h, axis=1, keepdims=True)

    square = lax.fori_loop(0, 8, finish, square)
    inverse = lax.rsqrt(square * (1.0 / D) + 1e-06)
    nrm_ref[...] = (hid_ref[...] * inverse * gain_ref[...]).astype(BF16)

    k_to_sib.wait_send()
    w_to_sib.wait_send()
    for i in (1, 2, 3):
        k_direct(i).wait_send()
        k_handed(i, core).wait_send()
        w_direct(i, False).wait_send()
        w_handed(i, core).wait_send()
    w_twin(False).wait_send()

    def sent(k, _):
        w = piece(k)
        for i in (1, 2, 3):
            to_y(w, i).wait_send()
        to_z(w).wait_send()
        return 0

    lax.fori_loop(0, 8, sent, 0)


def attend(offsets, queries, keys, values, out_proj, residual, gain):
    vm = pl.BlockSpec(memory_space=pltpu.VMEM)
    hbm = pl.BlockSpec(memory_space=pl.ANY)
    dma = pltpu.SemaphoreType.DMA
    return pl.pallas_call(
        attn_kernel,
        out_shape=(jax.ShapeDtypeStruct((TOK, D), F32), jax.ShapeDtypeStruct((TOK, D), BF16)),
        in_specs=[pl.BlockSpec(memory_space=pltpu.SMEM)] + [hbm] * 6,
        out_specs=(vm, vm),
        scratch_shapes=[
            pltpu.VMEM((SPAN, HEADS), BF16),
            pltpu.VMEM((TOK, D), BF16),
            pltpu.VMEM((1, D), F32),
            pltpu.VMEM((PEERS * SPAN, 2 * HD), BF16),
            pltpu.VMEM((PEERS * HEADS, 512), BF16),
            pltpu.VMEM((8 * SPAN, HD), F32),
            pltpu.VMEM((8 * SPAN, 2 * HD), F32),
            pltpu.VMEM((SPAN, HEADS), BF16),
            pltpu.VMEM((PEERS * SPAN, 512), BF16),
            pltpu.VMEM((PEERS * 3 * 2 * TOK, 512), BF16),
            pltpu.VMEM((2 * TOK, 512), F32),
            pltpu.VMEM((PEERS * TOK, 512), BF16),
            pltpu.VMEM((PEERS * TOK, 512), BF16),
            dma((6,)), dma((7,)), dma((7,)), dma((8,)), dma((8,)),
            dma((PEERS, 3)), dma((PEERS, 3)), dma((PEERS,)), dma((PEERS,)),
        ],
        compiler_params=pltpu.CompilerParams(
            collective_id=2, has_side_effects=True, vmem_limit_bytes=62 * 1024 * 1024
        ),
        cost_estimate=pl.CostEstimate(flops=9_000_000_000, bytes_accessed=4_000_000, transcendentals=10_000_000),
        name="attend",
    )(offsets, queries, keys, values, out_proj, residual, gain)


def shards(
    queries, keys, values, offsets, out_proj, residual, norm_gain, expert_ids, gate_probs, w_gate, w_up, w_down,
):
    hidden, normed = attend(offsets, queries, keys, values, out_proj, residual, norm_gain[None, :])
    return moe(hidden, normed, expert_ids.T, gate_probs.T, w_gate, w_up, w_down)


def solution(mesh):
    return jax.shard_map(
        shards,
        mesh=mesh,
        in_specs=(
            P(("dp", "ctx"), "exp"),
            P(("dp", "ctx"), None),
            P(("dp", "ctx"), None),
            P("dp"),
            P("exp", "ctx"),
            P(("dp", "ctx", "exp"), None),
            P(),
            P(("dp", "ctx", "exp"), None),
            P(("dp", "ctx", "exp"), None),
            P(("ctx", "exp"), None, None),
            P(("ctx", "exp"), None, None),
            P(("ctx", "exp"), None, None),
        ),
        out_specs=P(("dp", "ctx", "exp"), None),
        check_vma=False,
    )
```

```python
import math

import jax
import jax.numpy as jnp
from jax import lax
from jax.experimental import pallas as pl
from jax.experimental.pallas import tpu as pltpu
from jax.sharding import PartitionSpec as P

KVH = 4
HD = 128
D = 4096
HALF = D // 2
FF = 768
TOK = 48
CAP = 12
PEERS = 8
BLK = PEERS * CAP
SLOTS = PEERS * BLK
SPAN = PEERS * TOK
HEADS = 8 * HD

NEG_FILL = -1e30
MESH = pl.DeviceIdType.MESH
F32 = jnp.float32
BF16 = jnp.bfloat16


def over(a, n):
    return ((a.astype(F32) + 0.5) * (1.0 / n)).astype(jnp.int32)


def route_table(packed, expert_of, count, code, prob, member):
    ids, probs = packed[:8], packed[8:]
    width = packed.shape[1]
    for j in range(count):
        named = ids == expert_of(j).astype(F32)
        member[j:j + 1, :] = jnp.sum(jnp.where(named, 1.0, 0.0), axis=0, keepdims=True)
        prob[j:j + 1, :] = jnp.sum(jnp.where(named, probs, 0.0), axis=0, keepdims=True)
    before = lax.broadcasted_iota(jnp.int32, (width, width), 0)
    t = lax.broadcasted_iota(jnp.int32, (width, width), 1)
    block = over(t, TOK)
    earlier = jnp.where((before < t) & (before >= block * TOK), 1.0, 0.0).astype(BF16)
    inside = member[...]
    rank = jnp.dot(inside.astype(BF16), earlier, preferred_element_type=F32)
    code[...] = jnp.where(inside > 0.5, block[:8] * CAP + rank.astype(jnp.int32), -1)


def moe_kernel(
    hid_ref, nrm_ref, ids_ref, probs_ref, wg_hbm, wu_hbm, wd_hbm,
    out_ref,
    gat_a, gat_b, snd_a, snd_b, arr_a, arr_b, ret_a, ret_b, fin_a, fin_b, sib_b, zed, zin,
    xb, act, act_b, pm, wt_a, wt_b, wg, wu, wd,
    rts_a, rts_b, code_a, code_b, prob_a, prob_b, member_a, member_b, keep,
    w_sem, s_sem, r_sem,
):
    dp, c, e = lax.axis_index("dp"), lax.axis_index("ctx"), lax.axis_index("exp")
    x, core, y, zh = c // 2, lax.rem(c, 2), e // 2, lax.rem(e, 2)
    v = lax.rem(dp + e, 2)
    sib = 2 * x + 1 - core
    place_b = core * 4 + x

    def at_exp(other):
        return (lax.rem(v + other, 2), c, other)

    def at_ctx(other):
        return (dp, other, e)

    def at_far(other):
        return (1 - dp, other, 2 * y + 1 - zh)

    def chip_x(i):
        return lax.rem(x + i, 4)

    def at_x(i):
        return (dp, 2 * chip_x(i) + core, e)

    def row_y(i):
        return lax.rem(y + i, 4)

    def at_y(i):
        return (dp, c, 2 * row_y(i) + zh)

    at_sib = (dp, sib, e)
    at_z = at_far(c)

    weights = [
        pltpu.make_async_copy(src.at[0], dst, w_sem.at[i])
        for i, (src, dst) in enumerate(((wg_hbm, wg), (wu_hbm, wu), (wd_hbm, wd)))
    ]
    for w in weights:
        w.start()

    def rows(ref, index, size):
        return ref.at[pl.ds(pl.multiple_of(index * size, 16), size)]

    def copy(src, dst, stage, sent, got, dev):
        return pltpu.make_async_remote_copy(
            src_ref=src, dst_ref=dst, send_sem=s_sem.at[stage, sent], recv_sem=r_sem.at[stage, got],
            device_id=dev, device_id_type=MESH,
        )

    def same(ref, stage, index):
        return copy(ref, ref, stage, index, index, at_sib)

    def block_a(q, oy):
        return rows(gat_a, 4 * q + oy, TOK)

    def block_b(q, who, ox):
        return rows(gat_b, 8 * q + 4 * who + ox, TOK)

    barrier = pltpu.get_barrier_semaphore()

    def greet(i, _):
        oe, oc = lax.rem(e + i, PEERS), lax.rem(c + i, PEERS)
        for dev in (at_exp(oe), at_ctx(oc), at_far(oc)):
            pl.semaphore_signal(barrier, 1, device_id=dev, device_id_type=MESH)
        return 0

    lax.fori_loop(1, PEERS, greet, 0)
    block_a(0, y)[...] = nrm_ref[:, :HALF]
    block_b(0, core, x)[...] = nrm_ref[:, HALF:]
    pl.semaphore_wait(barrier, 3 * (PEERS - 1))

    def along(q):
        a, b = block_a(q, y), block_b(q, core, x)
        for i in (1, 3, 2):
            copy(a, a, q, i, i, at_y(i)).start()
            copy(b, b, 2 + q, i, i, at_x(i)).start()
        copy(b, b, 2 + q, 4, 4, at_sib).start()

    copy(block_a(0, y), block_a(1, y), 18, 0, 0, at_z).start()
    copy(block_b(0, core, x), block_b(1, core, x), 18, 1, 1, at_z).start()
    along(0)
    for rts, index, place, width in ((rts_a, y, y, 4 * TOK), (rts_b, place_b, place_b, SPAN)):
        token = lax.broadcasted_iota(jnp.int32, (TOK, width), 0)
        lane = lax.broadcasted_iota(jnp.int32, (TOK, width), 1)
        put = jnp.where(lane == token + place * TOK, 1.0, 0.0)
        spread = [
            jnp.dot(a, put, preferred_element_type=F32, precision=lax.Precision.HIGHEST)
            for a in (ids_ref[...].astype(F32), probs_ref[...])
        ]
        rows(rts, index, 16)[...] = jnp.concatenate(spread, axis=0)

    def slot_e(oe):
        far = lax.rem(oe + e, 2)
        return 4 * far + oe // 2, 4 * far + y

    def routes(i, _):
        oe, oc = lax.rem(e + i, PEERS), lax.rem(c + i, PEERS)
        _, mine = slot_e(oe)
        copy(rows(rts_a, y, 16), rows(rts_a, mine, 16), 19, i, mine, at_exp(oe)).start()
        own = rows(rts_b, place_b, 16)
        copy(own, own, 20, i, place_b, at_ctx(oc)).start()
        copy(own, rows(rts_b, 8 + place_b, 16), 21, i, place_b, at_far(oc)).start()
        return 0

    lax.fori_loop(1, PEERS, routes, 0)
    copy(rows(rts_b, place_b, 16), rows(rts_b, 8 + place_b, 16), 21, 0, place_b, at_z).start()
    same(block_a(1, y), 18, 0).wait_recv()
    same(block_b(1, core, x), 18, 1).wait_recv()
    along(1)

    i = lax.broadcasted_iota(jnp.int32, (4 * BLK, 4 * BLK), 0)
    at = lax.broadcasted_iota(jnp.int32, (4 * BLK, 4 * BLK), 1)
    from_c = over(i, TOK)
    rest = i - from_c * TOK
    from_y = over(rest, CAP)
    from_x = over(from_c, 2)
    want = from_y * BLK + ((from_c - 2 * from_x) * 4 + from_x) * CAP + rest - from_y * CAP
    pm[...] = jnp.where(at == want, 1.0, 0.0).astype(BF16)

    def hand_on(q, i):
        block = block_b(q, core, chip_x(4 - i))
        same(block, 2 + q, i).wait_recv()
        copy(block, block, 4 + q, i, i, at_sib).start()

    hand_on(0, 1)
    hand_on(0, 3)

    def routes_in(i, _):
        oe, oc = lax.rem(e + i, PEERS), lax.rem(c + i, PEERS)
        theirs, _ = slot_e(oe)
        same(rows(rts_a, theirs, 16), 19, theirs).wait_recv()
        other = lax.rem(oc, 2) * 4 + oc // 2
        same(rows(rts_b, other, 16), 20, other).wait_recv()
        same(rows(rts_b, 8 + other, 16), 21, other).wait_recv()
        return 0

    lax.fori_loop(1, PEERS, routes_in, 0)
    same(rows(rts_b, 8 + place_b, 16), 21, place_b).wait_recv()
    hand_on(0, 2)

    def gathered(rts, first, count):
        packed = rts[first * 16:first * 16 + 16, :]
        for k in range(first + 1, first + count):
            packed += rts[k * 16:k * 16 + 16, :]
        return packed

    member_b[...] = jnp.zeros_like(member_b)
    for q in range(2):
        route_table(
            gathered(rts_a, 4 * q, 4), lambda j: j * PEERS + e, PEERS, code_a.at[q], prob_a.at[q], member_a
        )
        route_table(
            gathered(rts_b, 8 * q, 8), lambda j: c * PEERS + 2 * j + zh, 4, code_b.at[q], prob_b.at[q], member_b
        )
    for i in (1, 3, 2):
        hand_on(1, i)

    slot_a = lax.broadcasted_iota(jnp.int32, (TOK, 4 * TOK), 0)
    slot_b = lax.broadcasted_iota(jnp.int32, (BLK, SPAN), 0)

    def select(q):
        for k in range(PEERS):
            wt_a[k * TOK:(k + 1) * TOK, :] = jnp.where(
                code_a[q, k:k + 1, :] == slot_a, 1.0, 0.0
            ).astype(BF16)
        for k in range(4):
            wt_b[k * BLK:(k + 1) * BLK, :] = jnp.where(
                code_b[q, k:k + 1, :] == slot_b, 1.0, 0.0
            ).astype(BF16)
        part = slice(q * SPAN, q * SPAN + SPAN)

        def tile(n, _):
            cols = pl.ds(pl.multiple_of(n * 512, 512), 512)
            snd_a[part, cols] = jnp.dot(
                wt_a[...], gat_a[q * 4 * TOK:(q + 1) * 4 * TOK, cols], preferred_element_type=F32
            ).astype(BF16)
            snd_b[part, cols] = jnp.dot(
                wt_b[...], gat_b[part, cols], preferred_element_type=F32
            ).astype(BF16)
            return 0

        lax.fori_loop(0, HALF // 512, tile, 0)

    def exchange(q, dst_a, dst_b, stage):
        for i in (1, 3, 2):
            for k in range(2):
                oc = 2 * chip_x(i) + k
                copy(
                    rows(snd_a, 8 * q + oc, TOK), rows(dst_a, 8 * q + c, TOK), stage + q, oc, c, at_ctx(oc)
                ).start()
            copy(
                rows(snd_b, 4 * q + row_y(i), BLK), rows(dst_b, 4 * q + y, BLK), stage + 2 + q, i, i, at_y(i)
            ).start()
        copy(rows(snd_a, 8 * q + sib, TOK), rows(dst_a, 8 * q + c, TOK), stage + q, sib, c, at_sib).start()
        rows(dst_a, 8 * q + c, TOK)[...] = rows(snd_a, 8 * q + c, TOK)[...]
        rows(dst_b, 4 * q + y, BLK)[...] = rows(snd_b, 4 * q + y, BLK)[...]

    def exchange_in(q, dst_a, dst_b, stage):
        for i in (1, 3, 2):
            same(rows(dst_b, 4 * q + row_y(4 - i), BLK), stage + 2 + q, i).wait_recv()

        def body(i, _):
            oc = lax.rem(c + i, PEERS)
            same(rows(dst_a, 8 * q + oc, TOK), stage + q, oc).wait_recv()
            return 0

        lax.fori_loop(1, PEERS, body, 0)

    def exchange_out(q, stage):
        for i in (1, 3, 2):
            same(rows(snd_b, 4 * q + row_y(i), BLK), stage + 2 + q, i).wait_send()

        def body(i, _):
            oc = lax.rem(c + i, PEERS)
            same(rows(snd_a, 8 * q + oc, TOK), stage + q, oc).wait_send()
            return 0

        lax.fori_loop(1, PEERS, body, 0)

    for q in (1, 0):
        for i in (1, 3, 2):
            same(block_a(q, row_y(4 - i)), q, i).wait_recv()
            same(block_b(q, 1 - core, chip_x(4 - i)), 4 + q, i).wait_recv()
        same(block_b(q, 1 - core, x), 2 + q, 4).wait_recv()
        select(q)
        if q == 0:
            exchange_out(1, 6)
        exchange(q, arr_a, arr_b, 6)

    for w in weights:
        w.wait()

    def experts(q):
        part = slice(q * SPAN, q * SPAN + SPAN)

        def reorder(n, _):
            cols = pl.ds(pl.multiple_of(n * 512, 512), 512)
            xb[:, cols] = jnp.dot(pm[...], arr_b[part, cols], preferred_element_type=F32).astype(BF16)
            return 0

        lax.fori_loop(0, HALF // 512, reorder, 0)

        def hidden_tile(n, _):
            cols = pl.ds(pl.multiple_of(n * 256, 256), 256)
            a, b = arr_a[part, :], xb[...]
            gate = jnp.dot(a, wg[:HALF, cols], preferred_element_type=F32)
            gate += jnp.dot(b, wg[HALF:, cols], preferred_element_type=F32)
            up = jnp.dot(a, wu[:HALF, cols], preferred_element_type=F32)
            up += jnp.dot(b, wu[HALF:, cols], preferred_element_type=F32)
            act[:, cols] = (gate / (1.0 + jnp.exp(-gate)) * up).astype(BF16)
            return 0

        lax.fori_loop(0, FF // 256, hidden_tile, 0)
        act_b[...] = lax.dot_general(
            pm[...], act[...], (((0,), (0,)), ((), ())), preferred_element_type=F32
        ).astype(BF16)

        def down(n, _):
            cols = pl.ds(pl.multiple_of(n * 512, 512), 512)
            late = pl.ds(pl.multiple_of(n * 512 + HALF, 512), 512)
            snd_a[part, cols] = jnp.dot(act[...], wd[:, cols], preferred_element_type=F32).astype(BF16)
            snd_b[part, cols] = jnp.dot(act_b[...], wd[:, late], preferred_element_type=F32).astype(BF16)
            return 0

        lax.fori_loop(0, HALF // 512, down, 0)

    for q in (1, 0):
        exchange_in(q, arr_a, arr_b, 6)
        if q == 0:
            exchange_out(0, 6)
        experts(q)
        exchange(q, ret_a, ret_b, 10)

    for q in range(2):
        for i in (1, 2, 3):
            same(block_a(q, y), q, i).wait_send()
            same(block_b(q, core, x), 2 + q, i).wait_send()
            same(block_b(q, core, x), 4 + q, i).wait_send()
        same(block_b(q, core, x), 2 + q, 4).wait_send()
    same(block_a(0, y), 18, 0).wait_send()
    same(block_b(0, core, x), 18, 1).wait_send()

    def half_b(q, who):
        return rows(gat_b, 2 * q + who, 4 * TOK)

    def mix(q):
        for k in range(PEERS):
            wt_a[k * TOK:(k + 1) * TOK, :] = jnp.where(
                code_a[q, k:k + 1, :] == slot_a, prob_a[q, k:k + 1, :], 0.0
            ).astype(BF16)
        for k in range(4):
            wt_b[k * BLK:(k + 1) * BLK, :] = jnp.where(
                code_b[q, k:k + 1, :] == slot_b, prob_b[q, k:k + 1, :], 0.0
            ).astype(BF16)
        part = slice(q * SPAN, q * SPAN + SPAN)

        def tile_b(n, _):
            cols = pl.ds(pl.multiple_of(n * 512, 512), 512)
            gat_b[part, cols] = lax.dot_general(
                wt_b[...], ret_b[part, cols], (((0,), (0,)), ((), ())), preferred_element_type=F32
            ).astype(BF16)
            return 0

        def tile_a(n, _):
            cols = pl.ds(pl.multiple_of(n * 512, 512), 512)
            gat_a[q * 4 * TOK:(q + 1) * 4 * TOK, cols] = lax.dot_general(
                wt_a[...], ret_a[part, cols], (((0,), (0,)), ((), ())), preferred_element_type=F32
            ).astype(BF16)
            return 0

        lax.fori_loop(0, HALF // 512, tile_b, 0)
        copy(half_b(q, 1 - core), rows(sib_b, q, 4 * TOK), 16 + q, 0, 0, at_sib).start()
        lax.fori_loop(0, HALF // 512, tile_a, 0)
        for i in (1, 3, 2):
            copy(block_a(q, row_y(i)), rows(fin_a, 3 * q + i - 1, TOK), 14 + q, i, i, at_y(i)).start()
        same(rows(sib_b, q, 4 * TOK), 16 + q, 0).wait_recv()
        for i in (1, 3, 2, 0):
            own = block_b(q, core, chip_x(i))
            own[...] = (
                own[...].astype(F32) + rows(sib_b, 4 * q + chip_x(i), TOK)[...].astype(F32)
            ).astype(BF16)
            if i:
                copy(own, rows(fin_b, 3 * q + i - 1, TOK), 16 + q, i, i, at_x(i)).start()

    for q in (1, 0):
        exchange_in(q, ret_a, ret_b, 10)
        mix(q)

    def home(q, own, fin, stage):
        total = own[...].astype(F32)
        for i in (1, 3, 2):
            same(rows(fin, 3 * q + i - 1, TOK), stage + q, i).wait_recv()
        for i in range(3):
            total += rows(fin, 3 * q + i, TOK)[...].astype(F32)
        return total

    zed[:TOK, :] = home(1, block_a(1, y), fin_a, 14).astype(BF16)
    copy(zed.at[:TOK], zin.at[:TOK], 18, 2, 2, at_z).start()
    zed[TOK:, :] = home(1, block_b(1, core, x), fin_b, 16).astype(BF16)
    copy(zed.at[TOK:], zin.at[TOK:], 18, 3, 3, at_z).start()
    keep[:TOK, :] = hid_ref[:, :HALF] + home(0, block_a(0, y), fin_a, 14)
    keep[TOK:, :] = hid_ref[:, HALF:] + home(0, block_b(0, core, x), fin_b, 16)
    same(zin.at[:TOK], 18, 2).wait_recv()
    out_ref[:, :HALF] = (keep[:TOK, :] + zin[:TOK, :].astype(F32)).astype(BF16)
    same(zin.at[TOK:], 18, 3).wait_recv()
    out_ref[:, HALF:] = (keep[TOK:, :] + zin[TOK:, :].astype(F32)).astype(BF16)

    same(zed.at[:TOK], 18, 2).wait_send()
    same(zed.at[TOK:], 18, 3).wait_send()
    for q in range(2):
        exchange_out(q, 10)
        for i in (1, 2, 3):
            same(block_a(q, row_y(i)), 14 + q, i).wait_send()
            same(block_b(q, core, chip_x(i)), 16 + q, i).wait_send()
        same(half_b(q, 1 - core), 16 + q, 0).wait_send()

    def routes_out(i, _):
        same(rows(rts_a, y, 16), 19, i).wait_send()
        same(rows(rts_b, place_b, 16), 20, i).wait_send()
        same(rows(rts_b, place_b, 16), 21, i).wait_send()
        return 0

    lax.fori_loop(1, PEERS, routes_out, 0)
    same(rows(rts_b, place_b, 16), 21, 0).wait_send()


def moe(hidden, normed, ids, probs, w_gate, w_up, w_down):
    vm = pl.BlockSpec(memory_space=pltpu.VMEM)
    hbm = pl.BlockSpec(memory_space=pl.ANY)
    half = [8 * TOK, 16 * TOK] + [SLOTS] * 6 + [6 * TOK, 6 * TOK, 8 * TOK, 2 * TOK, 2 * TOK, SPAN]
    return pl.pallas_call(
        moe_kernel,
        out_shape=jax.ShapeDtypeStruct((TOK, D), BF16),
        in_specs=[vm] * 4 + [hbm] * 3,
        out_specs=vm,
        scratch_shapes=[pltpu.VMEM((n, HALF), BF16) for n in half] + [
            pltpu.VMEM((SPAN, FF), BF16),
            pltpu.VMEM((SPAN, FF), BF16),
            pltpu.VMEM((4 * BLK, 4 * BLK), BF16),
            pltpu.VMEM((PEERS * TOK, 4 * TOK), BF16),
            pltpu.VMEM((4 * BLK, SPAN), BF16),
            pltpu.VMEM((D, FF), BF16),
            pltpu.VMEM((D, FF), BF16),
            pltpu.VMEM((FF, D), BF16),
            pltpu.VMEM((PEERS * 16, 4 * TOK), F32),
            pltpu.VMEM((2 * PEERS * 16, SPAN), F32),
            pltpu.VMEM((2, PEERS, 4 * TOK), jnp.int32),
            pltpu.VMEM((2, PEERS, SPAN), jnp.int32),
            pltpu.VMEM((2, PEERS, 4 * TOK), F32),
            pltpu.VMEM((2, PEERS, SPAN), F32),
            pltpu.VMEM((PEERS, 4 * TOK), F32),
            pltpu.VMEM((PEERS, SPAN), F32),
            pltpu.VMEM((2 * TOK, HALF), F32),
            pltpu.SemaphoreType.DMA((3,)),
            pltpu.SemaphoreType.DMA((22, PEERS)),
            pltpu.SemaphoreType.DMA((22, PEERS)),
        ],
        compiler_params=pltpu.CompilerParams(
            collective_id=1, has_side_effects=True, vmem_limit_bytes=62 * 1024 * 1024
        ),
        cost_estimate=pl.CostEstimate(flops=18_000_000_000, bytes_accessed=20_000_000, transcendentals=600_000),
        name="moe",
    )(hidden, normed, ids, probs, w_gate, w_up, w_down)


def attn_kernel(
    off_ref, q_hbm, k_hbm, v_hbm, w_hbm, res_hbm, gain_hbm,
    hid_ref, nrm_ref,
    q_ref, res_ref, gain_ref, kv, wbuf, mx, acc, att, pbuf, rbuf, tot, zsnd, zbuf,
    l_sem, kv_s, kv_r, w_s, w_r, y_s, y_r, z_s, z_r,
):
    dp, c, e = lax.axis_index("dp"), lax.axis_index("ctx"), lax.axis_index("exp")
    x, core, y, zh = c // 2, lax.rem(c, 2), e // 2, lax.rem(e, 2)
    sib = 2 * x + 1 - core

    def at_x(i):
        return (dp, 2 * lax.rem(x + i, 4) + core, e)

    def at_y(i):
        return (dp, c, 2 * lax.rem(y + i, 4) + zh)

    at_sib = (dp, sib, e)
    at_z = (dp, c, 2 * y + 1 - zh)
    at_twin = (1 - dp, c, e)

    def rows(ref, index, size):
        return ref.at[pl.ds(pl.multiple_of(index * size, 16), size)]

    def remote(src, dst, s, r, dev):
        return pltpu.make_async_remote_copy(
            src_ref=src, dst_ref=dst, send_sem=s, recv_sem=r, device_id=dev, device_id_type=MESH
        )

    kv_head = lax.rem(y, KVH)
    cols = pl.ds(pl.multiple_of(kv_head * HD, HD), HD)
    own = rows(kv, c, SPAN)
    loads = [
        pltpu.make_async_copy(k_hbm.at[:, cols], own.at[:, :HD], l_sem.at[0]),
        pltpu.make_async_copy(v_hbm.at[:, cols], own.at[:, HD:], l_sem.at[1]),
        pltpu.make_async_copy(w_hbm, rows(wbuf, c, HEADS), l_sem.at[2]),
        pltpu.make_async_copy(q_hbm, q_ref, l_sem.at[3]),
        pltpu.make_async_copy(res_hbm, res_ref, l_sem.at[4]),
        pltpu.make_async_copy(gain_hbm, gain_ref, l_sem.at[5]),
    ]
    for load in loads:
        load.start()
    barrier = pltpu.get_barrier_semaphore()
    peers = [at_x(i) for i in (1, 2, 3)] + [at_y(i) for i in (1, 2, 3)] + [at_sib, at_z, at_twin]
    for dev in peers:
        pl.semaphore_signal(barrier, 1, device_id=dev, device_id_type=MESH)
    loads[0].wait()
    loads[1].wait()
    pl.semaphore_wait(barrier, len(peers))

    def from_chip(buf, size, i, who):
        return rows(buf, 2 * lax.rem(x + 4 - i, 4) + who, size)

    def exchange(buf, size, s, r):
        def handed(i, who):
            block = from_chip(buf, size, i, who)
            return remote(block, block, s.at[3 + i], r.at[3 + i], at_sib)

        mine, theirs = rows(buf, c, size), rows(buf, sib, size)
        to_sib = remote(mine, mine, s.at[0], r.at[0], at_sib)
        from_sib = remote(theirs, theirs, s.at[0], r.at[0], at_sib)
        return handed, to_sib, from_sib

    k_handed, k_to_sib, k_from_sib = exchange(kv, SPAN, kv_s, kv_r)
    w_handed, w_to_sib, w_from_sib = exchange(wbuf, HEADS, w_s, w_r)

    def k_direct(i):
        return remote(own, own, kv_s.at[i], kv_r.at[i], at_x(i))

    def k_arrival(i):
        block = from_chip(kv, SPAN, i, core)
        return remote(block, block, kv_s.at[i], kv_r.at[i], at_sib)

    def w_direct(i, coming):
        block = from_chip(wbuf, HEADS, i, core) if coming else rows(wbuf, c, HEADS)
        part = rows(block, dp, 512) if i == 2 else block
        return remote(part, part, w_s.at[i], w_r.at[i], at_x(i))

    def w_twin(coming):
        part = rows(from_chip(wbuf, HEADS, 2, core), 1 - dp if coming else dp, 512)
        return remote(part, part, w_s.at[7], w_r.at[7], at_twin)

    k_to_sib.start()
    for i in (1, 3, 2):
        k_direct(i).start()

    scale = HD ** (-0.5) * math.log2(math.e)
    lane = lax.broadcasted_iota(jnp.int32, (1, 2 * SPAN), 1)
    ones = jnp.ones((2 * SPAN, HD), BF16)

    def group(i):
        chip = lax.rem(x + 4 - i, 4)
        at = pl.ds(pl.multiple_of(chip * 2 * SPAN, 2 * SPAN), 2 * SPAN)
        first, second = off_ref[2 * chip], off_ref[2 * chip + 1]
        key_pos = jnp.where(lane < SPAN, first + lane, second + lane - SPAN)
        if i:
            bias = jnp.where(key_pos <= off_ref[c] + SPAN - 1, 0.0, NEG_FILL)

        def head(h, _):
            hcols = pl.ds(pl.multiple_of(h * HD, HD), HD)
            mine = pl.ds(pl.multiple_of(h * SPAN, SPAN), SPAN)
            s = lax.dot_general(
                q_ref[:, hcols], kv[at, :HD], (((1,), (1,)), ((), ())), preferred_element_type=F32
            ) * scale
            if i:
                s = s + bias
            else:
                query_pos = off_ref[c] + lax.broadcasted_iota(jnp.int32, (SPAN, 1), 0)
                s = jnp.where(key_pos <= query_pos, s, NEG_FILL)
            top = jnp.max(s, axis=1, keepdims=True)
            if i:
                old = mx[mine, :]
                new = jnp.maximum(old, top)
                p = jnp.exp2(s - jnp.concatenate([new] * 6, axis=1)).astype(BF16)
            else:
                new = jnp.broadcast_to(top, (SPAN, HD))
                p = jnp.exp2(s - top).astype(BF16)
            mixed = jnp.dot(
                p, jnp.concatenate([kv[at, HD:], ones], axis=1), preferred_element_type=F32
            )
            if i:
                keep = jnp.exp2(old - new)
                mixed = acc[mine, :] * jnp.concatenate([keep, keep], axis=1) + mixed
            mx[mine, :] = new
            acc[mine, :] = mixed
            return 0

        lax.fori_loop(0, 8, head, 0, unroll=8)

    loads[2].wait()
    w_to_sib.start()
    w_direct(2, False).start()
    for load in loads[3:]:
        load.wait()
    k_from_sib.wait_recv()
    group(0)
    w_direct(1, False).start()
    w_direct(3, False).start()
    for i in (1, 3):
        k_arrival(i).wait_recv()
        k_handed(i, core).start()
    k_handed(1, 1 - core).wait_recv()
    group(1)
    k_arrival(2).wait_recv()
    k_handed(2, core).start()
    k_handed(3, 1 - core).wait_recv()
    group(3)
    k_handed(2, 1 - core).wait_recv()
    w_direct(2, True).wait_recv()
    w_twin(False).start()
    group(2)

    def divide(h, _):
        hcols = pl.ds(pl.multiple_of(h * HD, HD), HD)
        mine = pl.ds(pl.multiple_of(h * SPAN, SPAN), SPAN)
        att[:, hcols] = (acc[mine, :HD] / acc[mine, HD:]).astype(BF16)
        return 0

    lax.fori_loop(0, 8, divide, 0)

    def piece(k):
        k2 = k // 2
        chip = lax.rem(x + 4 - lax.rem(2 * k2, 4) - k2 // 2, 4)
        return 2 * chip + lax.rem(core + k, 2)

    def to_y(w, i):
        return remote(
            rows(pbuf, w * 4 + lax.rem(y + i, 4), 2 * TOK), rows(rbuf, w * 3 + i - 1, 2 * TOK),
            y_s.at[w, i - 1], y_r.at[w, i - 1], at_y(i),
        )

    def by_way(w, k):
        wide = slice(k * 256, k * 256 + 256)
        return remote(
            rows(pbuf, w * 4 + lax.rem(y + 2, 4), 2 * TOK).at[:, wide], rows(rbuf, w * 3 + 1, 2 * TOK).at[:, wide],
            y_s.at[w, 1 + 2 * k], y_r.at[w, 1 + 2 * k], at_y(1 + 2 * k),
        )

    def relay(k, _):
        w = piece(k)
        for h in range(2):
            wide = slice(h * 256, h * 256 + 256)
            by_way(w, h).wait_recv()
            block = rows(pbuf, w * 4 + lax.rem(y + 1 + 2 * h, 4), 2 * TOK)
            block[:, wide] = (
                block[:, wide].astype(F32) + rows(rbuf, w * 3 + 1, 2 * TOK)[:, wide].astype(F32)
            ).astype(BF16)
            to_y(w, 1 + 2 * h).start()
        return 0

    def to_z(w):
        return remote(rows(zsnd, w, TOK), rows(zbuf, w, TOK), z_s.at[w], z_r.at[w], at_z)

    def project(k, _):
        w = piece(k)
        rows(pbuf, w, SPAN)[...] = jnp.dot(
            att[...], rows(wbuf, w, HEADS)[...], preferred_element_type=F32
        ).astype(BF16)
        for h in range(2):
            by_way(w, h).start()
        return 0

    def reduce(k, _):
        w = piece(k)
        total = rows(pbuf, w * 4 + y, 2 * TOK)[...].astype(F32)
        for i in (1, 3):
            to_y(w, i).wait_recv()
            total += rows(rbuf, w * 3 + i - 1, 2 * TOK)[...].astype(F32)
        tot[...] = total
        rows(zsnd, w, TOK)[...] = rows(tot, 1 - zh, TOK)[...].astype(BF16)
        to_z(w).start()
        wcols = pl.ds(pl.multiple_of(w * 512, 512), 512)
        hid_ref[:, wcols] = rows(tot, zh, TOK)[...] + res_ref[:, wcols].astype(F32)
        return 0

    w_from_sib.wait_recv()
    lax.fori_loop(0, 2, project, 0)
    lax.fori_loop(0, 2, relay, 0)
    w_twin(True).wait_recv()
    w_handed(2, core).start()
    project(2, 0)
    lax.fori_loop(0, 2, reduce, 0)
    w_handed(2, 1 - core).wait_recv()
    project(3, 0)
    lax.fori_loop(2, 4, relay, 0)
    for i in (1, 3):
        w_direct(i, True).wait_recv()
        w_handed(i, core).start()
    lax.fori_loop(0, 2, lambda j, _: project(4 + 2 * j, 0), 0)
    for i in (1, 3):
        w_handed(i, 1 - core).wait_recv()
    lax.fori_loop(0, 2, lambda j, _: project(5 + 2 * j, 0), 0)
    lax.fori_loop(4, 8, relay, 0)
    lax.fori_loop(2, 8, reduce, 0)

    square = jnp.zeros((TOK, 1), F32)

    def finish(k, square):
        w = piece(k)
        to_z(w).wait_recv()
        wcols = pl.ds(pl.multiple_of(w * 512, 512), 512)
        h = hid_ref[:, wcols] + rows(zbuf, w, TOK)[...].astype(F32)
        hid_ref[:, wcols] = h
        return square + jnp.sum(h * h, axis=1, keepdims=True)

    square = lax.fori_loop(0, 8, finish, square)
    inverse = lax.rsqrt(square * (1.0 / D) + 1e-06)
    nrm_ref[...] = (hid_ref[...] * inverse * gain_ref[...]).astype(BF16)

    k_to_sib.wait_send()
    w_to_sib.wait_send()
    for i in (1, 2, 3):
        k_direct(i).wait_send()
        k_handed(i, core).wait_send()
        w_direct(i, False).wait_send()
        w_handed(i, core).wait_send()
    w_twin(False).wait_send()

    def sent(k, _):
        w = piece(k)
        for h in range(2):
            by_way(w, h).wait_send()
            to_y(w, 1 + 2 * h).wait_send()
        to_z(w).wait_send()
        return 0

    lax.fori_loop(0, 8, sent, 0)


def attend(offsets, queries, keys, values, out_proj, residual, gain):
    vm = pl.BlockSpec(memory_space=pltpu.VMEM)
    hbm = pl.BlockSpec(memory_space=pl.ANY)
    dma = pltpu.SemaphoreType.DMA
    return pl.pallas_call(
        attn_kernel,
        out_shape=(jax.ShapeDtypeStruct((TOK, D), F32), jax.ShapeDtypeStruct((TOK, D), BF16)),
        in_specs=[pl.BlockSpec(memory_space=pltpu.SMEM)] + [hbm] * 6,
        out_specs=(vm, vm),
        scratch_shapes=[
            pltpu.VMEM((SPAN, HEADS), BF16),
            pltpu.VMEM((TOK, D), BF16),
            pltpu.VMEM((1, D), F32),
            pltpu.VMEM((PEERS * SPAN, 2 * HD), BF16),
            pltpu.VMEM((PEERS * HEADS, 512), BF16),
            pltpu.VMEM((8 * SPAN, HD), F32),
            pltpu.VMEM((8 * SPAN, 2 * HD), F32),
            pltpu.VMEM((SPAN, HEADS), BF16),
            pltpu.VMEM((PEERS * SPAN, 512), BF16),
            pltpu.VMEM((PEERS * 3 * 2 * TOK, 512), BF16),
            pltpu.VMEM((2 * TOK, 512), F32),
            pltpu.VMEM((PEERS * TOK, 512), BF16),
            pltpu.VMEM((PEERS * TOK, 512), BF16),
            dma((6,)), dma((7,)), dma((7,)), dma((8,)), dma((8,)),
            dma((PEERS, 4)), dma((PEERS, 4)), dma((PEERS,)), dma((PEERS,)),
        ],
        compiler_params=pltpu.CompilerParams(
            collective_id=2, has_side_effects=True, vmem_limit_bytes=62 * 1024 * 1024
        ),
        cost_estimate=pl.CostEstimate(flops=9_000_000_000, bytes_accessed=4_000_000, transcendentals=10_000_000),
        name="attend",
    )(offsets, queries, keys, values, out_proj, residual, gain)


def shards(
    queries, keys, values, offsets, out_proj, residual, norm_gain, expert_ids, gate_probs, w_gate, w_up, w_down,
):
    hidden, normed = attend(offsets, queries, keys, values, out_proj, residual, norm_gain[None, :])
    return moe(hidden, normed, expert_ids.T, gate_probs.T, w_gate, w_up, w_down)


def solution(mesh):
    return jax.shard_map(
        shards,
        mesh=mesh,
        in_specs=(
            P(("dp", "ctx"), "exp"),
            P(("dp", "ctx"), None),
            P(("dp", "ctx"), None),
            P("dp"),
            P("exp", "ctx"),
            P(("dp", "ctx", "exp"), None),
            P(),
            P(("dp", "ctx", "exp"), None),
            P(("dp", "ctx", "exp"), None),
            P(("ctx", "exp"), None, None),
            P(("ctx", "exp"), None, None),
            P(("ctx", "exp"), None, None),
        ),
        out_specs=P(("dp", "ctx", "exp"), None),
        check_vma=False,
    )
```
